32 devices in a mesh: dp: 8 (over y, x, core), freq: 4 (over z).
Axes of the slice: x: 2, y: 2, z: 4, core: 2. Of those that a mesh axis runs over, the one named last changes fastest.
Arguments:
- records: float32 [8, 2, 1024, 2048], P('dp', None, None, 'freq'), may hold values from -6 to 6
- stem_weight: bfloat16 [256, 512], replicated, may hold values from -0.375 to 0.375
- conv_weight: bfloat16 [3, 3, 16, 512], replicated, may hold values from -0.875 to 0.875
- mix_weight: bfloat16 [3, 512, 512], replicated, may hold values from -0.25 to 0.25
- head_weight: float32 [512, 10], replicated, may hold values from -0.25 to 0.25
- labels: int32 [8], P('dp'), may hold values from 0 to 9
- band_bounds: int32 [33], replicated, may hold values from 0 to 1048576, as said below
Outputs:
- loss: float32 [], replicated
- grad_stem: float32 [256, 512], replicated
- grad_conv: float32 [3, 3, 16, 512], replicated
- grad_mix: float32 [3, 512, 512], replicated
- grad_head: float32 [512, 10], replicated
The draws below stay inside these ranges and needn't reach their ends.
Inputs may be any that keep to these rules, and one draw needn't show every extreme that they name: `band_bounds`: strictly increasing multiples of 128; the first is 0 and the last is half of 2097152.
All inputs are finite; a program needn't handle non-finite values.
Results may differ from the reference program's by a relative error of at most 0.0018.
Values may be sent and summed in bfloat16 or wider, within the bound.
No kernel may reach another device: no remote copies, remote signals or barrier semaphores. Data moves between devices by JAX's collectives and lax.ppermute only.
A program may use at most 192 MiB of HBM per device.

```python
import jax
import jax.numpy as jnp
from jax import lax

RECORDS = 8
N1 = 1024
N2 = 2048
POOL = 128
CHANNELS = 512
GROUP_WIDTH = 16
KW = 3
LAYERS = 3
CLASSES = 10


def draw_band_bounds(key, part):
    positions = N1 * N2 // 2 // POOL
    bands = CHANNELS // GROUP_WIDTH
    cuts = jax.random.permutation(key, positions - 1)[:bands - 1] + 1
    cuts = jnp.sort(cuts).astype(jnp.int32)
    edges = jnp.concatenate([jnp.zeros((1,), jnp.int32), cuts, jnp.full((1,), positions, jnp.int32)])
    return (edges * POOL).astype(jnp.int32)


def with_ends(values, key, low, top_value):
    longest = values.shape.index(max(values.shape))
    spots = []
    for shift in (0, 1):
        where = [jax.random.randint(jax.random.fold_in(key, axis), (), 0, length) for axis, length in enumerate(values.shape)]
        where[longest] = (where[longest] + shift) % values.shape[longest]
        spots.append(tuple(where))
    return values.at[spots[0]].set(low).at[spots[1]].set(top_value)


def shard_levels(key, dims, split, least, top_value):
    level, own = 1.0, jax.random.fold_in(key, 6)
    for axis_at, shards_of in split:
        steps = jnp.exp(jax.random.uniform(jax.random.fold_in(own, axis_at), (shards_of,), jnp.float32, least / len(split), top_value / len(split)))
        level = level * jnp.repeat(steps, dims[axis_at] // shards_of).reshape([-1 if axis == axis_at else 1 for axis in range(len(dims))])
    return level


def centred(key, extent, scale, limit, shards=(), kind=jnp.bfloat16):
    loudness = shard_levels(key, extent, shards, -0.22, 0.18) if shards else 1.0
    drawn = jax.random.normal(key, extent, jnp.float32) * scale * loudness
    return jnp.minimum(jnp.maximum(drawn, -limit), limit).astype(kind)


def setup_inputs(seed: int = 0) -> dict:
    key_list = jax.random.split(jax.random.key(seed), 8)
    records = centred(key_list[0], (RECORDS, 2, N1, N2), 1.0, 6.0, ((0, 8), (3, 4)), jnp.float32)
    stem_weight = centred(key_list[1], (2 * POOL, CHANNELS), (2 * POOL) ** -0.5, 0.375)
    conv_weight = centred(key_list[2], (LAYERS, KW, GROUP_WIDTH, CHANNELS), (KW * GROUP_WIDTH) ** -0.5, 0.875)
    mix_weight = centred(key_list[3], (LAYERS, CHANNELS, CHANNELS), CHANNELS ** -0.5, 0.25)
    head_weight = centred(key_list[4], (CHANNELS, CLASSES), CHANNELS ** -0.5, 0.25, (), jnp.float32)
    labels = with_ends(jax.random.randint(key_list[5], (RECORDS,), 0, CLASSES), jax.random.fold_in(key_list[5], 1), 0, CLASSES - 1).astype(jnp.int32)
    band_bounds = draw_band_bounds(jax.random.fold_in(key_list[7], 71), 0)
    return {"records": records, "stem_weight": stem_weight, "conv_weight": conv_weight, "mix_weight": mix_weight, "head_weight": head_weight, "labels": labels, "band_bounds": band_bounds}


EXACT_DOTS = lax.Precision.HIGHEST
EPS = 1e-05

def spectra_features(record):
    total_len = N1 * N2
    signal = (record[0] + 1j * record[1]).reshape(total_len)
    angles = jnp.arange(total_len).astype(record.dtype) * (jnp.pi / total_len)
    signal = signal * (jnp.cos(angles) - 1j * jnp.sin(angles))
    spectrum = jnp.fft.fft(signal)
    mirrored = spectrum[::-1]
    z_real = jnp.real(spectrum)
    z_imag = jnp.imag(spectrum)
    m_real = jnp.real(mirrored)
    m_imag = jnp.imag(mirrored)
    half_len = total_len // 2
    power_a = (((z_real + m_real) ** 2 + (z_imag - m_imag) ** 2) * 0.25)[:half_len]
    power_b = (((z_imag + m_imag) ** 2 + (z_real - m_real) ** 2) * 0.25)[:half_len]
    feat_a = jnp.log1p(power_a / total_len).reshape(half_len // POOL, POOL)
    feat_b = jnp.log1p(power_b / total_len).reshape(half_len // POOL, POOL)
    return jnp.concatenate([feat_a, feat_b], axis=1).astype(jnp.bfloat16)

def conv_forward(padded, tap_weights, span_len):
    groups = padded.shape[-1] // GROUP_WIDTH
    record_count = padded.shape[0]
    result = jnp.zeros((record_count, span_len, groups, GROUP_WIDTH), jnp.float32)
    for tap_idx in range(KW):
        window = padded[:, tap_idx:tap_idx + span_len].astype(jnp.float32).reshape(record_count, span_len, groups, GROUP_WIDTH)
        kernel = tap_weights[tap_idx].astype(jnp.float32).reshape(GROUP_WIDTH, groups, GROUP_WIDTH)
        result = result + jnp.einsum('rpgi,igo->rpgo', window, kernel, precision=EXACT_DOTS)
    return result.reshape(record_count, span_len, groups * GROUP_WIDTH)

def conv_backward(grad_padded, tap_weights, span_len):
    groups = grad_padded.shape[-1] // GROUP_WIDTH
    record_count = grad_padded.shape[0]
    result = jnp.zeros((record_count, span_len, groups, GROUP_WIDTH), jnp.float32)
    for tap_idx in range(KW):
        shift_at = KW - 1 - tap_idx
        window = grad_padded[:, shift_at:shift_at + span_len].astype(jnp.float32).reshape(record_count, span_len, groups, GROUP_WIDTH)
        kernel = tap_weights[tap_idx].astype(jnp.float32).reshape(GROUP_WIDTH, groups, GROUP_WIDTH)
        result = result + jnp.einsum('rpgo,igo->rpgi', window, kernel, precision=EXACT_DOTS)
    return result.reshape(record_count, span_len, groups * GROUP_WIDTH)

def conv_weight_grad(padded, grad_pre, span_len):
    groups = padded.shape[-1] // GROUP_WIDTH
    record_count = padded.shape[0]
    grad_split = grad_pre.astype(jnp.float32).reshape(record_count, span_len, groups, GROUP_WIDTH)
    tap_list = []
    for tap_idx in range(KW):
        window = padded[:, tap_idx:tap_idx + span_len].astype(jnp.float32).reshape(record_count, span_len, groups, GROUP_WIDTH)
        tap_grad = jnp.einsum('rpgi,rpgo->igo', window, grad_split, precision=EXACT_DOTS)
        tap_list.append(tap_grad.reshape(GROUP_WIDTH, groups * GROUP_WIDTH))
    return jnp.stack(tap_list)

def record_step(record, label, stem_weight, conv_weight, mix_weight, head_weight, band_bounds):
    features_in = spectra_features(record)[None]
    positions = features_in.shape[1]
    channels = stem_weight.shape[1]
    groups = channels // GROUP_WIDTH
    stream = jnp.einsum('rpf,fc->rpc', features_in.astype(jnp.float32), stem_weight.astype(jnp.float32), precision=EXACT_DOTS)
    saved_layers = []
    for layer_idx in range(LAYERS):
        scales = lax.rsqrt(lax.optimization_barrier(jnp.mean(stream * stream, axis=-1, keepdims=True)) + EPS)
        normed = (stream * scales).astype(jnp.bfloat16)
        padded = jnp.pad(normed, ((0, 0), (1, 1), (0, 0)))
        preact = conv_forward(padded, conv_weight[layer_idx], positions)
        activated = jax.nn.silu(preact).astype(jnp.bfloat16)
        saved_layers.append((stream, padded, preact, activated))
        stream = stream + jnp.einsum('rpc,cd->rpd', activated.astype(jnp.float32), mix_weight[layer_idx].astype(jnp.float32), precision=EXACT_DOTS)
    starts = (jnp.arange(positions) * POOL).astype(jnp.int32)[:, None]
    member = ((starts >= band_bounds[None, :-1]) & (starts < band_bounds[None, 1:])).astype(jnp.float32)
    counts = ((band_bounds[1:] - band_bounds[:-1]) // POOL).astype(jnp.float32)
    band_sum = jnp.einsum('pg,rpgo->rgo', member, stream.reshape(1, positions, groups, GROUP_WIDTH), precision=EXACT_DOTS)
    pooled = (band_sum / counts[:, None]).reshape(1, channels)
    logits = jnp.dot(pooled, head_weight, precision=EXACT_DOTS)
    exponents = jnp.exp(logits)
    denominator = lax.optimization_barrier(jnp.sum(exponents, axis=-1, keepdims=True))
    one_hot = (jnp.arange(CLASSES) == label).astype(jnp.float32)[None]
    loss_term = jnp.sum(jnp.log(denominator[:, 0]) - lax.optimization_barrier(jnp.sum(one_hot * logits, axis=-1))) / RECORDS
    grad_logits = (exponents / denominator - one_hot) / RECORDS
    grad_head = jnp.dot(pooled.T, grad_logits, precision=EXACT_DOTS)
    grad_band = jnp.dot(grad_logits, head_weight.T, precision=EXACT_DOTS).reshape(1, groups, GROUP_WIDTH) / counts[:, None]
    grad_stream = (member[None, :, :, None] * grad_band[:, None]).reshape(1, positions, channels)
    conv_grads = [None] * LAYERS
    mix_grads = [None] * LAYERS
    for layer_idx in reversed(range(LAYERS)):
        stream_in, padded, preact, activated = saved_layers[layer_idx]
        grad_out = grad_stream.astype(jnp.bfloat16)
        mix_grads[layer_idx] = jnp.einsum('rpc,rpd->cd', activated.astype(jnp.float32), grad_out.astype(jnp.float32), precision=EXACT_DOTS)
        grad_act = jnp.einsum('rpd,cd->rpc', grad_out.astype(jnp.float32), mix_weight[layer_idx].astype(jnp.float32), precision=EXACT_DOTS)
        gate_value = jax.nn.sigmoid(preact)
        grad_pre = (grad_act * gate_value * (1.0 + preact * (1.0 - gate_value))).astype(jnp.bfloat16)
        grad_padded = jnp.pad(grad_pre, ((0, 0), (1, 1), (0, 0)))
        grad_normed = conv_backward(grad_padded, conv_weight[layer_idx], positions)
        conv_grads[layer_idx] = conv_weight_grad(padded, grad_pre, positions)
        scales = lax.rsqrt(lax.optimization_barrier(jnp.mean(stream_in * stream_in, axis=-1, keepdims=True)) + EPS)
        grad_stream = grad_stream + scales * grad_normed - stream_in * scales ** 3 * lax.optimization_barrier(jnp.mean(stream_in * grad_normed, axis=-1, keepdims=True))
    grad_stem = jnp.einsum('rpf,rpc->fc', features_in.astype(jnp.float32), grad_stream, precision=EXACT_DOTS)
    return (loss_term, grad_stem, jnp.stack(conv_grads), jnp.stack(mix_grads), grad_head)

def reference(records, stem_weight, conv_weight, mix_weight, head_weight, labels, band_bounds):

    def one_record(paired):
        return record_step(paired[0], paired[1], stem_weight, conv_weight, mix_weight, head_weight, band_bounds)
    results = lax.map(one_record, (records, labels))
    return (jnp.sum(results[0]), lax.optimization_barrier(jnp.sum(results[1], axis=0)), lax.optimization_barrier(jnp.sum(results[2], axis=0)), lax.optimization_barrier(jnp.sum(results[3], axis=0)), lax.optimization_barrier(jnp.sum(results[4], axis=0)))
```

```python
import functools

import jax
import jax.numpy as jnp
import numpy as np
from jax import lax
from jax.experimental import pallas as pl
from jax.experimental.pallas import tpu as pltpu
from jax.sharding import PartitionSpec as P

POOL = 128
GROUP_WIDTH = 16
KW = 3
EPS = 1e-05
LANES = 128
HALF_MXU = 256
HALO = 16
TILE = 256
F32 = jnp.float32
BF16 = jnp.bfloat16


def split16(values):
    high = values.astype(BF16)
    return high, (values - high.astype(F32)).astype(BF16)


def table_pair(values):
    high = values.astype(jnp.bfloat16)
    return np.stack([high, (values - high.astype(np.float64)).astype(jnp.bfloat16)])


def first_tables(first_len, second_len):
    total_len = first_len * second_len
    rows = np.arange(first_len // 2)
    odd = 2 * rows + 1
    angles = (np.outer(np.arange(first_len), odd) % (2 * first_len)) * (np.pi / first_len)
    twiddles = (np.outer(np.arange(second_len), odd) % (2 * total_len)) * (np.pi / total_len)

    def by_block(a, b):
        blocks = first_len // 2 // LANES
        a = a.reshape(a.shape[0], blocks, 1, LANES)
        b = b.reshape(b.shape[0], blocks, 1, LANES)
        return np.concatenate([a, b], axis=2).reshape(a.shape[0], -1)

    section = table_pair(by_block(np.cos(angles), -np.sin(angles)))
    twiddle = by_block(np.cos(twiddles), np.sin(twiddles)).astype(np.float32)
    return section, twiddle


def second_tables(second_len):
    quarter = second_len // 4
    idx = np.arange(quarter)
    angles = np.outer(np.arange(1, 4), idx) * (2 * np.pi / second_len)
    spread = np.stack([np.cos(angles), np.sin(angles)], axis=1)[..., None] * np.ones(LANES)
    order = np.concatenate([idx[: quarter // 2], idx[quarter // 2 :][::-1]])
    inner = (np.outer(order, idx) % quarter) * (2 * np.pi / quarter)
    table = table_pair(np.concatenate([np.cos(inner), np.sin(inner)], axis=1))
    flip = np.eye(LANES)[::-1].astype(jnp.bfloat16)
    return spread.astype(np.float32), table, flip


def level_of(exponent, mantissa):
    return mantissa * jnp.exp(exponent * np.log(2.0).astype(np.float32)) * (1.0 / (16384.0 * 32767.0))


def first_kernel(devices, place_ref, x_ref, table_ref, twiddle_ref, *refs):
    outs, codes = refs[:devices], refs[devices]
    signals, _, tile = x_ref.shape
    row = lax.broadcasted_iota(jnp.int32, (HALO, 2 * LANES), 0)
    for signal in range(signals):
        high, low = split16(x_ref[signal].T)
        both = jnp.dot(high, table_ref[0], preferred_element_type=F32)
        both += jnp.dot(low, table_ref[0], preferred_element_type=F32)
        both += jnp.dot(high, table_ref[1], preferred_element_type=F32)
        for at in range(0, both.shape[1], 2 * LANES):
            real, imag = both[:, at : at + LANES], both[:, at + LANES : at + 2 * LANES]
            cosine = twiddle_ref[:, at : at + LANES]
            sine = twiddle_ref[:, at + LANES : at + 2 * LANES]
            turned = jnp.concatenate(
                [real * cosine + imag * sine, imag * cosine - real * sine], axis=1
            )
            top = jnp.maximum(jnp.max(jnp.abs(turned), axis=0, keepdims=True), 1e-20)
            exponent = jnp.ceil(jnp.log(top) * (1.0 / np.log(2.0)))
            mantissa = jnp.floor(
                top * jnp.exp(-exponent * np.log(2.0).astype(np.float32)) * 16384.0
            ) + 1.0
            level = 1.0 / level_of(exponent, mantissa)
            coded = jnp.round(turned * level).astype(jnp.int32)
            head = jnp.where(row == 0, exponent, jnp.where(row == 1, mantissa, 0.0))
            codes[signal, :tile, at : at + 2 * LANES] = coded.astype(jnp.int16)
            codes[signal, tile:, at : at + 2 * LANES] = head.astype(jnp.int32).astype(jnp.int16)
    for shift in range(devices):
        to = (place_ref[0] + shift) % devices
        lanes = pl.ds(pl.multiple_of((to // signals) * 2 * LANES, 2 * LANES), 2 * LANES)
        outs[shift][...] = codes[to % signals, :, lanes]


def first_section(place, records, at, signals, devices, section, twiddle):
    first_len, cols = records.shape[-2:]
    tile = 256
    steps = cols // tile
    width = section.shape[-1]
    shape = jax.ShapeDtypeStruct((steps * (tile + HALO), 2 * LANES), jnp.int16)
    return pl.pallas_call(
        functools.partial(first_kernel, devices),
        out_shape=[shape] * devices,
        grid_spec=pltpu.PrefetchScalarGridSpec(
            num_scalar_prefetch=1,
            grid=(steps,),
            in_specs=[
                pl.BlockSpec((signals, first_len, tile), lambda i, s: (at, 0, i)),
                pl.BlockSpec(section.shape, lambda i, s: (0, 0, 0)),
                pl.BlockSpec((tile, width), lambda i, s: (s[0] * steps + i, 0)),
            ],
            out_specs=[pl.BlockSpec((tile + HALO, 2 * LANES), lambda i, s: (i, 0))] * devices,
            scratch_shapes=[pltpu.VMEM((signals, tile + HALO, width), jnp.int16)],
        ),
        compiler_params=pltpu.CompilerParams(vmem_limit_bytes=60 * 1024 * 1024),
        cost_estimate=pl.CostEstimate(
            flops=6 * signals * first_len * cols * width, bytes_accessed=2**23, transcendentals=0
        ),
        name="first_section",
    )(place, records, section, twiddle)


def second_kernel(devices, total_len, place_ref, *refs):
    received, refs = refs[:devices], refs[devices:]
    (spread_ref, table_ref, flip_ref), refs = refs[:3], refs[3:]
    outs, (signal, right, rest, packed) = refs[:devices], refs[devices:]
    place = place_ref[0]
    cols = signal.shape[0] // devices
    tile = 256
    quarter = signal.shape[0] // 4
    run = quarter // 2 // devices
    for shift in range(devices):
        source = (place - shift + devices) % devices
        for i in range(cols // tile):
            at = i * (tile + HALO)
            head = received[shift][at + tile : at + tile + HALO, :].astype(jnp.int32).astype(F32)
            values = received[shift][at : at + tile, :].astype(jnp.int32).astype(F32)
            rows = pl.ds(pl.multiple_of(source * cols + i * tile, tile), tile)
            signal[rows, :] = values * level_of(head[0:1], head[1:2])
    step = min(quarter, 128)
    for at in range(0, quarter, step):
        parts = [signal[g * quarter + at : g * quarter + at + step, :] for g in range(4)]
        re = [v[:, :LANES] for v in parts]
        im = [v[:, LANES:] for v in parts]
        sum_r, dif_r = re[0] + re[2], re[0] - re[2]
        sum_i, dif_i = im[0] + im[2], im[0] - im[2]
        odd_r, odm_r = re[1] + re[3], re[1] - re[3]
        odd_i, odm_i = im[1] + im[3], im[1] - im[3]
        turned = [
            (sum_r + odd_r, sum_i + odd_i),
            (dif_r + odm_i, dif_i - odm_r),
            (sum_r - odd_r, sum_i - odd_i),
            (dif_r - odm_i, dif_i + odm_r),
        ]
        for c in range(4):
            real, imag = turned[c]
            if c:
                cosine = spread_ref[c - 1, 0, at : at + step, :]
                sine = spread_ref[c - 1, 1, at : at + step, :]
                real, imag = real * cosine + imag * sine, imag * cosine - real * sine
            first = slice(2 * LANES * c, 2 * LANES * c + LANES)
            second = slice(2 * LANES * c + LANES, 2 * LANES * (c + 1))
            for ref, r, i in zip((right, rest), split16(real), split16(imag)):
                ref[at : at + step, first] = r
                ref[at : at + step, second] = i
                ref[quarter + at : quarter + at + step, first] = i
                ref[quarter + at : quarter + at + step, second] = -r
    row = lax.broadcasted_iota(jnp.int32, (HALO, LANES), 0)
    edges = [jnp.zeros((HALO, LANES), F32) for _ in range(devices)]
    for c in range(4):
        lanes = slice(2 * LANES * c, 2 * LANES * (c + 1))
        both = jnp.dot(table_ref[0], right[:, lanes], preferred_element_type=F32)
        both += jnp.dot(table_ref[0], rest[:, lanes], preferred_element_type=F32)
        both += jnp.dot(table_ref[1], right[:, lanes], preferred_element_type=F32)
        power = both[:, :LANES] ** 2 + both[:, LANES:] ** 2
        features = jnp.log1p(power * (1.0 / total_len))
        low = features[: quarter // 2].astype(BF16)
        high = jnp.dot(
            features[quarter // 2 :].astype(BF16), flip_ref[...], preferred_element_type=F32
        )
        for part, values, group in ((0, low, c), (1, high.astype(BF16), 4 + 3 - c)):
            wide = values.astype(F32)
            for to in range(devices):
                packed[to, group * run : (group + 1) * run, :] = values[to * run : (to + 1) * run]
                if group % 4 == 3 and to > 0:
                    edges[to] = jnp.where(
                        row == 2 * part, wide[to * run - 1 : to * run], edges[to]
                    )
                if group % 4 == 0 and to < devices - 1:
                    edges[to] = jnp.where(
                        row == 2 * part + 1, wide[(to + 1) * run : (to + 1) * run + 1], edges[to]
                    )
    for to in range(devices):
        packed[to, 8 * run :, :] = edges[to].astype(BF16)
    for shift in range(devices):
        outs[shift][...] = packed[(place + shift) % devices]


def second_section(place, received, second_len, total_len, spread, table, flip):
    devices = len(received)
    quarter = second_len // 4
    run = quarter // 2 // devices
    shape = (8 * run + HALO, LANES)
    vmem = pl.BlockSpec(memory_space=pltpu.VMEM)
    return pl.pallas_call(
        functools.partial(second_kernel, devices, total_len),
        out_shape=[jax.ShapeDtypeStruct(shape, BF16)] * devices,
        in_specs=[pl.BlockSpec(memory_space=pltpu.SMEM)] + [vmem] * (devices + 3),
        out_specs=[vmem] * devices,
        scratch_shapes=[
            pltpu.VMEM((second_len, 2 * LANES), F32),
            pltpu.VMEM((2 * quarter, 8 * LANES), BF16),
            pltpu.VMEM((2 * quarter, 8 * LANES), BF16),
            pltpu.VMEM((devices,) + shape, BF16),
        ],
        compiler_params=pltpu.CompilerParams(vmem_limit_bytes=32 * 1024 * 1024),
        cost_estimate=pl.CostEstimate(
            flops=96 * LANES * quarter * quarter, bytes_accessed=2**23, transcendentals=0
        ),
        name="second_section",
    )(place, *received, spread, table, flip)


def position_column(start, run, at, rows):
    row = at + lax.broadcasted_iota(jnp.int32, (rows, 1), 0)
    return start + row // run + 32 * (row % run)


def halo_column(start, count):
    row = lax.broadcasted_iota(jnp.int32, (HALO, 1), 0)
    return start + jnp.where(row < 8, row - 8, count + row - 8)


def silu_gate(v):
    return 0.5 + 0.5 * jnp.tanh(0.5 * v)


def close_ends(padded, halo, run):
    count = padded.shape[0] - 2 * run
    row = lax.broadcasted_iota(jnp.int32, (run, 1), 0)
    tail = padded[count : count + run, :].astype(F32)
    head = padded[run : 2 * run, :].astype(F32)
    before = jnp.where(row == 0, halo[7:8], pltpu.roll(tail, 1, 0))
    after = jnp.where(row == run - 1, halo[8:9], pltpu.roll(head, run - 1, 0))
    padded[:run, :] = before.astype(BF16)
    padded[run + count :, :] = after.astype(BF16)
    row = lax.broadcasted_iota(jnp.int32, (HALO, 1), 0)
    down = jnp.where(row == 8, tail[run - 1 : run], pltpu.roll(halo, 1, 0))
    up = jnp.where(row == 7, head[:1], pltpu.roll(halo, HALO - 1, 0))
    return [v.astype(BF16) for v in (down, halo, up)]


def taps_product(windows, kernels, layer):
    halves = []
    for half in range(kernels.shape[1]):
        lanes = slice(half * HALF_MXU, (half + 1) * HALF_MXU)
        total = None
        for tap in range(KW):
            term = jnp.dot(
                windows[tap](lanes), kernels[layer, half, tap], preferred_element_type=F32
            )
            total = term if total is None else total + term
        halves.append(total)
    return jnp.concatenate(halves, axis=1)


def forward_kernel(run, devices, chunks, place_ref, *refs):
    received, refs = refs[: chunks * devices], refs[chunks * devices :]
    (stem, kernels, mix, bounds, streams_out, preacts_out, padded_out, feats_out, partial_out,
     streams, preacts, padded, feats, halos, sems) = refs
    layers = mix.shape[0]
    count = 32 * run
    place = place_ref[0]
    start = place * count
    signals = 2 // chunks
    blocks = devices // signals

    row16 = lax.broadcasted_iota(jnp.int32, (HALO, LANES), 0)
    edge = [jnp.zeros((HALO, LANES), F32) for _ in range(2)]
    for chunk in range(chunks):
        for shift in range(devices):
            ref = received[chunk * devices + shift]
            source = (place - shift + devices) % devices
            ends = ref[8 * run :, :].astype(F32)
            channel = chunk if chunks == 2 else source % 2
            lanes = pl.ds(pl.multiple_of(channel * LANES, LANES), LANES)
            for part in range(2):
                block = source // signals
                block = 2 * blocks - 1 - block if part else block
                for c in range(4):
                    at = pl.multiple_of((block + 8 * c) * run, run)
                    feats[pl.ds(at, run), lanes] = ref[
                        (part * 4 + c) * run : (part * 4 + c + 1) * run, :
                    ]
                for which in range(2):
                    value = ends[2 * part + which : 2 * part + which + 1]
                    at = row16 == block + 8 * which
                    for k in range(2):
                        edge[k] = jnp.where(at & (channel == k), value, edge[k])
    for k in range(2):
        feats[count:, k * LANES : (k + 1) * LANES] = edge[k].astype(BF16)
    copies = [pltpu.make_async_copy(feats, feats_out, sems.at[3 * layers])]
    copies[0].start()

    halo_place = halo_column(start, count)
    inside = ((halo_place >= 0) & (halo_place < devices * count)).astype(F32)

    def norm(values):
        scale = lax.rsqrt(jnp.mean(values * values, axis=-1, keepdims=True) + EPS)
        return values * scale

    def stem_tile(i, _):
        at = pl.multiple_of(i * TILE, TILE)
        rows = pl.ds(at, TILE)
        values = jnp.dot(feats[rows, :], stem[...], preferred_element_type=F32)
        streams[0, rows, :] = values
        padded[0, pl.ds(pl.multiple_of(at + run, run), TILE), :] = norm(values).astype(BF16)
        return 0

    lax.fori_loop(0, count // TILE, stem_tile, 0)
    halo_stream = jnp.dot(feats[count:, :], stem[...], preferred_element_type=F32)
    streams[0, count:, :] = halo_stream
    halos[...] = norm(halo_stream) * inside
    partial_out[...] = jnp.zeros_like(partial_out)

    for layer in range(layers):
        here = padded.at[layer]
        windows = close_ends(here, halos[...].astype(BF16).astype(F32), run)
        for k, (src, dst) in enumerate(((streams, streams_out), (padded, padded_out))):
            copy = pltpu.make_async_copy(src.at[layer], dst.at[layer], sems.at[3 * layer + k])
            copy.start()
            copies.append(copy)
        last = layer == layers - 1

        def layer_tile(i, _, layer=layer, here=here, last=last):
            at = pl.multiple_of(i * TILE, TILE)
            rows = pl.ds(at, TILE)
            taps = [
                lambda lanes, t=t: here[pl.ds(pl.multiple_of(at + t * run, run), TILE), lanes]
                for t in range(KW)
            ]
            preact = taps_product(taps, kernels, layer)
            preacts[layer, rows, :] = preact
            active = (preact * silu_gate(preact)).astype(BF16)
            values = streams[layer, rows, :] + jnp.dot(
                active, mix[layer], preferred_element_type=F32
            )
            if last:
                place = position_column(start, run, at, TILE)
                member = (place >= bounds[0:1, :]) & (place < bounds[1:2, :])
                kept = jnp.where(member, values, 0.0)
                partial_out[...] += jnp.sum(kept.reshape(TILE // 8, 8, kept.shape[1]), axis=0)
            else:
                streams[layer + 1, rows, :] = values
                padded[layer + 1, pl.ds(pl.multiple_of(at + run, run), TILE), :] = norm(
                    values
                ).astype(BF16)
            return 0

        lax.fori_loop(0, count // TILE, layer_tile, 0)
        preact = taps_product([lambda lanes, v=v: v[:, lanes] for v in windows], kernels, layer)
        preacts[layer, count:, :] = preact
        if not last:
            active = (preact * silu_gate(preact)).astype(BF16)
            values = streams[layer, count:, :] + jnp.dot(
                active, mix[layer], preferred_element_type=F32
            )
            streams[layer + 1, count:, :] = values
            halos[...] = norm(values) * inside
        copy = pltpu.make_async_copy(
            preacts.at[layer], preacts_out.at[layer], sems.at[3 * layer + 2]
        )
        copy.start()
        copies.append(copy)
    for copy in copies:
        copy.wait()


def backward_kernel(run, devices, all_records, place_ref, *refs):
    sums, refs = refs[:devices], refs[devices:]
    (streams_in, preacts_in, padded_in, feats_in, bounds, head, kernels, mix_t, grads,
     streams, preacts, padded, feats, grad, ahead, active, out16, sems) = refs
    layers = mix_t.shape[0]
    channels = grads.shape[1]
    count = 32 * run
    start = place_ref[0] * count
    order = []
    for layer in reversed(range(layers)):
        for k, (src, dst) in enumerate(
            ((preacts_in, preacts), (padded_in, padded), (streams_in, streams))
        ):
            order.append(pltpu.make_async_copy(src.at[layer], dst.at[layer], sems.at[3 * layer + k]))
    order.append(pltpu.make_async_copy(feats_in, feats, sems.at[3 * layers]))
    for copy in order:
        copy.start()

    total = sums[0][...]
    for ref in sums[1:]:
        total = total + ref[...]
    band_sum = jnp.sum(total, axis=0, keepdims=True)
    counts = (bounds[1:2, :] - bounds[0:1, :]).astype(F32)
    pooled = band_sum / counts
    classes = place_ref[2]
    row = lax.broadcasted_iota(jnp.int32, (HALO, 1), 0)
    logits = jnp.sum(head[...] * pooled, axis=1, keepdims=True)
    exponents = jnp.where(row < classes, jnp.exp(logits), 0.0)
    denominator = jnp.sum(exponents, axis=0, keepdims=True)
    one_hot = (row == place_ref[1]).astype(F32)
    loss = (jnp.log(denominator) - jnp.sum(one_hot * logits, axis=0, keepdims=True)) / all_records
    grad_logits = (exponents / denominator - one_hot) / all_records
    grad_pooled = jnp.sum(head[...] * grad_logits, axis=0, keepdims=True)
    grad_band = grad_pooled / counts
    lead = (place_ref[0] == 0).astype(F32)
    head_at = layers * channels + feats.shape[1] + layers * KW * GROUP_WIDTH
    grads[head_at : head_at + HALO, :] = lead * jnp.where(
        row == HALO - 1, loss, grad_logits * pooled
    )
    if head_at + HALO < grads.shape[0]:
        grads[head_at + HALO :, :] = jnp.zeros_like(grads[head_at + HALO :, :])

    def spread(place):
        member = (place >= bounds[0:1, :]) & (place < bounds[1:2, :])
        return jnp.where(member, grad_band, 0.0)

    def spread_tile(i, _):
        at = pl.multiple_of(i * TILE, TILE)
        grad[pl.ds(at, TILE), :] = spread(position_column(start, run, at, TILE))
        return 0

    lax.fori_loop(0, count // TILE, spread_tile, 0)
    halo_place = halo_column(start, count)
    inside = ((halo_place >= 0) & (halo_place < devices * count)).astype(F32)
    grad[count:, :] = spread(halo_place)

    def gate_grad(preact, grad_act):
        gate = silu_gate(preact)
        return grad_act * gate * (1.0 + preact * (1.0 - gate)), preact * gate

    def stream_grad(grad_out, stream, grad_normed):
        scale = lax.rsqrt(jnp.mean(stream * stream, axis=-1, keepdims=True) + EPS)
        inner = jnp.mean(stream * grad_normed, axis=-1, keepdims=True)
        return grad_out + scale * grad_normed - stream * (scale * scale * scale * inner)

    def transposed(a, b):
        return lax.dot_general(a, b, (((0,), (0,)), ((), ())), preferred_element_type=F32)

    for layer in reversed(range(layers)):
        mine = 3 * (layers - 1 - layer)
        order[mine].wait()
        order[mine + 1].wait()

        def act_tile(i, _, layer=layer):
            at = pl.multiple_of(i * TILE, TILE)
            rows = pl.ds(at, TILE)
            outgoing = grad[rows, :].astype(BF16)
            out16[rows, :] = outgoing
            grad_act = jnp.dot(outgoing, mix_t[layer], preferred_element_type=F32)
            grad_pre, act = gate_grad(preacts[layer, rows, :], grad_act)
            active[rows, :] = act.astype(BF16)
            ahead[pl.ds(pl.multiple_of(at + run, run), TILE), :] = grad_pre.astype(BF16)
            return 0

        lax.fori_loop(0, count // TILE, act_tile, 0)
        grad_act = jnp.dot(grad[count:, :].astype(BF16), mix_t[layer], preferred_element_type=F32)
        halo, _ = gate_grad(preacts[layer, count:, :], grad_act)
        halo = (halo * inside).astype(BF16).astype(F32)
        windows = close_ends(ahead, halo, run)

        def mix_tile(i, _, layer=layer):
            at = pl.multiple_of(i * HALF_MXU, HALF_MXU)
            to = pl.multiple_of(layer * channels + at, HALF_MXU)
            grads[pl.ds(to, HALF_MXU), :] = transposed(
                active[:, pl.ds(at, HALF_MXU)], out16[...]
            )
            return 0

        lax.fori_loop(0, channels // HALF_MXU, mix_tile, 0)

        for half in range(channels // HALF_MXU):
            lanes = slice(half * HALF_MXU, (half + 1) * HALF_MXU)
            at_row = lax.broadcasted_iota(jnp.int32, (HALF_MXU, HALF_MXU), 0) // GROUP_WIDTH
            at_col = lax.broadcasted_iota(jnp.int32, (HALF_MXU, HALF_MXU), 1) // GROUP_WIDTH
            for tap in range(KW):
                full = transposed(
                    padded[layer, tap * run : tap * run + count, lanes],
                    ahead[run : run + count, lanes],
                )
                full = jnp.where(at_row == at_col, full, 0.0)
                folded = jnp.sum(
                    full.reshape(HALF_MXU // GROUP_WIDTH, GROUP_WIDTH, HALF_MXU), axis=0
                )
                to = layers * channels + feats.shape[1] + (layer * KW + tap) * GROUP_WIDTH
                grads[to : to + GROUP_WIDTH, lanes] = folded
        order[mine + 2].wait()

        def stream_tile(i, _, layer=layer):
            at = pl.multiple_of(i * TILE, TILE)
            rows = pl.ds(at, TILE)
            taps = [
                lambda lanes, t=t: ahead[
                    pl.ds(pl.multiple_of(at + (KW - 1 - t) * run, run), TILE), lanes
                ]
                for t in range(KW)
            ]
            grad_normed = taps_product(taps, kernels, layer)
            grad[rows, :] = stream_grad(grad[rows, :], streams[layer, rows, :], grad_normed)
            return 0

        lax.fori_loop(0, count // TILE, stream_tile, 0)
        if layer:
            grad_normed = taps_product(
                [lambda lanes, v=v: v[:, lanes] for v in reversed(windows)], kernels, layer
            )
            grad[count:, :] = stream_grad(
                grad[count:, :], streams[layer, count:, :], grad_normed
            )

    order[-1].wait()

    def split_tile(i, _):
        rows = pl.ds(pl.multiple_of(i * TILE, TILE), TILE)
        values = grad[rows, :]
        high = values.astype(BF16)
        out16[rows, :] = high
        active[rows, :] = (values - high.astype(F32)).astype(BF16)
        return 0

    lax.fori_loop(0, count // TILE, split_tile, 0)
    main = feats[:count, :]
    grads[layers * channels : layers * channels + feats.shape[1], :] = transposed(
        main, out16[...]
    ) + transposed(main, active[...])


def weights_kernel(conv_ref, mix_ref, kernels_ref, turned_ref, mix_t_ref):
    row = lax.broadcasted_iota(jnp.int32, (HALF_MXU, HALF_MXU), 0) // GROUP_WIDTH
    col = lax.broadcasted_iota(jnp.int32, (HALF_MXU, HALF_MXU), 1) // GROUP_WIDTH
    for tap in range(KW):
        for half in range(kernels_ref.shape[0]):
            taps = conv_ref[tap, :, half * HALF_MXU : (half + 1) * HALF_MXU].astype(F32)
            dense = jnp.concatenate([taps] * (HALF_MXU // GROUP_WIDTH), axis=0)
            dense = jnp.where(row == col, dense, 0.0)
            kernels_ref[half, tap] = dense.astype(BF16)
            turned_ref[half, tap] = dense.T.astype(BF16)
    mix_t_ref[...] = mix_ref[...].astype(F32).T.astype(BF16)


def dense_weights(conv_weight, mix_weight):
    layers, taps, width, channels = conv_weight.shape
    dense = (layers, channels // HALF_MXU, taps, HALF_MXU, HALF_MXU)
    by_layer = lambda shape: pl.BlockSpec(
        (None,) + shape[1:], lambda i: (i,) + (0,) * (len(shape) - 1)
    )
    return pl.pallas_call(
        weights_kernel,
        out_shape=[
            jax.ShapeDtypeStruct(dense, BF16),
            jax.ShapeDtypeStruct(dense, BF16),
            jax.ShapeDtypeStruct(mix_weight.shape, BF16),
        ],
        grid=(layers,),
        in_specs=[by_layer(conv_weight.shape), by_layer(mix_weight.shape)],
        out_specs=[by_layer(dense), by_layer(dense), by_layer(mix_weight.shape)],
        compiler_params=pltpu.CompilerParams(vmem_limit_bytes=32 * 1024 * 1024),
        cost_estimate=pl.CostEstimate(flops=0, bytes_accessed=2**24, transcendentals=0),
        name="dense_weights",
    )(conv_weight, mix_weight)


def exchange(x, axis, bit):
    size = lax.axis_size(axis)
    return lax.ppermute(x, axis, [(i, i ^ (1 << bit)) for i in range(size)])


def sum_everywhere(x):
    dp_bits = lax.axis_size("dp").bit_length() - 1
    freq = lax.axis_size("freq")
    place = lax.axis_index("dp")
    for bit in range(dp_bits):
        half = x.shape[0] // 2
        mine = (place >> bit) & 1
        sent = lax.dynamic_slice_in_dim(x, (1 - mine) * half, half, 0)
        kept = lax.dynamic_slice_in_dim(x, mine * half, half, 0)
        x = kept + exchange(sent, "dp", bit)
    part = x.shape[0] // freq
    parts = lax.all_to_all(x.reshape(freq, part, -1), "freq", 0, 0, tiled=True)
    x = jnp.sum(parts, axis=0)
    x = from_all(x, "freq").reshape(freq * part, -1)
    for bit in reversed(range(dp_bits)):
        mine = (place >> bit) & 1
        other = exchange(x, "dp", bit)
        x = jnp.concatenate(
            [jnp.where(mine == 0, x, other), jnp.where(mine == 0, other, x)], axis=0
        )
    return x


def from_all(x, axis):
    size = lax.axis_size(axis)
    pieces = all_of(x, axis)
    stacked = jnp.stack(pieces)
    order = (jnp.arange(size) - lax.axis_index(axis)) % size
    return stacked[(-order) % size]


def shifted(pieces, axis):
    size = len(pieces)
    return [pieces[0]] + [
        lax.ppermute(pieces[k], axis, [(i, (i + k) % size) for i in range(size)])
        for k in range(1, size)
    ]


def all_of(x, axis):
    size = lax.axis_size(axis)
    pieces = [x]
    for shift in range(1, size):
        pieces.append(lax.ppermute(x, axis, [(i, (i + shift) % size) for i in range(size)]))
    return pieces


def local(records, stem_weight, conv_weight, mix_weight, head_weight, labels, band_bounds):
    freq = lax.axis_size("freq")
    place = lax.axis_index("freq").astype(jnp.int32)
    first_len, cols = records.shape[2:]
    second_len = cols * freq
    total_len = first_len * second_len
    layers, channels = mix_weight.shape[:2]
    classes = head_weight.shape[1]
    blocks = first_len // 2 // LANES
    run = second_len // 8 // freq
    count = 32 * run

    section, twiddle = (jnp.asarray(t) for t in first_tables(first_len, second_len))
    spread, table, flip = (jnp.asarray(t) for t in second_tables(second_len))
    here = place.reshape(1)
    signals = freq // blocks
    chunks = 2 // signals
    sent = [
        first_section(here, records[0], c, signals, freq, section, twiddle) for c in range(chunks)
    ]
    arrived = [shifted(pieces, "freq") for pieces in sent]
    features = [
        second_section(here, a, second_len, total_len, spread, table, flip) for a in arrived
    ]
    received = [piece for f in features for piece in shifted(f, "freq")]
    kernels, kernels_t, mix_t = dense_weights(conv_weight, mix_weight)
    head_t = jnp.pad(head_weight.T, ((0, HALO - classes), (0, 0)))
    steps = jnp.repeat(band_bounds // POOL, GROUP_WIDTH)
    bounds = jnp.stack([steps[:channels], steps[GROUP_WIDTH:]]).astype(jnp.int32)

    vmem = pl.BlockSpec(memory_space=pltpu.VMEM)
    hbm = pl.BlockSpec(memory_space=pl.ANY)
    smem = pl.BlockSpec(memory_space=pltpu.SMEM)
    saved = [
        ((layers, count + HALO, channels), F32),
        ((layers, count + HALO, channels), F32),
        ((layers, count + 2 * run, channels), BF16),
        ((count + HALO, 2 * LANES), BF16),
    ]
    *kept, partial = pl.pallas_call(
        functools.partial(forward_kernel, run, freq, chunks),
        out_shape=[jax.ShapeDtypeStruct(s, d) for s, d in saved]
        + [jax.ShapeDtypeStruct((8, channels), F32)],
        in_specs=[smem] + [vmem] * (len(received) + 4),
        out_specs=[hbm] * 4 + [vmem],
        scratch_shapes=[pltpu.VMEM(s, d) for s, d in saved]
        + [pltpu.VMEM((HALO, channels), F32), pltpu.SemaphoreType.DMA((3 * layers + 1,))],
        compiler_params=pltpu.CompilerParams(vmem_limit_bytes=56 * 1024 * 1024),
        name="network_ahead",
    )(here, *received, stem_weight, kernels, mix_weight, bounds)

    sums = all_of(partial, "freq")
    rows = layers * channels + 2 * LANES + layers * KW * GROUP_WIDTH + HALO
    unit_rows = 8 * lax.axis_size("dp") * freq
    rows = -(-rows // unit_rows) * unit_rows
    scalars = jnp.stack([place, labels[0], jnp.int32(classes)])
    grads = pl.pallas_call(
        functools.partial(backward_kernel, run, freq, lax.axis_size("dp")),
        out_shape=jax.ShapeDtypeStruct((rows, channels), F32),
        in_specs=[smem] + [vmem] * freq + [hbm] * 4 + [vmem] * 4,
        out_specs=vmem,
        scratch_shapes=[pltpu.VMEM(s, d) for s, d in saved]
        + [
            pltpu.VMEM((count + HALO, channels), F32),
            pltpu.VMEM((count + 2 * run, channels), BF16),
            pltpu.VMEM((count, channels), BF16),
            pltpu.VMEM((count, channels), BF16),
            pltpu.SemaphoreType.DMA((3 * layers + 1,)),
        ],
        compiler_params=pltpu.CompilerParams(vmem_limit_bytes=60 * 1024 * 1024),
        name="network_back",
    )(scalars, *sums, *kept, bounds, head_t, kernels_t, mix_t)

    total = sum_everywhere(grads)
    mix_rows = layers * channels
    conv_at = mix_rows + 2 * LANES
    head_at = conv_at + layers * KW * GROUP_WIDTH
    return (
        total[head_at + HALO - 1, 0],
        total[mix_rows:conv_at],
        total[conv_at:head_at].reshape(layers, KW, GROUP_WIDTH, channels),
        total[:mix_rows].reshape(layers, channels, channels),
        total[head_at : head_at + classes].T,
    )


def solution(mesh):
    in_specs = (P("dp", None, None, "freq"), P(), P(), P(), P(), P("dp"), P())
    out_specs = (P(), P(), P(), P(), P())
    return jax.shard_map(local, mesh=mesh, in_specs=in_specs, out_specs=out_specs, check_vma=False)
```

```python
import functools

import jax
import jax.numpy as jnp
import numpy as np
from jax import lax
from jax.experimental import pallas as pl
from jax.experimental.pallas import tpu as pltpu
from jax.sharding import PartitionSpec as P

POOL = 128
GROUP_WIDTH = 16
KW = 3
EPS = 1e-05
LANES = 128
HALF_MXU = 256
HALO = 16
TILE = 1024
F32 = jnp.float32
BF16 = jnp.bfloat16


def split16(values):
    high = values.astype(BF16)
    return high, (values - high.astype(F32)).astype(BF16)


def table_pair(values):
    high = values.astype(jnp.bfloat16)
    return np.stack([high, (values - high.astype(np.float64)).astype(jnp.bfloat16)])


def first_tables(first_len, second_len):
    total_len = first_len * second_len
    rows = np.arange(first_len // 2)
    odd = 2 * rows + 1
    angles = (np.outer(np.arange(first_len), odd) % (2 * first_len)) * (np.pi / first_len)
    twiddles = (np.outer(np.arange(second_len), odd) % (2 * total_len)) * (np.pi / total_len)

    def by_block(a, b):
        blocks = first_len // 2 // LANES
        a = a.reshape(a.shape[0], blocks, 1, LANES)
        b = b.reshape(b.shape[0], blocks, 1, LANES)
        return np.concatenate([a, b], axis=2).reshape(a.shape[0], -1)

    section = table_pair(by_block(np.cos(angles), -np.sin(angles)))
    twiddle = by_block(np.cos(twiddles), np.sin(twiddles)).astype(np.float32)
    return section, twiddle


def second_tables(second_len):
    quarter = second_len // 4
    idx = np.arange(quarter)
    angles = np.outer(np.arange(1, 4), idx) * (2 * np.pi / second_len)
    spread = np.stack([np.cos(angles), np.sin(angles)], axis=1)[..., None] * np.ones(LANES)
    order = np.concatenate([idx[: quarter // 2], idx[quarter // 2 :][::-1]])
    inner = (np.outer(order, idx) % quarter) * (2 * np.pi / quarter)
    table = table_pair(np.concatenate([np.cos(inner), np.sin(inner)], axis=1))
    flip = np.eye(LANES)[::-1].astype(jnp.bfloat16)
    return spread.astype(np.float32), table, flip


def level_of(exponent, mantissa):
    return mantissa * jnp.exp(exponent * np.log(2.0).astype(np.float32)) * (1.0 / (16384.0 * 32767.0))


def first_kernel(devices, place_ref, x_ref, table_ref, twiddle_ref, *refs):
    outs, codes = refs[:devices], refs[devices]
    signals, _, tile = x_ref.shape
    row = lax.broadcasted_iota(jnp.int32, (HALO, 2 * LANES), 0)
    for signal in range(signals):
        high, low = split16(x_ref[signal].T)
        both = jnp.dot(high, table_ref[0], preferred_element_type=F32)
        both += jnp.dot(low, table_ref[0], preferred_element_type=F32)
        both += jnp.dot(high, table_ref[1], preferred_element_type=F32)
        for at in range(0, both.shape[1], 2 * LANES):
            real, imag = both[:, at : at + LANES], both[:, at + LANES : at + 2 * LANES]
            cosine = twiddle_ref[:, at : at + LANES]
            sine = twiddle_ref[:, at + LANES : at + 2 * LANES]
            turned = jnp.concatenate(
                [real * cosine + imag * sine, imag * cosine - real * sine], axis=1
            )
            top = jnp.maximum(jnp.max(jnp.abs(turned), axis=0, keepdims=True), 1e-20)
            exponent = jnp.ceil(jnp.log(top) * (1.0 / np.log(2.0)))
            mantissa = jnp.floor(
                top * jnp.exp(-exponent * np.log(2.0).astype(np.float32)) * 16384.0
            ) + 1.0
            level = 1.0 / level_of(exponent, mantissa)
            coded = jnp.round(turned * level).astype(jnp.int32)
            head = jnp.where(row == 0, exponent, jnp.where(row == 1, mantissa, 0.0))
            codes[signal, :tile, at : at + 2 * LANES] = coded.astype(jnp.int16)
            codes[signal, tile:, at : at + 2 * LANES] = head.astype(jnp.int32).astype(jnp.int16)
    for shift in range(devices):
        to = (place_ref[0] + shift) % devices
        lanes = pl.ds(pl.multiple_of((to // signals) * 2 * LANES, 2 * LANES), 2 * LANES)
        outs[shift][...] = codes[to % signals, :, lanes]


def first_section(place, records, at, signals, devices, section, twiddle):
    first_len, cols = records.shape[-2:]
    tile = 256
    steps = cols // tile
    width = section.shape[-1]
    shape = jax.ShapeDtypeStruct((steps * (tile + HALO), 2 * LANES), jnp.int16)
    return pl.pallas_call(
        functools.partial(first_kernel, devices),
        out_shape=[shape] * devices,
        grid_spec=pltpu.PrefetchScalarGridSpec(
            num_scalar_prefetch=1,
            grid=(steps,),
            in_specs=[
                pl.BlockSpec((signals, first_len, tile), lambda i, s: (at, 0, i)),
                pl.BlockSpec(section.shape, lambda i, s: (0, 0, 0)),
                pl.BlockSpec((tile, width), lambda i, s: (s[0] * steps + i, 0)),
            ],
            out_specs=[pl.BlockSpec((tile + HALO, 2 * LANES), lambda i, s: (i, 0))] * devices,
            scratch_shapes=[pltpu.VMEM((signals, tile + HALO, width), jnp.int16)],
        ),
        compiler_params=pltpu.CompilerParams(vmem_limit_bytes=60 * 1024 * 1024),
        cost_estimate=pl.CostEstimate(
            flops=6 * signals * first_len * cols * width, bytes_accessed=2**23, transcendentals=0
        ),
        name="first_section",
    )(place, records, section, twiddle)


def second_kernel(devices, total_len, place_ref, *refs):
    received, refs = refs[:devices], refs[devices:]
    (spread_ref, table_ref, flip_ref), refs = refs[:3], refs[3:]
    outs, (signal, right, rest, packed) = refs[:devices], refs[devices:]
    place = place_ref[0]
    cols = signal.shape[0] // devices
    tile = 256
    quarter = signal.shape[0] // 4
    run = quarter // 2 // devices
    for shift in range(devices):
        source = (place - shift + devices) % devices
        for i in range(cols // tile):
            at = i * (tile + HALO)
            head = received[shift][at + tile : at + tile + HALO, :].astype(jnp.int32).astype(F32)
            values = received[shift][at : at + tile, :].astype(jnp.int32).astype(F32)
            rows = pl.ds(pl.multiple_of(source * cols + i * tile, tile), tile)
            signal[rows, :] = values * level_of(head[0:1], head[1:2])
    step = min(quarter, 128)
    for at in range(0, quarter, step):
        parts = [signal[g * quarter + at : g * quarter + at + step, :] for g in range(4)]
        re = [v[:, :LANES] for v in parts]
        im = [v[:, LANES:] for v in parts]
        sum_r, dif_r = re[0] + re[2], re[0] - re[2]
        sum_i, dif_i = im[0] + im[2], im[0] - im[2]
        odd_r, odm_r = re[1] + re[3], re[1] - re[3]
        odd_i, odm_i = im[1] + im[3], im[1] - im[3]
        turned = [
            (sum_r + odd_r, sum_i + odd_i),
            (dif_r + odm_i, dif_i - odm_r),
            (sum_r - odd_r, sum_i - odd_i),
            (dif_r - odm_i, dif_i + odm_r),
        ]
        for c in range(4):
            real, imag = turned[c]
            if c:
                cosine = spread_ref[c - 1, 0, at : at + step, :]
                sine = spread_ref[c - 1, 1, at : at + step, :]
                real, imag = real * cosine + imag * sine, imag * cosine - real * sine
            first = slice(2 * LANES * c, 2 * LANES * c + LANES)
            second = slice(2 * LANES * c + LANES, 2 * LANES * (c + 1))
            for ref, r, i in zip((right, rest), split16(real), split16(imag)):
                ref[at : at + step, first] = r
                ref[at : at + step, second] = i
                ref[quarter + at : quarter + at + step, first] = i
                ref[quarter + at : quarter + at + step, second] = -r
    row = lax.broadcasted_iota(jnp.int32, (HALO, LANES), 0)
    edges = [jnp.zeros((HALO, LANES), F32) for _ in range(devices)]
    for c in range(4):
        lanes = slice(2 * LANES * c, 2 * LANES * (c + 1))
        both = jnp.dot(table_ref[0], right[:, lanes], preferred_element_type=F32)
        both += jnp.dot(table_ref[0], rest[:, lanes], preferred_element_type=F32)
        both += jnp.dot(table_ref[1], right[:, lanes], preferred_element_type=F32)
        power = both[:, :LANES] ** 2 + both[:, LANES:] ** 2
        features = jnp.log1p(power * (1.0 / total_len))
        low = features[: quarter // 2].astype(BF16)
        high = jnp.dot(
            features[quarter // 2 :].astype(BF16), flip_ref[...], preferred_element_type=F32
        )
        for part, values, group in ((0, low, c), (1, high.astype(BF16), 4 + 3 - c)):
            wide = values.astype(F32)
            for to in range(devices):
                packed[to, group * run : (group + 1) * run, :] = values[to * run : (to + 1) * run]
                if group % 4 == 3 and to > 0:
                    edges[to] = jnp.where(
                        row == 2 * part, wide[to * run - 1 : to * run], edges[to]
                    )
                if group % 4 == 0 and to < devices - 1:
                    edges[to] = jnp.where(
                        row == 2 * part + 1, wide[(to + 1) * run : (to + 1) * run + 1], edges[to]
                    )
    for to in range(devices):
        packed[to, 8 * run :, :] = edges[to].astype(BF16)
    for shift in range(devices):
        outs[shift][...] = packed[(place + shift) % devices]


def second_section(place, received, second_len, total_len, spread, table, flip):
    devices = len(received)
    quarter = second_len // 4
    run = quarter // 2 // devices
    shape = (8 * run + HALO, LANES)
    vmem = pl.BlockSpec(memory_space=pltpu.VMEM)
    return pl.pallas_call(
        functools.partial(second_kernel, devices, total_len),
        out_shape=[jax.ShapeDtypeStruct(shape, BF16)] * devices,
        in_specs=[pl.BlockSpec(memory_space=pltpu.SMEM)] + [vmem] * (devices + 3),
        out_specs=[vmem] * devices,
        scratch_shapes=[
            pltpu.VMEM((second_len, 2 * LANES), F32),
            pltpu.VMEM((2 * quarter, 8 * LANES), BF16),
            pltpu.VMEM((2 * quarter, 8 * LANES), BF16),
            pltpu.VMEM((devices,) + shape, BF16),
        ],
        compiler_params=pltpu.CompilerParams(vmem_limit_bytes=32 * 1024 * 1024),
        cost_estimate=pl.CostEstimate(
            flops=96 * LANES * quarter * quarter, bytes_accessed=2**23, transcendentals=0
        ),
        name="second_section",
    )(place, *received, spread, table, flip)


def position_column(start, run, at, rows):
    row = at + lax.broadcasted_iota(jnp.int32, (rows, 1), 0)
    return start + row // run + 32 * (row % run)


def halo_column(start, count):
    row = lax.broadcasted_iota(jnp.int32, (HALO, 1), 0)
    return start + jnp.where(row < 8, row - 8, count + row - 8)


def silu_gate(v):
    return 0.5 + 0.5 * jnp.tanh(0.5 * v)


def close_ends(padded, halo, run):
    count = padded.shape[0] - 2 * run - HALO
    row = lax.broadcasted_iota(jnp.int32, (run, 1), 0)
    tail = padded[count : count + run, :].astype(F32)
    head = padded[run : 2 * run, :].astype(F32)
    before = jnp.where(row == 0, halo[7:8], pltpu.roll(tail, 1, 0))
    after = jnp.where(row == run - 1, halo[8:9], pltpu.roll(head, run - 1, 0))
    padded[:run, :] = before.astype(BF16)
    padded[run + count : 2 * run + count, :] = after.astype(BF16)
    padded[2 * run + count :, :] = halo.astype(BF16)
    row = lax.broadcasted_iota(jnp.int32, (HALO, 1), 0)
    down = jnp.where(row == 8, tail[run - 1 : run], pltpu.roll(halo, 1, 0))
    up = jnp.where(row == 7, head[:1], pltpu.roll(halo, HALO - 1, 0))
    return [v.astype(BF16) for v in (down, halo, up)]


def taps_product(windows, kernels):
    halves = []
    for half in range(kernels.shape[0]):
        lanes = slice(half * HALF_MXU, (half + 1) * HALF_MXU)
        total = None
        for tap in range(KW):
            term = jnp.dot(
                windows[tap](lanes), kernels[half, tap], preferred_element_type=F32
            )
            total = term if total is None else total + term
        halves.append(total)
    return jnp.concatenate(halves, axis=1)


def forward_kernel(run, devices, chunks, place_ref, *refs):
    received, refs = refs[: chunks * devices], refs[chunks * devices :]
    (stem, kernels, mix, bounds, preacts_out, scales_out, padded_out, feats_out, partial_out,
     preacts, scales, padded, feats, stream, halos, sems) = refs
    layers = mix.shape[0]
    count = 32 * run
    place = place_ref[0]
    start = place * count
    signals = 2 // chunks
    blocks = devices // signals

    row16 = lax.broadcasted_iota(jnp.int32, (HALO, LANES), 0)
    edge = [jnp.zeros((HALO, LANES), F32) for _ in range(2)]
    for chunk in range(chunks):
        for shift in range(devices):
            ref = received[chunk * devices + shift]
            source = (place - shift + devices) % devices
            ends = ref[8 * run :, :].astype(F32)
            channel = chunk if chunks == 2 else source % 2
            lanes = pl.ds(pl.multiple_of(channel * LANES, LANES), LANES)
            for part in range(2):
                block = source // signals
                block = 2 * blocks - 1 - block if part else block
                for c in range(4):
                    at = pl.multiple_of((block + 8 * c) * run, run)
                    feats[pl.ds(at, run), lanes] = ref[
                        (part * 4 + c) * run : (part * 4 + c + 1) * run, :
                    ]
                for which in range(2):
                    value = ends[2 * part + which : 2 * part + which + 1]
                    at = row16 == block + 8 * which
                    for k in range(2):
                        edge[k] = jnp.where(at & (channel == k), value, edge[k])
    for k in range(2):
        feats[count:, k * LANES : (k + 1) * LANES] = edge[k].astype(BF16)
    copies = []

    def save(source, target):
        copy = pltpu.make_async_copy(source, target, sems.at[len(copies)])
        copy.start()
        copies.append(copy)

    save(feats, feats_out)
    halo_place = halo_column(start, count)
    inside = ((halo_place >= 0) & (halo_place < devices * count)).astype(F32)
    tile = min(TILE, count)

    def norm(layer, rows, values):
        scale = lax.rsqrt(jnp.mean(values * values, axis=-1, keepdims=True) + EPS)
        scales[layer, rows, :] = jnp.broadcast_to(scale, (values.shape[0], LANES))
        return values * scale

    def put_normed(layer, at, values):
        normed = norm(layer, pl.ds(at, tile), values)
        padded[layer, pl.ds(pl.multiple_of(at + run, run), tile), :] = normed.astype(BF16)

    def stem_tile(i, _):
        at = pl.multiple_of(i * tile, tile)
        values = jnp.dot(feats[pl.ds(at, tile), :], stem[...], preferred_element_type=F32)
        stream[pl.ds(at, tile), :] = values
        put_normed(0, at, values)
        return 0

    lax.fori_loop(0, count // tile, stem_tile, 0)
    values = jnp.dot(feats[count:, :], stem[...], preferred_element_type=F32)
    stream[count:, :] = values
    halos[...] = norm(0, slice(count, count + HALO), values) * inside
    partial_out[...] = jnp.zeros_like(partial_out)

    for layer in range(layers):
        here = padded.at[layer]
        windows = close_ends(here, halos[...].astype(BF16).astype(F32), run)
        save(here, padded_out.at[layer])
        save(scales.at[layer], scales_out.at[layer])
        last = layer == layers - 1

        def layer_tile(i, _, layer=layer, here=here, last=last):
            at = pl.multiple_of(i * tile, tile)
            rows = pl.ds(at, tile)
            taps = [
                lambda lanes, t=t: here[pl.ds(pl.multiple_of(at + t * run, run), tile), lanes]
                for t in range(KW)
            ]
            preact = taps_product(taps, kernels.at[layer])
            preacts[layer, rows, :] = preact
            active = (preact * silu_gate(preact)).astype(BF16)
            values = stream[rows, :] + jnp.dot(active, mix[layer], preferred_element_type=F32)
            if last:
                place = position_column(start, run, at, tile)
                member = (place >= bounds[0:1, :]) & (place < bounds[1:2, :])
                kept = jnp.where(member, values, 0.0)
                partial_out[...] += jnp.sum(kept.reshape(tile // 8, 8, kept.shape[1]), axis=0)
            else:
                stream[rows, :] = values
                put_normed(layer + 1, at, values)
            return 0

        lax.fori_loop(0, count // tile, layer_tile, 0)
        preact = taps_product([lambda lanes, v=v: v[:, lanes] for v in windows], kernels.at[layer])
        preacts[layer, count:, :] = preact
        save(preacts.at[layer], preacts_out.at[layer])
        if not last:
            active = (preact * silu_gate(preact)).astype(BF16)
            values = stream[count:, :] + jnp.dot(active, mix[layer], preferred_element_type=F32)
            stream[count:, :] = values
            halos[...] = norm(layer + 1, slice(count, count + HALO), values) * inside
    for copy in copies:
        copy.wait()


def backward_kernel(run, devices, all_records, place_ref, *refs):
    sums, refs = refs[:devices], refs[devices:]
    (preacts_in, scales_in, padded_in, feats_in, bounds, head, kernels, mix_t, kept, sent,
     preacts, scales, padded, feats, feats_t, grad, ahead, active_t, ahead_t, out16, sems) = refs
    layers = mix_t.shape[0]
    channels = grad.shape[1]
    count = 32 * run
    start = place_ref[0] * count
    core = place_ref[3]
    tile = min(TILE, count)
    tiles = count // tile

    arriving = []
    for layer in reversed(range(layers)):
        cuts = [pl.ds(k * tile, tile) for k in range(tiles)] + [pl.ds(count, HALO)]
        copies = [(preacts_in.at[layer, cut, :], preacts.at[layer, cut, :]) for cut in cuts]
        copies += [(padded_in.at[layer], padded.at[layer]), (scales_in.at[layer], scales.at[layer])]
        arriving.append(copies)
    arriving.append([(feats_in, feats)])
    at = 0
    for k, copies in enumerate(arriving):
        arriving[k] = [
            pltpu.make_async_copy(*copy, sems.at[at + j]) for j, copy in enumerate(copies)
        ]
        at += len(copies)
        for copy in arriving[k]:
            copy.start()

    def put(at, value):
        half, at = divmod(at, kept.shape[0])
        rows = slice(at, at + value.shape[0])

        @pl.when(core == half)
        def _():
            kept[rows, :] = value

        @pl.when(core != half)
        def _():
            sent[rows, :] = value

    total = sums[0][...]
    for ref in sums[1:]:
        total = total + ref[...]
    band_sum = jnp.sum(total, axis=0, keepdims=True)
    counts = (bounds[1:2, :] - bounds[0:1, :]).astype(F32)
    pooled = band_sum / counts
    row = lax.broadcasted_iota(jnp.int32, (HALO, 1), 0)
    logits = jnp.sum(head[...] * pooled, axis=1, keepdims=True)
    exponents = jnp.where(row < place_ref[2], jnp.exp(logits), 0.0)
    denominator = jnp.sum(exponents, axis=0, keepdims=True)
    one_hot = (row == place_ref[1]).astype(F32)
    loss = jnp.log(denominator) - jnp.sum(one_hot * logits, axis=0, keepdims=True)
    loss = loss / all_records
    grad_logits = (exponents / denominator - one_hot) / all_records
    grad_pooled = jnp.sum(head[...] * grad_logits, axis=0, keepdims=True)
    grad_band = grad_pooled / counts
    lead = (place_ref[0] == 0).astype(F32)
    stem_at = layers * channels
    conv_at = stem_at + 2 * LANES
    head_at = conv_at + layers * KW * GROUP_WIDTH
    put(head_at, lead * jnp.where(row == HALO - 1, loss, grad_logits * pooled))
    rest = 2 * kept.shape[0] - head_at - HALO
    if rest:
        put(head_at + HALO, jnp.zeros((rest, channels), F32))

    def spread(place):
        member = (place >= bounds[0:1, :]) & (place < bounds[1:2, :])
        return jnp.where(member, grad_band, 0.0)

    halo_place = halo_column(start, count)
    inside = ((halo_place >= 0) & (halo_place < devices * count)).astype(F32)
    grad[count:, :] = spread(halo_place)

    def gate_grad(value, grad_act):
        gate = silu_gate(value)
        return grad_act * gate * (1.0 + value * (1.0 - gate)), value * gate

    def stream_grad(layer, outgoing, rows, normed, grad_normed):
        scale = jnp.concatenate([scales[layer, rows, :]] * (channels // LANES), axis=1)
        normed = normed.astype(F32)
        inner = jnp.mean(normed * grad_normed, axis=-1, keepdims=True)
        return outgoing + scale * (grad_normed - normed * inner)

    at_row = lax.broadcasted_iota(jnp.int32, (HALF_MXU, HALF_MXU), 0) // GROUP_WIDTH
    at_col = lax.broadcasted_iota(jnp.int32, (HALF_MXU, HALF_MXU), 1) // GROUP_WIDTH
    for layer in reversed(range(layers)):
        copies = arriving[layers - 1 - layer]
        top, bottom = layer == layers - 1, layer == 0

        def act_tile(i, _, layer=layer, top=top):
            at = pl.multiple_of(i * tile, tile)
            rows = pl.ds(at, tile)
            if top:
                values = spread(position_column(start, run, at, tile))
                grad[rows, :] = values
            else:
                values = grad[rows, :]
            outgoing = values.astype(BF16)
            out16[rows, :] = outgoing
            grad_act = jnp.dot(outgoing, mix_t[layer], preferred_element_type=F32)
            grad_pre, act = gate_grad(preacts[layer, rows, :], grad_act)
            grad_pre = grad_pre.astype(BF16)
            active_t[:, rows] = act.astype(BF16).T
            ahead_t[:, rows] = grad_pre.T
            ahead[pl.ds(pl.multiple_of(at + run, run), tile), :] = grad_pre
            return 0

        if top:
            for k in range(tiles):
                copies[k].wait()
                lax.fori_loop(k, k + 1, act_tile, 0)
        else:
            for k in range(tiles):
                copies[k].wait()
            lax.fori_loop(0, tiles, act_tile, 0)
        copies[tiles].wait()
        grad_act = jnp.dot(grad[count:, :].astype(BF16), mix_t[layer], preferred_element_type=F32)
        halo, _ = gate_grad(preacts[layer, count:, :], grad_act)
        halo = (halo * inside).astype(BF16).astype(F32)
        windows = close_ends(ahead, halo, run)

        for half in range(channels // HALF_MXU):
            value = jnp.dot(
                active_t[half * HALF_MXU : (half + 1) * HALF_MXU, :],
                out16[...],
                preferred_element_type=F32,
            )
            put(layer * channels + half * HALF_MXU, value)

        copies[tiles + 1].wait()
        for tap in range(KW):
            folded = []
            for half in range(channels // HALF_MXU):
                lanes = slice(half * HALF_MXU, (half + 1) * HALF_MXU)
                full = jnp.dot(
                    ahead_t[lanes, :],
                    padded[layer, tap * run : tap * run + count, lanes],
                    preferred_element_type=F32,
                ).T
                full = jnp.where(at_row == at_col, full, 0.0)
                folded.append(
                    jnp.sum(full.reshape(HALF_MXU // GROUP_WIDTH, GROUP_WIDTH, HALF_MXU), axis=0)
                )
            at = conv_at + (layer * KW + tap) * GROUP_WIDTH
            put(at, jnp.concatenate(folded, axis=1))
        copies[tiles + 2].wait()

        def stream_tile(i, _, layer=layer, bottom=bottom):
            at = pl.multiple_of(i * tile, tile)
            rows = pl.ds(at, tile)
            taps = [
                lambda lanes, t=t: ahead[
                    pl.ds(pl.multiple_of(at + (KW - 1 - t) * run, run), tile), lanes
                ]
                for t in range(KW)
            ]
            grad_normed = taps_product(taps, kernels.at[layer])
            normed = padded[layer, pl.ds(pl.multiple_of(at + run, run), tile), :]
            value = stream_grad(layer, grad[rows, :], rows, normed, grad_normed)
            if bottom:
                high, low = split16(value)
                out16[rows, :] = high
                active_t[:, rows] = low.T
            else:
                grad[rows, :] = value
            return 0

        lax.fori_loop(0, tiles, stream_tile, 0)
        if not bottom:
            grad_normed = taps_product(
                [lambda lanes, v=v: v[:, lanes] for v in reversed(windows)], kernels.at[layer]
            )
            normed = padded[layer, count + 2 * run :, :]
            rows = slice(count, count + HALO)
            grad[rows, :] = stream_grad(layer, grad[rows, :], rows, normed, grad_normed)

    arriving[-1][0].wait()
    feats_t[...] = feats[:count, :].T
    value = jnp.dot(feats_t[...], out16[...], preferred_element_type=F32)
    rest = jnp.dot(active_t[...], feats[:count, :], preferred_element_type=F32)
    put(stem_at, value + rest.T)


def network_back(scalars, sums, saved, bounds, head_t, kernels_t, mix_t, half_rows):
    preacts, scales, padded, feats = saved
    layers, rows, channels = preacts.shape
    count = rows - HALO
    tiles = count // min(TILE, count)
    devices = len(sums)
    vmem = pl.BlockSpec(memory_space=pltpu.VMEM)
    hbm = pl.BlockSpec(memory_space=pl.ANY)
    return pl.pallas_call(
        functools.partial(backward_kernel, count // 32, devices, lax.axis_size("dp")),
        out_shape=[jax.ShapeDtypeStruct((half_rows, channels), F32)] * 2,
        in_specs=[pl.BlockSpec(memory_space=pltpu.SMEM)] + [vmem] * devices + [hbm] * 4 + [vmem] * 4,
        out_specs=[vmem] * 2,
        scratch_shapes=[pltpu.VMEM(x.shape, x.dtype) for x in saved]
        + [
            pltpu.VMEM((feats.shape[1], count), BF16),
            pltpu.VMEM((rows, channels), F32),
            pltpu.VMEM(padded.shape[1:], BF16),
            pltpu.VMEM((channels, count), BF16),
            pltpu.VMEM((channels, count), BF16),
            pltpu.VMEM((count, channels), BF16),
            pltpu.SemaphoreType.DMA((layers * (tiles + 3) + 1,)),
        ],
        compiler_params=pltpu.CompilerParams(vmem_limit_bytes=60 * 1024 * 1024),
        name="network_back",
    )(scalars, *sums, *saved, bounds, head_t, kernels_t, mix_t)


def weights_kernel(conv_ref, mix_ref, kernels_ref, turned_ref, mix_t_ref):
    row = lax.broadcasted_iota(jnp.int32, (HALF_MXU, HALF_MXU), 0) // GROUP_WIDTH
    col = lax.broadcasted_iota(jnp.int32, (HALF_MXU, HALF_MXU), 1) // GROUP_WIDTH
    for tap in range(KW):
        for half in range(kernels_ref.shape[0]):
            taps = conv_ref[tap, :, half * HALF_MXU : (half + 1) * HALF_MXU].astype(F32)
            dense = jnp.concatenate([taps] * (HALF_MXU // GROUP_WIDTH), axis=0)
            dense = jnp.where(row == col, dense, 0.0)
            kernels_ref[half, tap] = dense.astype(BF16)
            turned_ref[half, tap] = dense.T.astype(BF16)
    mix_t_ref[...] = mix_ref[...].astype(F32).T.astype(BF16)


def dense_weights(conv_weight, mix_weight):
    layers, taps, width, channels = conv_weight.shape
    dense = (layers, channels // HALF_MXU, taps, HALF_MXU, HALF_MXU)
    by_layer = lambda shape: pl.BlockSpec(
        (None,) + shape[1:], lambda i: (i,) + (0,) * (len(shape) - 1)
    )
    return pl.pallas_call(
        weights_kernel,
        out_shape=[
            jax.ShapeDtypeStruct(dense, BF16),
            jax.ShapeDtypeStruct(dense, BF16),
            jax.ShapeDtypeStruct(mix_weight.shape, BF16),
        ],
        grid=(layers,),
        in_specs=[by_layer(conv_weight.shape), by_layer(mix_weight.shape)],
        out_specs=[by_layer(dense), by_layer(dense), by_layer(mix_weight.shape)],
        compiler_params=pltpu.CompilerParams(vmem_limit_bytes=32 * 1024 * 1024),
        cost_estimate=pl.CostEstimate(flops=0, bytes_accessed=2**24, transcendentals=0),
        name="dense_weights",
    )(conv_weight, mix_weight)


def swap(x, axis, step):
    return lax.ppermute(x, axis, [(i, i ^ step) for i in range(lax.axis_size(axis))])


def encode(values, out_ref):
    rows = values.shape[0]
    top = jnp.maximum(jnp.max(jnp.abs(values), axis=1, keepdims=True), 1e-30)
    exponent = jnp.ceil(jnp.log(top) * (1.0 / np.log(2.0)) + 1e-4)
    scale = jnp.exp(-exponent * np.log(2.0).astype(np.float32)) * 32767.0
    out_ref[:rows, :] = jnp.round(values * scale).astype(jnp.int32).astype(jnp.int16)
    out_ref[rows:, :] = jnp.zeros((HALO, values.shape[1]), jnp.int16)
    across = jnp.broadcast_to(exponent, (rows, LANES)).T[:HALO, :]
    out_ref[rows:, :rows] = across.astype(jnp.int32).astype(jnp.int16)


def decode(ref):
    rows = ref.shape[0] - HALO
    across = ref[rows:, :rows].astype(jnp.int32).astype(F32)
    exponent = jnp.concatenate([across] * (LANES // HALO), axis=0).T[:, :1]
    scale = jnp.exp(exponent * np.log(2.0).astype(np.float32)) * (1.0 / 32767.0)
    return ref[:rows, :].astype(jnp.int32).astype(F32) * scale


def cut_kernel(size, place_ref, *refs):
    inputs, outs = refs[:-size], refs[-size:]
    rows = inputs[0].shape[0] // size
    for k in range(size):
        at = pl.multiple_of((place_ref[0] ^ k) * rows, rows)
        value = inputs[0][pl.ds(at, rows), :]
        for ref in inputs[1:]:
            value = value + ref[pl.ds(at, rows), :]
        if k:
            encode(value, outs[k])
        else:
            outs[0][...] = value


def sum_kernel(first_ref, *refs):
    value = first_ref[...]
    for ref in refs[:-1]:
        value = value + decode(ref)
    refs[-1][...] = value


def pieces_kernel(place_ref, *refs):
    inputs, out_ref = refs[:-1], refs[-1]
    rows = inputs[0].shape[0] - HALO
    for k, ref in enumerate(inputs):
        at = pl.multiple_of((place_ref[0] ^ k) * rows, rows)
        out_ref[pl.ds(at, rows), :] = decode(ref)


def encode_kernel(x_ref, out_ref):
    encode(x_ref[...], out_ref)


def small_call(kernel, name, out_shape, place, *args):
    vmem = pl.BlockSpec(memory_space=pltpu.VMEM)
    smem = pl.BlockSpec(memory_space=pltpu.SMEM)
    several = isinstance(out_shape, list)
    lead = [] if place is None else [place.reshape(1).astype(jnp.int32)]
    return pl.pallas_call(
        kernel,
        out_shape=out_shape,
        in_specs=[smem] * len(lead) + [vmem] * len(args),
        out_specs=[vmem] * len(out_shape) if several else vmem,
        compiler_params=pltpu.CompilerParams(vmem_limit_bytes=32 * 1024 * 1024),
        name=name,
    )(*lead, *args)


def scatter_pieces(parts, coded, axis, stride):
    size = lax.axis_size(axis) // stride
    place = lax.axis_index(axis) // stride
    rows, channels = parts[0].shape[0] // size, parts[0].shape[1]
    if coded:
        whole = jax.ShapeDtypeStruct(parts[0].shape, F32)
        parts = [small_call(sum_kernel, "sum_pieces", whole, None, *parts)]
    shapes = [jax.ShapeDtypeStruct((rows, channels), F32)]
    shapes += [jax.ShapeDtypeStruct((rows + HALO, channels), jnp.int16)] * (size - 1)
    own, *others = small_call(
        functools.partial(cut_kernel, size), "cut_pieces", shapes, place, *parts
    )
    return [own] + [swap(piece, axis, (k + 1) * stride) for k, piece in enumerate(others)]


def gather_pieces(x, axis, stride):
    size = lax.axis_size(axis) // stride
    place = lax.axis_index(axis) // stride
    rows, channels = x.shape
    shape = jax.ShapeDtypeStruct((rows + HALO, channels), jnp.int16)
    coded = small_call(encode_kernel, "code_piece", shape, None, x)
    pieces = [coded] + [swap(coded, axis, k * stride) for k in range(1, size)]
    whole = jax.ShapeDtypeStruct((size * rows, channels), F32)
    return small_call(pieces_kernel, "lay_pieces", whole, place, *pieces)


def spread_kernel(core_ref, mine_ref, other_ref, *refs):
    outs, sems = refs[:-1], refs[-1]
    for core, halves in enumerate(((mine_ref, other_ref), (other_ref, mine_ref))):

        @pl.when(core_ref[0] == core)
        def _(halves=halves):
            copies = []
            half, at = 0, 0
            for out_ref in outs:
                done, rows = 0, out_ref.shape[0]
                while done < rows:
                    step = min(rows - done, halves[half].shape[0] - at)
                    source = halves[half].at[pl.ds(at, step), :]
                    target = out_ref.at[pl.ds(done, step), :]
                    copies.append(pltpu.make_async_copy(source, target, sems.at[len(copies)]))
                    done, at = done + step, at + step
                    if at == halves[half].shape[0]:
                        half, at = half + 1, 0
            for copy in copies:
                copy.start()
            for copy in copies:
                copy.wait()


def sum_everywhere(kept, sent, sizes):
    core = lax.axis_index("dp") % 2
    parts = scatter_pieces([kept, swap(sent, "dp", 1)], False, "dp", 2)
    parts = scatter_pieces(parts, True, "freq", 1)
    x = small_call(
        sum_kernel, "sum_pieces", jax.ShapeDtypeStruct(parts[0].shape, F32), None, *parts
    )
    x = gather_pieces(x, "freq", 1)
    x = gather_pieces(x, "dp", 2)
    other = swap(x, "dp", 1)
    hbm = pl.BlockSpec(memory_space=pl.ANY)
    vmem = pl.BlockSpec(memory_space=pltpu.VMEM)
    return pl.pallas_call(
        spread_kernel,
        out_shape=[jax.ShapeDtypeStruct((rows, x.shape[1]), F32) for rows in sizes],
        in_specs=[pl.BlockSpec(memory_space=pltpu.SMEM), vmem, vmem],
        out_specs=[hbm] * len(sizes),
        scratch_shapes=[pltpu.SemaphoreType.DMA((len(sizes) + 2,))],
        name="spread_rows",
    )(core.reshape(1).astype(jnp.int32), x, other)


def shifted(pieces, axis):
    size = len(pieces)
    return [pieces[0]] + [
        lax.ppermute(pieces[k], axis, [(i, (i + k) % size) for i in range(size)])
        for k in range(1, size)
    ]


def all_of(x, axis):
    size = lax.axis_size(axis)
    pieces = [x]
    for shift in range(1, size):
        pieces.append(lax.ppermute(x, axis, [(i, (i + shift) % size) for i in range(size)]))
    return pieces


def local(records, stem_weight, conv_weight, mix_weight, head_weight, labels, band_bounds):
    freq = lax.axis_size("freq")
    place = lax.axis_index("freq").astype(jnp.int32)
    first_len, cols = records.shape[2:]
    second_len = cols * freq
    total_len = first_len * second_len
    layers, channels = mix_weight.shape[:2]
    classes = head_weight.shape[1]
    blocks = first_len // 2 // LANES
    run = second_len // 8 // freq
    count = 32 * run

    section, twiddle = (jnp.asarray(t) for t in first_tables(first_len, second_len))
    spread, table, flip = (jnp.asarray(t) for t in second_tables(second_len))
    here = place.reshape(1)
    signals = freq // blocks
    chunks = 2 // signals
    sent = [
        first_section(here, records[0], c, signals, freq, section, twiddle) for c in range(chunks)
    ]
    arrived = [shifted(pieces, "freq") for pieces in sent]
    features = [
        second_section(here, a, second_len, total_len, spread, table, flip) for a in arrived
    ]
    received = [piece for f in features for piece in shifted(f, "freq")]
    kernels, kernels_t, mix_t = dense_weights(conv_weight, mix_weight)
    head_t = jnp.pad(head_weight.T, ((0, HALO - classes), (0, 0)))
    steps = jnp.repeat(band_bounds // POOL, GROUP_WIDTH)
    bounds = jnp.stack([steps[:channels], steps[GROUP_WIDTH:]]).astype(jnp.int32)

    vmem = pl.BlockSpec(memory_space=pltpu.VMEM)
    hbm = pl.BlockSpec(memory_space=pl.ANY)
    smem = pl.BlockSpec(memory_space=pltpu.SMEM)
    saved = [
        ((layers, count + HALO, channels), F32),
        ((layers, count + HALO, LANES), F32),
        ((layers, count + 2 * run + HALO, channels), BF16),
        ((count + HALO, 2 * LANES), BF16),
    ]
    *kept, partial = pl.pallas_call(
        functools.partial(forward_kernel, run, freq, chunks),
        out_shape=[jax.ShapeDtypeStruct(s, d) for s, d in saved]
        + [jax.ShapeDtypeStruct((8, channels), F32)],
        in_specs=[smem] + [vmem] * (len(received) + 4),
        out_specs=[hbm] * 4 + [vmem],
        scratch_shapes=[pltpu.VMEM(s, d) for s, d in saved]
        + [
            pltpu.VMEM((count + HALO, channels), F32),
            pltpu.VMEM((HALO, channels), F32),
            pltpu.SemaphoreType.DMA((3 * layers + 1,)),
        ],
        compiler_params=pltpu.CompilerParams(vmem_limit_bytes=56 * 1024 * 1024),
        name="network_ahead",
    )(here, *received, stem_weight, kernels, mix_weight, bounds)

    sums = all_of(partial, "freq")
    core = (lax.axis_index("dp") % 2).astype(jnp.int32)
    scalars = jnp.stack([place, labels[0], jnp.int32(classes), core])
    sizes = [layers * channels, 2 * LANES, layers * KW * GROUP_WIDTH, HALO]
    step = HALO * lax.axis_size("dp") // 2 * freq
    half_rows = -(-sum(sizes) // (2 * step)) * step
    halves = network_back(scalars, sums, kept, bounds, head_t, kernels_t, mix_t, half_rows)
    mix, stem, conv, ends = sum_everywhere(*halves, sizes)
    return (
        ends[HALO - 1, 0],
        stem,
        conv.reshape(layers, KW, GROUP_WIDTH, channels),
        mix.reshape(layers, channels, channels),
        ends[:classes].T,
    )


def solution(mesh):
    in_specs = (P("dp", None, None, "freq"), P(), P(), P(), P(), P("dp"), P())
    out_specs = (P(), P(), P(), P(), P())
    return jax.shard_map(local, mesh=mesh, in_specs=in_specs, out_specs=out_specs, check_vma=False)
```

```python
import functools

import jax
import jax.numpy as jnp
import numpy as np
from jax import lax
from jax.experimental import pallas as pl
from jax.experimental.pallas import tpu as pltpu
from jax.sharding import PartitionSpec as P

POOL = 128
GROUP_WIDTH = 16
KW = 3
EPS = 1e-05
LANES = 128
HALF_MXU = 256
HALO = 16
TILE = 1024
F32 = jnp.float32
BF16 = jnp.bfloat16


def split16(values):
    high = values.astype(BF16)
    return high, (values - high.astype(F32)).astype(BF16)


def table_pair(values):
    high = values.astype(jnp.bfloat16)
    return np.stack([high, (values - high.astype(np.float64)).astype(jnp.bfloat16)])


def first_tables(first_len, second_len):
    total_len = first_len * second_len
    rows = np.arange(first_len // 2)
    odd = 2 * rows + 1
    angles = (np.outer(np.arange(first_len), odd) % (2 * first_len)) * (np.pi / first_len)
    twiddles = (np.outer(np.arange(second_len), odd) % (2 * total_len)) * (np.pi / total_len)

    def by_block(a, b):
        blocks = first_len // 2 // LANES
        a = a.reshape(a.shape[0], blocks, 1, LANES)
        b = b.reshape(b.shape[0], blocks, 1, LANES)
        return np.concatenate([a, b], axis=2).reshape(a.shape[0], -1)

    section = table_pair(by_block(np.cos(angles), -np.sin(angles)))
    twiddle = by_block(np.cos(twiddles), np.sin(twiddles)).astype(np.float32)
    return section, twiddle


def second_tables(second_len):
    quarter = second_len // 4
    idx = np.arange(quarter)
    angles = np.outer(np.arange(1, 4), idx) * (2 * np.pi / second_len)
    spread = np.stack([np.cos(angles), np.sin(angles)], axis=1)[..., None] * np.ones(LANES)
    order = np.concatenate([idx[: quarter // 2], idx[quarter // 2 :][::-1]])
    inner = (np.outer(order, idx) % quarter) * (2 * np.pi / quarter)
    table = table_pair(np.concatenate([np.cos(inner), np.sin(inner)], axis=1))
    flip = np.eye(LANES)[::-1].astype(jnp.bfloat16)
    return spread.astype(np.float32), table, flip


def level_of(exponent, mantissa):
    return mantissa * jnp.exp(exponent * np.log(2.0).astype(np.float32)) * (1.0 / (16384.0 * 32767.0))


def first_kernel(devices, place_ref, x_ref, table_ref, twiddle_ref, *refs):
    outs, (highs, lows, codes) = refs[:devices], refs[devices:]
    signals, cols, _ = highs.shape
    block = pl.program_id(0)

    @pl.when(block == 0)
    def _():
        for signal in range(signals):
            highs[signal], lows[signal] = split16(x_ref[signal].T)

    row = lax.broadcasted_iota(jnp.int32, (HALO, 2 * LANES), 0)
    cosine, sine = twiddle_ref[:, :LANES], twiddle_ref[:, LANES:]
    for signal in range(signals):
        both = jnp.dot(highs[signal], table_ref[0], preferred_element_type=F32)
        both += jnp.dot(lows[signal], table_ref[0], preferred_element_type=F32)
        both += jnp.dot(highs[signal], table_ref[1], preferred_element_type=F32)
        real, imag = both[:, :LANES], both[:, LANES:]
        turned = jnp.concatenate(
            [real * cosine + imag * sine, imag * cosine - real * sine], axis=1
        )
        top = jnp.maximum(jnp.max(jnp.abs(turned), axis=0, keepdims=True), 1e-20)
        exponent = jnp.ceil(jnp.log(top) * (1.0 / np.log(2.0)))
        mantissa = jnp.floor(
            top * jnp.exp(-exponent * np.log(2.0).astype(np.float32)) * 16384.0
        ) + 1.0
        level = 1.0 / level_of(exponent, mantissa)
        codes[:cols, :] = jnp.round(turned * level).astype(jnp.int32).astype(jnp.int16)
        head = jnp.where(row == 0, exponent, jnp.where(row == 1, mantissa, 0.0))
        codes[cols:, :] = head.astype(jnp.int32).astype(jnp.int16)
        for shift in range(devices):

            @pl.when((place_ref[0] + shift) % devices == block * signals + signal)
            def _(shift=shift):
                outs[shift][...] = codes[...]


def first_section(place, records, at, signals, devices, section, twiddle):
    first_len, cols = records.shape[-2:]
    blocks = devices // signals
    shape = (cols + HALO, 2 * LANES)
    return pl.pallas_call(
        functools.partial(first_kernel, devices),
        out_shape=[jax.ShapeDtypeStruct(shape, jnp.int16)] * devices,
        grid_spec=pltpu.PrefetchScalarGridSpec(
            num_scalar_prefetch=1,
            grid=(blocks,),
            in_specs=[
                pl.BlockSpec((signals, first_len, cols), lambda i, s: (at, 0, 0)),
                pl.BlockSpec((2, first_len, 2 * LANES), lambda i, s: (0, 0, i)),
                pl.BlockSpec((cols, 2 * LANES), lambda i, s: (s[0], i)),
            ],
            out_specs=[pl.BlockSpec(shape, lambda i, s: (0, 0))] * devices,
            scratch_shapes=[
                pltpu.VMEM((signals, cols, first_len), BF16),
                pltpu.VMEM((signals, cols, first_len), BF16),
                pltpu.VMEM(shape, jnp.int16),
            ],
        ),
        compiler_params=pltpu.CompilerParams(vmem_limit_bytes=60 * 1024 * 1024),
        cost_estimate=pl.CostEstimate(
            flops=6 * signals * first_len * first_len * cols, bytes_accessed=2**23, transcendentals=0
        ),
        name="first_section",
    )(place, records, section, twiddle)


def second_kernel(devices, total_len, place_ref, *refs):
    received, refs = refs[:devices], refs[devices:]
    (spread_ref, table_ref, flip_ref), refs = refs[:3], refs[3:]
    outs, (signal, right, rest, packed) = refs[:devices], refs[devices:]
    place = place_ref[0]
    cols = signal.shape[0] // devices
    quarter = signal.shape[0] // 4
    run = quarter // 2 // devices
    for shift in range(devices):
        source = (place - shift + devices) % devices
        head = received[shift][cols:, :].astype(jnp.int32).astype(F32)
        values = received[shift][:cols, :].astype(jnp.int32).astype(F32)
        rows = pl.ds(pl.multiple_of(source * cols, cols), cols)
        signal[rows, :] = values * level_of(head[0:1], head[1:2])
    step = min(quarter, 128)
    for at in range(0, quarter, step):
        parts = [signal[g * quarter + at : g * quarter + at + step, :] for g in range(4)]
        re = [v[:, :LANES] for v in parts]
        im = [v[:, LANES:] for v in parts]
        sum_r, dif_r = re[0] + re[2], re[0] - re[2]
        sum_i, dif_i = im[0] + im[2], im[0] - im[2]
        odd_r, odm_r = re[1] + re[3], re[1] - re[3]
        odd_i, odm_i = im[1] + im[3], im[1] - im[3]
        turned = [
            (sum_r + odd_r, sum_i + odd_i),
            (dif_r + odm_i, dif_i - odm_r),
            (sum_r - odd_r, sum_i - odd_i),
            (dif_r - odm_i, dif_i + odm_r),
        ]
        for c in range(4):
            real, imag = turned[c]
            if c:
                cosine = spread_ref[c - 1, 0, at : at + step, :]
                sine = spread_ref[c - 1, 1, at : at + step, :]
                real, imag = real * cosine + imag * sine, imag * cosine - real * sine
            first = slice(2 * LANES * c, 2 * LANES * c + LANES)
            second = slice(2 * LANES * c + LANES, 2 * LANES * (c + 1))
            for ref, r, i in zip((right, rest), split16(real), split16(imag)):
                ref[at : at + step, first] = r
                ref[at : at + step, second] = i
                ref[quarter + at : quarter + at + step, first] = i
                ref[quarter + at : quarter + at + step, second] = -r
    row = lax.broadcasted_iota(jnp.int32, (HALO, LANES), 0)
    edges = [jnp.zeros((HALO, LANES), F32) for _ in range(devices)]
    for c in range(4):
        lanes = slice(2 * LANES * c, 2 * LANES * (c + 1))
        both = jnp.dot(table_ref[0], right[:, lanes], preferred_element_type=F32)
        both += jnp.dot(table_ref[0], rest[:, lanes], preferred_element_type=F32)
        both += jnp.dot(table_ref[1], right[:, lanes], preferred_element_type=F32)
        power = both[:, :LANES] ** 2 + both[:, LANES:] ** 2
        features = jnp.log1p(power * (1.0 / total_len))
        low = features[: quarter // 2].astype(BF16)
        high = jnp.dot(
            features[quarter // 2 :].astype(BF16), flip_ref[...], preferred_element_type=F32
        )
        for part, values, group in ((0, low, c), (1, high.astype(BF16), 4 + 3 - c)):
            wide = values.astype(F32)
            for to in range(devices):
                packed[to, group * run : (group + 1) * run, :] = values[to * run : (to + 1) * run]
                if group % 4 == 3 and to > 0:
                    edges[to] = jnp.where(
                        row == 2 * part, wide[to * run - 1 : to * run], edges[to]
                    )
                if group % 4 == 0 and to < devices - 1:
                    edges[to] = jnp.where(
                        row == 2 * part + 1, wide[(to + 1) * run : (to + 1) * run + 1], edges[to]
                    )
    for to in range(devices):
        packed[to, 8 * run :, :] = edges[to].astype(BF16)
    for shift in range(devices):
        outs[shift][...] = packed[(place + shift) % devices]


def second_section(place, received, second_len, total_len, spread, table, flip):
    devices = len(received)
    quarter = second_len // 4
    run = quarter // 2 // devices
    shape = (8 * run + HALO, LANES)
    vmem = pl.BlockSpec(memory_space=pltpu.VMEM)
    return pl.pallas_call(
        functools.partial(second_kernel, devices, total_len),
        out_shape=[jax.ShapeDtypeStruct(shape, BF16)] * devices,
        in_specs=[pl.BlockSpec(memory_space=pltpu.SMEM)] + [vmem] * (devices + 3),
        out_specs=[vmem] * devices,
        scratch_shapes=[
            pltpu.VMEM((second_len, 2 * LANES), F32),
            pltpu.VMEM((2 * quarter, 8 * LANES), BF16),
            pltpu.VMEM((2 * quarter, 8 * LANES), BF16),
            pltpu.VMEM((devices,) + shape, BF16),
        ],
        compiler_params=pltpu.CompilerParams(vmem_limit_bytes=32 * 1024 * 1024),
        cost_estimate=pl.CostEstimate(
            flops=96 * LANES * quarter * quarter, bytes_accessed=2**23, transcendentals=0
        ),
        name="second_section",
    )(place, *received, spread, table, flip)


def position_column(start, run, at, rows):
    row = at + lax.broadcasted_iota(jnp.int32, (rows, 1), 0)
    return start + row // run + 32 * (row % run)


def halo_column(start, count):
    row = lax.broadcasted_iota(jnp.int32, (HALO, 1), 0)
    return start + jnp.where(row < 8, row - 8, count + row - 8)


def silu_gate(v):
    return 0.5 + 0.5 * jnp.tanh(0.5 * v)


def close_ends(padded, halo, run):
    count = padded.shape[0] - 2 * run - HALO
    row = lax.broadcasted_iota(jnp.int32, (run, 1), 0)
    tail = padded[count : count + run, :].astype(F32)
    head = padded[run : 2 * run, :].astype(F32)
    before = jnp.where(row == 0, halo[7:8], pltpu.roll(tail, 1, 0))
    after = jnp.where(row == run - 1, halo[8:9], pltpu.roll(head, run - 1, 0))
    padded[:run, :] = before.astype(BF16)
    padded[run + count : 2 * run + count, :] = after.astype(BF16)
    padded[2 * run + count :, :] = halo.astype(BF16)
    row = lax.broadcasted_iota(jnp.int32, (HALO, 1), 0)
    down = jnp.where(row == 8, tail[run - 1 : run], pltpu.roll(halo, 1, 0))
    up = jnp.where(row == 7, head[:1], pltpu.roll(halo, HALO - 1, 0))
    return [v.astype(BF16) for v in (down, halo, up)]


def taps_product(windows, kernels):
    halves = []
    for half in range(kernels.shape[0]):
        lanes = slice(half * HALF_MXU, (half + 1) * HALF_MXU)
        total = None
        for tap in range(KW):
            term = jnp.dot(
                windows[tap](lanes), kernels[half, tap], preferred_element_type=F32
            )
            total = term if total is None else total + term
        halves.append(total)
    return jnp.concatenate(halves, axis=1)


def forward_kernel(run, devices, chunks, place_ref, *refs):
    received, refs = refs[: chunks * devices], refs[chunks * devices :]
    (stem_in, kernels_in, mix_in, bounds, preacts_out, scales_out, padded_out, feats_out, partial_out,
     preacts, scales, padded, feats, stem, kernels, mix, stream, halos, sems, sems_in, sems_tile) = refs
    layers = mix.shape[0]
    weights = [pltpu.make_async_copy(stem_in, stem, sems_in.at[0])]
    for layer in range(layers):
        for k, (src, dst) in enumerate(((kernels_in, kernels), (mix_in, mix))):
            weights.append(
                pltpu.make_async_copy(src.at[layer], dst.at[layer], sems_in.at[1 + 2 * layer + k])
            )
    for copy in weights:
        copy.start()
    count = 32 * run
    place = place_ref[0]
    start = place * count
    signals = 2 // chunks
    blocks = devices // signals

    row16 = lax.broadcasted_iota(jnp.int32, (HALO, LANES), 0)
    edge = [jnp.zeros((HALO, LANES), F32) for _ in range(2)]
    for chunk in range(chunks):
        for shift in range(devices):
            ref = received[chunk * devices + shift]
            source = (place - shift + devices) % devices
            ends = ref[8 * run :, :].astype(F32)
            channel = chunk if chunks == 2 else source % 2
            lanes = pl.ds(pl.multiple_of(channel * LANES, LANES), LANES)
            for part in range(2):
                block = source // signals
                block = 2 * blocks - 1 - block if part else block
                for c in range(4):
                    at = pl.multiple_of((block + 8 * c) * run, run)
                    feats[pl.ds(at, run), lanes] = ref[
                        (part * 4 + c) * run : (part * 4 + c + 1) * run, :
                    ]
                for which in range(2):
                    value = ends[2 * part + which : 2 * part + which + 1]
                    at = row16 == block + 8 * which
                    for k in range(2):
                        edge[k] = jnp.where(at & (channel == k), value, edge[k])
    for k in range(2):
        feats[count:, k * LANES : (k + 1) * LANES] = edge[k].astype(BF16)
    copies = []

    saved = []

    def save(source, target):
        copy = pltpu.make_async_copy(source, target, sems.at[len(saved)])
        copy.start()
        saved.append(copy)

    save(feats, feats_out)
    halo_place = halo_column(start, count)
    inside = ((halo_place >= 0) & (halo_place < devices * count)).astype(F32)
    tile = min(TILE, count)

    def norm(layer, rows, values):
        scale = lax.rsqrt(jnp.mean(values * values, axis=-1, keepdims=True) + EPS)
        scales[layer, rows, :] = jnp.broadcast_to(scale, (values.shape[0], LANES))
        return values * scale

    def put_normed(layer, at, values):
        normed = norm(layer, pl.ds(at, tile), values)
        padded[layer, pl.ds(pl.multiple_of(at + run, run), tile), :] = normed.astype(BF16)

    def stem_tile(i, _):
        at = pl.multiple_of(i * tile, tile)
        values = jnp.dot(feats[pl.ds(at, tile), :], stem[...], preferred_element_type=F32)
        stream[pl.ds(at, tile), :] = values
        put_normed(0, at, values)
        return 0

    weights[0].wait()
    lax.fori_loop(0, count // tile, stem_tile, 0)
    values = jnp.dot(feats[count:, :], stem[...], preferred_element_type=F32)
    stream[count:, :] = values
    halos[...] = norm(0, slice(count, count + HALO), values) * inside
    partial_out[...] = jnp.zeros_like(partial_out)

    for layer in range(layers):
        here = padded.at[layer]
        windows = close_ends(here, halos[...].astype(BF16).astype(F32), run)
        save(here, padded_out.at[layer])
        save(scales.at[layer], scales_out.at[layer])
        last = layer == layers - 1
        weights[1 + 2 * layer].wait()
        weights[2 + 2 * layer].wait()

        def save_tile(i, layer=layer):
            rows = pl.ds(pl.multiple_of(i * tile, tile), tile)
            return pltpu.make_async_copy(
                preacts.at[layer, rows, :], preacts_out.at[layer, rows, :], sems_tile.at[layer, i]
            )

        def layer_tile(i, _, layer=layer, here=here, last=last, save_tile=save_tile):
            at = pl.multiple_of(i * tile, tile)
            rows = pl.ds(at, tile)
            taps = [
                lambda lanes, t=t: here[pl.ds(pl.multiple_of(at + t * run, run), tile), lanes]
                for t in range(KW)
            ]
            preact = taps_product(taps, kernels.at[layer])
            preacts[layer, rows, :] = preact
            save_tile(i).start()
            active = (preact * silu_gate(preact)).astype(BF16)
            values = stream[rows, :] + jnp.dot(active, mix[layer], preferred_element_type=F32)
            if last:
                place = position_column(start, run, at, tile)
                member = (place >= bounds[0:1, :]) & (place < bounds[1:2, :])
                kept = jnp.where(member, values, 0.0)
                partial_out[...] += jnp.sum(kept.reshape(tile // 8, 8, kept.shape[1]), axis=0)
            else:
                stream[rows, :] = values
                put_normed(layer + 1, at, values)
            return 0

        lax.fori_loop(0, count // tile, layer_tile, 0)
        preact = taps_product([lambda lanes, v=v: v[:, lanes] for v in windows], kernels.at[layer])
        preacts[layer, count:, :] = preact
        rest = pl.ds(count, HALO)
        save(preacts.at[layer, rest, :], preacts_out.at[layer, rest, :])
        copies.extend(save_tile(i) for i in range(count // tile))
        if not last:
            active = (preact * silu_gate(preact)).astype(BF16)
            values = stream[count:, :] + jnp.dot(active, mix[layer], preferred_element_type=F32)
            stream[count:, :] = values
            halos[...] = norm(layer + 1, slice(count, count + HALO), values) * inside
    for copy in saved + copies:
        copy.wait()


def backward_kernel(run, devices, all_records, place_ref, *refs):
    sums, refs = refs[:devices], refs[devices:]
    (preacts_in, scales_in, padded_in, feats_in, bounds, head, kernels_in, mix_in, kept, sent,
     preacts, scales, padded, feats, kernels, mix_t, sums_out, grad, ahead, active_t, out16,
     sems, sems_out) = refs
    layers = mix_t.shape[0]
    channels = grad.shape[1]
    count = 32 * run
    start = place_ref[0] * count
    core = place_ref[3]
    tile = min(TILE, count)
    tiles = count // tile

    arriving = []
    for layer in reversed(range(layers)):
        cuts = [pl.ds(k * tile, tile) for k in range(tiles)] + [pl.ds(count, HALO)]
        copies = [(preacts_in.at[layer, cut, :], preacts.at[layer, cut, :]) for cut in cuts]
        copies += [(padded_in.at[layer], padded.at[layer]), (scales_in.at[layer], scales.at[layer])]
        copies += [(kernels_in.at[layer], kernels.at[layer])]
        copies = [(mix_in.at[layer], mix_t.at[layer])] + copies
        arriving.append(copies)
    arriving.append([(feats_in, feats)])
    at = 0
    for k, copies in enumerate(arriving):
        arriving[k] = [
            pltpu.make_async_copy(*copy, sems.at[at + j]) for j, copy in enumerate(copies)
        ]
        at += len(copies)
        for copy in arriving[k]:
            copy.start()

    half_rows = kept.shape[0]
    leaving = []

    def put(at, value):
        sums_out[at : at + value.shape[0], :] = value

    def leave(at, rows):
        half, to = divmod(at, half_rows)
        source, sem = sums_out.at[pl.ds(at, rows), :], sems_out.at[len(leaving)]
        to = pl.ds(to, rows)
        leaving.append(pltpu.make_async_copy(source, kept.at[to, :], sem))

        @pl.when(core == half)
        def _():
            pltpu.make_async_copy(source, kept.at[to, :], sem).start()

        @pl.when(core != half)
        def _():
            pltpu.make_async_copy(source, sent.at[to, :], sem).start()

    total = sums[0][...]
    for ref in sums[1:]:
        total = total + ref[...]
    band_sum = jnp.sum(total, axis=0, keepdims=True)
    counts = (bounds[1:2, :] - bounds[0:1, :]).astype(F32)
    pooled = band_sum / counts
    row = lax.broadcasted_iota(jnp.int32, (HALO, 1), 0)
    logits = jnp.sum(head[...] * pooled, axis=1, keepdims=True)
    exponents = jnp.where(row < place_ref[2], jnp.exp(logits), 0.0)
    denominator = jnp.sum(exponents, axis=0, keepdims=True)
    one_hot = (row == place_ref[1]).astype(F32)
    loss = jnp.log(denominator) - jnp.sum(one_hot * logits, axis=0, keepdims=True)
    loss = loss / all_records
    grad_logits = (exponents / denominator - one_hot) / all_records
    grad_pooled = jnp.sum(head[...] * grad_logits, axis=0, keepdims=True)
    grad_band = grad_pooled / counts
    lead = (place_ref[0] == 0).astype(F32)
    stem_at = layers * channels
    conv_at = stem_at + 2 * LANES
    head_at = conv_at + layers * KW * GROUP_WIDTH
    put(head_at, lead * jnp.where(row == HALO - 1, loss, grad_logits * pooled))
    rest = 2 * half_rows - head_at - HALO
    if rest:
        put(head_at + HALO, jnp.zeros((rest, channels), F32))

    def spread(place):
        member = (place >= bounds[0:1, :]) & (place < bounds[1:2, :])
        return jnp.where(member, grad_band, 0.0)

    halo_place = halo_column(start, count)
    inside = ((halo_place >= 0) & (halo_place < devices * count)).astype(F32)
    grad[count:, :] = spread(halo_place)

    def gate_grad(value, grad_act):
        gate = silu_gate(value)
        return grad_act * gate * (1.0 + value * (1.0 - gate)), value * gate

    def stream_grad(layer, outgoing, rows, normed, grad_normed):
        scale = jnp.concatenate([scales[layer, rows, :]] * (channels // LANES), axis=1)
        normed = normed.astype(F32)
        inner = jnp.mean(normed * grad_normed, axis=-1, keepdims=True)
        return outgoing + scale * (grad_normed - normed * inner)

    at_row = lax.broadcasted_iota(jnp.int32, (HALF_MXU, HALF_MXU), 0) // GROUP_WIDTH
    at_col = lax.broadcasted_iota(jnp.int32, (HALF_MXU, HALF_MXU), 1) // GROUP_WIDTH
    for layer in reversed(range(layers)):
        copies = arriving[layers - 1 - layer]
        top, bottom = layer == layers - 1, layer == 0

        def act_tile(i, _, layer=layer, top=top):
            at = pl.multiple_of(i * tile, tile)
            rows = pl.ds(at, tile)
            if top:
                values = spread(position_column(start, run, at, tile))
                grad[rows, :] = values
            else:
                values = grad[rows, :]
            outgoing = values.astype(BF16)
            out16[rows, :] = outgoing
            grad_act = jnp.dot(outgoing, mix_t[layer], preferred_element_type=F32)
            grad_pre, act = gate_grad(preacts[layer, rows, :], grad_act)
            grad_pre = grad_pre.astype(BF16)
            active_t[:, rows] = act.astype(BF16).T
            ahead[pl.ds(pl.multiple_of(at + run, run), tile), :] = grad_pre
            return 0

        copies[0].wait()
        if top:
            for k in range(tiles):
                copies[1 + k].wait()
                lax.fori_loop(k, k + 1, act_tile, 0)
        else:
            for k in range(tiles):
                copies[1 + k].wait()
            lax.fori_loop(0, tiles, act_tile, 0)
        copies[1 + tiles].wait()
        grad_act = jnp.dot(grad[count:, :].astype(BF16), mix_t[layer], preferred_element_type=F32)
        halo, _ = gate_grad(preacts[layer, count:, :], grad_act)
        halo = (halo * inside).astype(BF16).astype(F32)
        windows = close_ends(ahead, halo, run)

        put(
            layer * channels,
            jnp.dot(active_t[...], out16[...], preferred_element_type=F32),
        )
        leave(layer * channels, channels)

        copies[tiles + 2].wait()
        for tap in range(KW):
            folded = []
            for half in range(channels // HALF_MXU):
                lanes = slice(half * HALF_MXU, (half + 1) * HALF_MXU)
                full = lax.dot_general(
                    padded[layer, tap * run : tap * run + count, lanes],
                    ahead[run : run + count, lanes],
                    (((0,), (0,)), ((), ())),
                    preferred_element_type=F32,
                )
                full = jnp.where(at_row == at_col, full, 0.0)
                folded.append(
                    jnp.sum(full.reshape(HALF_MXU // GROUP_WIDTH, GROUP_WIDTH, HALF_MXU), axis=0)
                )
            at = conv_at + (layer * KW + tap) * GROUP_WIDTH
            put(at, jnp.concatenate(folded, axis=1))
        copies[tiles + 3].wait()
        copies[tiles + 4].wait()

        def stream_tile(i, _, layer=layer, bottom=bottom):
            at = pl.multiple_of(i * tile, tile)
            rows = pl.ds(at, tile)
            taps = [
                lambda lanes, t=t: ahead[
                    pl.ds(pl.multiple_of(at + (KW - 1 - t) * run, run), tile), lanes
                ]
                for t in range(KW)
            ]
            grad_normed = taps_product(taps, kernels.at[layer])
            normed = padded[layer, pl.ds(pl.multiple_of(at + run, run), tile), :]
            value = stream_grad(layer, grad[rows, :], rows, normed, grad_normed)
            if bottom:
                high, low = split16(value)
                out16[rows, :] = high
                active_t[:, rows] = low.T
            else:
                grad[rows, :] = value
            return 0

        lax.fori_loop(0, tiles, stream_tile, 0)
        if not bottom:
            grad_normed = taps_product(
                [lambda lanes, v=v: v[:, lanes] for v in reversed(windows)], kernels.at[layer]
            )
            normed = padded[layer, count + 2 * run :, :]
            rows = slice(count, count + HALO)
            grad[rows, :] = stream_grad(layer, grad[rows, :], rows, normed, grad_normed)

    arriving[-1][0].wait()
    value = lax.dot_general(
        feats[:count, :], out16[...], (((0,), (0,)), ((), ())), preferred_element_type=F32
    )
    rest = jnp.dot(active_t[...], feats[:count, :], preferred_element_type=F32)
    put(stem_at, value + rest.T)
    leave(stem_at, 2 * half_rows - stem_at)
    for copy in leaving:
        copy.wait()


def network_back(scalars, sums, saved, bounds, head_t, kernels_t, mix_t, half_rows):
    preacts, scales, padded, feats = saved
    layers, rows, channels = preacts.shape
    count = rows - HALO
    tiles = count // min(TILE, count)
    devices = len(sums)
    vmem = pl.BlockSpec(memory_space=pltpu.VMEM)
    hbm = pl.BlockSpec(memory_space=pl.ANY)
    return pl.pallas_call(
        functools.partial(backward_kernel, count // 32, devices, lax.axis_size("dp")),
        out_shape=[jax.ShapeDtypeStruct((half_rows, channels), F32)] * 2,
        in_specs=[pl.BlockSpec(memory_space=pltpu.SMEM)]
        + [vmem] * devices
        + [hbm] * 4
        + [vmem] * 2
        + [hbm] * 2,
        out_specs=[hbm] * 2,
        scratch_shapes=[pltpu.VMEM(x.shape, x.dtype) for x in saved]
        + [
            pltpu.VMEM(kernels_t.shape, BF16),
            pltpu.VMEM(mix_t.shape, BF16),
            pltpu.VMEM((2 * half_rows, channels), F32),
            pltpu.VMEM((rows, channels), F32),
            pltpu.VMEM(padded.shape[1:], BF16),
            pltpu.VMEM((channels, count), BF16),
            pltpu.VMEM((count, channels), BF16),
            pltpu.SemaphoreType.DMA((layers * (tiles + 5) + 1,)),
            pltpu.SemaphoreType.DMA((layers + 1,)),
        ],
        compiler_params=pltpu.CompilerParams(vmem_limit_bytes=60 * 1024 * 1024),
        name="network_back",
    )(scalars, *sums, *saved, bounds, head_t, kernels_t, mix_t)


def weights_kernel(conv_ref, mix_ref, kernels_ref, turned_ref, mix_t_ref):
    row = lax.broadcasted_iota(jnp.int32, (HALF_MXU, HALF_MXU), 0) // GROUP_WIDTH
    col = lax.broadcasted_iota(jnp.int32, (HALF_MXU, HALF_MXU), 1) // GROUP_WIDTH
    for tap in range(KW):
        for half in range(kernels_ref.shape[0]):
            taps = conv_ref[tap, :, half * HALF_MXU : (half + 1) * HALF_MXU].astype(F32)
            dense = jnp.concatenate([taps] * (HALF_MXU // GROUP_WIDTH), axis=0)
            dense = jnp.where(row == col, dense, 0.0)
            kernels_ref[half, tap] = dense.astype(BF16)
            turned_ref[half, tap] = dense.T.astype(BF16)
    mix_t_ref[...] = mix_ref[...].astype(F32).T.astype(BF16)


def dense_weights(conv_weight, mix_weight):
    layers, taps, width, channels = conv_weight.shape
    dense = (layers, channels // HALF_MXU, taps, HALF_MXU, HALF_MXU)
    by_layer = lambda shape: pl.BlockSpec(
        (None,) + shape[1:], lambda i: (i,) + (0,) * (len(shape) - 1)
    )
    return pl.pallas_call(
        weights_kernel,
        out_shape=[
            jax.ShapeDtypeStruct(dense, BF16),
            jax.ShapeDtypeStruct(dense, BF16),
            jax.ShapeDtypeStruct(mix_weight.shape, BF16),
        ],
        grid=(layers,),
        in_specs=[by_layer(conv_weight.shape), by_layer(mix_weight.shape)],
        out_specs=[by_layer(dense), by_layer(dense), by_layer(mix_weight.shape)],
        compiler_params=pltpu.CompilerParams(vmem_limit_bytes=32 * 1024 * 1024),
        cost_estimate=pl.CostEstimate(flops=0, bytes_accessed=2**24, transcendentals=0),
        name="dense_weights",
    )(conv_weight, mix_weight)


def swap(x, axis, step):
    return lax.ppermute(x, axis, [(i, i ^ step) for i in range(lax.axis_size(axis))])


def encode(values, out_ref):
    rows = values.shape[0]
    top = jnp.maximum(jnp.max(jnp.abs(values), axis=1, keepdims=True), 1e-30)
    exponent = jnp.ceil(jnp.log(top) * (1.0 / np.log(2.0)) + 1e-4)
    scale = jnp.exp(-exponent * np.log(2.0).astype(np.float32)) * 32767.0
    out_ref[:rows, :] = jnp.round(values * scale).astype(jnp.int32).astype(jnp.int16)
    out_ref[rows:, :] = jnp.zeros((HALO, values.shape[1]), jnp.int16)
    across = jnp.broadcast_to(exponent, (rows, LANES)).T[:HALO, :]
    out_ref[rows:, :rows] = across.astype(jnp.int32).astype(jnp.int16)


def decode(ref):
    rows = ref.shape[0] - HALO
    across = ref[rows:, :rows].astype(jnp.int32).astype(F32)
    exponent = jnp.concatenate([across] * (LANES // HALO), axis=0).T[:, :1]
    scale = jnp.exp(exponent * np.log(2.0).astype(np.float32)) * (1.0 / 32767.0)
    return ref[:rows, :].astype(jnp.int32).astype(F32) * scale


def cut_kernel(size, place_ref, *refs):
    inputs, outs = refs[:-size], refs[-size:]
    rows = inputs[0].shape[0] // size
    for k in range(size):
        at = pl.multiple_of((place_ref[0] ^ k) * rows, rows)
        value = inputs[0][pl.ds(at, rows), :]
        for ref in inputs[1:]:
            value = value + ref[pl.ds(at, rows), :]
        if k:
            encode(value, outs[k])
        else:
            outs[0][...] = value


def sum_kernel(first_ref, *refs):
    value = first_ref[...]
    for ref in refs[:-1]:
        value = value + decode(ref)
    refs[-1][...] = value


def pieces_kernel(place_ref, *refs):
    inputs, out_ref = refs[:-1], refs[-1]
    rows = inputs[0].shape[0] - HALO
    for k, ref in enumerate(inputs):
        at = pl.multiple_of((place_ref[0] ^ k) * rows, rows)
        out_ref[pl.ds(at, rows), :] = decode(ref)


def encode_kernel(x_ref, out_ref):
    encode(x_ref[...], out_ref)


def small_call(kernel, name, out_shape, place, *args):
    vmem = pl.BlockSpec(memory_space=pltpu.VMEM)
    smem = pl.BlockSpec(memory_space=pltpu.SMEM)
    several = isinstance(out_shape, list)
    lead = [] if place is None else [place.reshape(1).astype(jnp.int32)]
    return pl.pallas_call(
        kernel,
        out_shape=out_shape,
        in_specs=[smem] * len(lead) + [vmem] * len(args),
        out_specs=[vmem] * len(out_shape) if several else vmem,
        compiler_params=pltpu.CompilerParams(vmem_limit_bytes=32 * 1024 * 1024),
        name=name,
    )(*lead, *args)


def scatter_pieces(parts, coded, axis, stride):
    size = lax.axis_size(axis) // stride
    place = lax.axis_index(axis) // stride
    rows, channels = parts[0].shape[0] // size, parts[0].shape[1]
    if coded:
        whole = jax.ShapeDtypeStruct(parts[0].shape, F32)
        parts = [small_call(sum_kernel, "sum_pieces", whole, None, *parts)]
    shapes = [jax.ShapeDtypeStruct((rows, channels), F32)]
    shapes += [jax.ShapeDtypeStruct((rows + HALO, channels), jnp.int16)] * (size - 1)
    own, *others = small_call(
        functools.partial(cut_kernel, size), "cut_pieces", shapes, place, *parts
    )
    return [own] + [swap(piece, axis, (k + 1) * stride) for k, piece in enumerate(others)]


def gather_pieces(x, axis, stride):
    size = lax.axis_size(axis) // stride
    place = lax.axis_index(axis) // stride
    rows, channels = x.shape
    shape = jax.ShapeDtypeStruct((rows + HALO, channels), jnp.int16)
    coded = small_call(encode_kernel, "code_piece", shape, None, x)
    pieces = [coded] + [swap(coded, axis, k * stride) for k in range(1, size)]
    whole = jax.ShapeDtypeStruct((size * rows, channels), F32)
    return small_call(pieces_kernel, "lay_pieces", whole, place, *pieces)


def spread_half(core, half_ref, is_mine, outs, sems):
    half_rows = half_ref.shape[0]
    for half in range(2):

        @pl.when((core == half) if is_mine else (core != half))
        def _(half=half):
            copies, first = [], 0
            for out_ref in outs:
                low = max(first, half * half_rows)
                high = min(first + out_ref.shape[0], (half + 1) * half_rows)
                if low < high:
                    copies.append(
                        pltpu.make_async_copy(
                            half_ref.at[pl.ds(low - half * half_rows, high - low), :],
                            out_ref.at[pl.ds(low - first, high - low), :],
                            sems.at[len(copies)],
                        )
                    )
                first += out_ref.shape[0]
            for copy in copies:
                copy.start()
            for copy in copies:
                copy.wait()


def spread_mine(core_ref, mine_ref, *refs):
    spread_half(core_ref[0], mine_ref, True, refs[:-1], refs[-1])


def spread_other(classes, head_at, core_ref, mine_ref, other_ref, *refs):
    refs = refs[(len(refs) - 3) // 2 :]
    *outs, head_ref, loss_ref, sems = refs
    spread_half(core_ref[0], other_ref, False, outs, sems)
    half, at = divmod(head_at, mine_ref.shape[0])
    mine, other = mine_ref[at : at + HALO, :], other_ref[at : at + HALO, :]
    ends = jnp.where(core_ref[0] == half, mine, other)
    head_ref[...] = ends[:classes]
    loss_ref[...] = ends[HALO - 1 : HALO, :1]


def sum_everywhere(kept, sent, sizes, classes):
    core = (lax.axis_index("dp") % 2).reshape(1).astype(jnp.int32)
    parts = scatter_pieces([kept, swap(sent, "dp", 1)], False, "dp", 2)
    parts = scatter_pieces(parts, True, "freq", 1)
    x = small_call(
        sum_kernel, "sum_pieces", jax.ShapeDtypeStruct(parts[0].shape, F32), None, *parts
    )
    x = gather_pieces(x, "freq", 1)
    x = gather_pieces(x, "dp", 2)
    other = swap(x, "dp", 1)
    channels = x.shape[1]
    shapes = [jax.ShapeDtypeStruct((rows, channels), F32) for rows in sizes[:-1]]
    hbm = pl.BlockSpec(memory_space=pl.ANY)
    vmem = pl.BlockSpec(memory_space=pltpu.VMEM)
    smem = pl.BlockSpec(memory_space=pltpu.SMEM)
    sems = [pltpu.SemaphoreType.DMA((len(sizes),))]
    halves = pl.pallas_call(
        spread_mine,
        out_shape=shapes,
        in_specs=[smem, vmem],
        out_specs=[hbm] * len(shapes),
        scratch_shapes=sems,
        cost_estimate=pl.CostEstimate(flops=0, bytes_accessed=2**23, transcendentals=0),
        name="spread_mine",
    )(core, x)
    return pl.pallas_call(
        functools.partial(spread_other, classes, sum(sizes[:-1])),
        out_shape=shapes
        + [
            jax.ShapeDtypeStruct((classes, channels), F32),
            jax.ShapeDtypeStruct((1, 1), F32),
        ],
        in_specs=[smem, vmem, vmem] + [hbm] * len(shapes),
        out_specs=[hbm] * len(shapes) + [vmem] * 2,
        scratch_shapes=sems,
        input_output_aliases={3 + k: k for k in range(len(shapes))},
        name="spread_other",
    )(core, x, other, *halves)


def shifted(pieces, axis):
    size = len(pieces)
    return [pieces[0]] + [
        lax.ppermute(pieces[k], axis, [(i, (i + k) % size) for i in range(size)])
        for k in range(1, size)
    ]


def all_of(x, axis):
    size = lax.axis_size(axis)
    pieces = [x]
    for shift in range(1, size):
        pieces.append(lax.ppermute(x, axis, [(i, (i + shift) % size) for i in range(size)]))
    return pieces


def local(records, stem_weight, conv_weight, mix_weight, head_weight, labels, band_bounds):
    freq = lax.axis_size("freq")
    place = lax.axis_index("freq").astype(jnp.int32)
    first_len, cols = records.shape[2:]
    second_len = cols * freq
    total_len = first_len * second_len
    layers, channels = mix_weight.shape[:2]
    classes = head_weight.shape[1]
    blocks = first_len // 2 // LANES
    run = second_len // 8 // freq
    count = 32 * run

    section, twiddle = (jnp.asarray(t) for t in first_tables(first_len, second_len))
    spread, table, flip = (jnp.asarray(t) for t in second_tables(second_len))
    here = place.reshape(1)
    signals = freq // blocks
    chunks = 2 // signals
    sent = [
        first_section(here, records[0], c, signals, freq, section, twiddle) for c in range(chunks)
    ]
    arrived = [shifted(pieces, "freq") for pieces in sent]
    features = [
        second_section(here, a, second_len, total_len, spread, table, flip) for a in arrived
    ]
    received = [piece for f in features for piece in shifted(f, "freq")]
    kernels, kernels_t, mix_t = dense_weights(conv_weight, mix_weight)
    head_t = jnp.pad(head_weight.T, ((0, HALO - classes), (0, 0)))
    steps = jnp.repeat(band_bounds // POOL, GROUP_WIDTH)
    bounds = jnp.stack([steps[:channels], steps[GROUP_WIDTH:]]).astype(jnp.int32)

    vmem = pl.BlockSpec(memory_space=pltpu.VMEM)
    hbm = pl.BlockSpec(memory_space=pl.ANY)
    smem = pl.BlockSpec(memory_space=pltpu.SMEM)
    saved = [
        ((layers, count + HALO, channels), F32),
        ((layers, count + HALO, LANES), F32),
        ((layers, count + 2 * run + HALO, channels), BF16),
        ((count + HALO, 2 * LANES), BF16),
    ]
    *kept, partial = pl.pallas_call(
        functools.partial(forward_kernel, run, freq, chunks),
        out_shape=[jax.ShapeDtypeStruct(s, d) for s, d in saved]
        + [jax.ShapeDtypeStruct((8, channels), F32)],
        in_specs=[smem] + [vmem] * len(received) + [hbm] * 3 + [vmem],
        out_specs=[hbm] * 4 + [vmem],
        scratch_shapes=[pltpu.VMEM(s, d) for s, d in saved]
        + [
            pltpu.VMEM(stem_weight.shape, BF16),
            pltpu.VMEM(kernels.shape, BF16),
            pltpu.VMEM(mix_weight.shape, BF16),
            pltpu.VMEM((count + HALO, channels), F32),
            pltpu.VMEM((HALO, channels), F32),
            pltpu.SemaphoreType.DMA((3 * layers + 1,)),
            pltpu.SemaphoreType.DMA((2 * layers + 1,)),
            pltpu.SemaphoreType.DMA((layers, count // min(TILE, count))),
        ],
        compiler_params=pltpu.CompilerParams(vmem_limit_bytes=56 * 1024 * 1024),
        name="network_ahead",
    )(here, *received, stem_weight, kernels, mix_weight, bounds)

    sums = all_of(partial, "freq")
    core = (lax.axis_index("dp") % 2).astype(jnp.int32)
    scalars = jnp.stack([place, labels[0], jnp.int32(classes), core])
    sizes = [layers * channels, 2 * LANES, layers * KW * GROUP_WIDTH, HALO]
    step = HALO * lax.axis_size("dp") // 2 * freq
    half_rows = -(-sum(sizes) // (2 * step)) * step
    halves = network_back(scalars, sums, kept, bounds, head_t, kernels_t, mix_t, half_rows)
    mix, stem, conv, head, loss = sum_everywhere(*halves, sizes, classes)
    return (
        loss.reshape(()),
        stem,
        conv.reshape(layers, KW, GROUP_WIDTH, channels),
        mix.reshape(layers, channels, channels),
        head.T,
    )


def solution(mesh):
    in_specs = (P("dp", None, None, "freq"), P(), P(), P(), P(), P("dp"), P())
    out_specs = (P(), P(), P(), P(), P())
    return jax.shard_map(local, mesh=mesh, in_specs=in_specs, out_specs=out_specs, check_vma=False)
```

```python
import functools

import jax
import jax.numpy as jnp
import numpy as np
from jax import lax
from jax.experimental import pallas as pl
from jax.experimental.pallas import tpu as pltpu
from jax.sharding import PartitionSpec as P

POOL = 128
GROUP_WIDTH = 16
KW = 3
EPS = 1e-05
LANES = 128
HALF_MXU = 256
HALO = 16
TILE = 1024
F32 = jnp.float32
BF16 = jnp.bfloat16


def split16(values):
    high = values.astype(BF16)
    return high, (values - high.astype(F32)).astype(BF16)


def table_pair(values):
    high = values.astype(jnp.bfloat16)
    return np.stack([high, (values - high.astype(np.float64)).astype(jnp.bfloat16)])


def first_tables(first_len, second_len):
    total_len = first_len * second_len
    rows = np.arange(first_len // 2)
    odd = 2 * rows + 1
    angles = (np.outer(np.arange(first_len), odd) % (2 * first_len)) * (np.pi / first_len)
    twiddles = (np.outer(np.arange(second_len), odd) % (2 * total_len)) * (np.pi / total_len)

    def by_block(a, b):
        blocks = first_len // 2 // LANES
        a = a.reshape(a.shape[0], blocks, 1, LANES)
        b = b.reshape(b.shape[0], blocks, 1, LANES)
        return np.concatenate([a, b], axis=2).reshape(a.shape[0], -1)

    section = table_pair(by_block(np.cos(angles), -np.sin(angles)))
    twiddle = by_block(np.cos(twiddles), np.sin(twiddles)).astype(np.float32)
    return section, twiddle


def second_tables(second_len):
    quarter = second_len // 4
    idx = np.arange(quarter)
    angles = np.outer(np.arange(1, 4), idx) * (2 * np.pi / second_len)
    spread = np.stack([np.cos(angles), np.sin(angles)], axis=1)[..., None] * np.ones(LANES)
    order = np.concatenate([idx[: quarter // 2], idx[quarter // 2 :][::-1]])
    inner = (np.outer(order, idx) % quarter) * (2 * np.pi / quarter)
    table = table_pair(np.concatenate([np.cos(inner), np.sin(inner)], axis=1))
    flip = np.eye(LANES)[::-1].astype(jnp.bfloat16)
    return spread.astype(np.float32), table, flip


def level_of(exponent, mantissa):
    return mantissa * jnp.exp(exponent * np.log(2.0).astype(np.float32)) * (1.0 / (16384.0 * 32767.0))


def first_kernel(devices, place_ref, x_ref, table_ref, twiddle_ref, *refs):
    outs, (highs, lows, codes) = refs[:devices], refs[devices:]
    signals, cols, _ = highs.shape
    block = pl.program_id(0)

    @pl.when(block == 0)
    def _():
        for signal in range(signals):
            highs[signal], lows[signal] = split16(x_ref[signal].T)

    row = lax.broadcasted_iota(jnp.int32, (HALO, 2 * LANES), 0)
    cosine, sine = twiddle_ref[:, :LANES], twiddle_ref[:, LANES:]
    for signal in range(signals):
        both = jnp.dot(highs[signal], table_ref[0], preferred_element_type=F32)
        both += jnp.dot(lows[signal], table_ref[0], preferred_element_type=F32)
        both += jnp.dot(highs[signal], table_ref[1], preferred_element_type=F32)
        real, imag = both[:, :LANES], both[:, LANES:]
        turned = jnp.concatenate(
            [real * cosine + imag * sine, imag * cosine - real * sine], axis=1
        )
        top = jnp.maximum(jnp.max(jnp.abs(turned), axis=0, keepdims=True), 1e-20)
        exponent = jnp.ceil(jnp.log(top) * (1.0 / np.log(2.0)))
        mantissa = jnp.floor(
            top * jnp.exp(-exponent * np.log(2.0).astype(np.float32)) * 16384.0
        ) + 1.0
        level = 1.0 / level_of(exponent, mantissa)
        codes[:cols, :] = jnp.round(turned * level).astype(jnp.int32).astype(jnp.int16)
        head = jnp.where(row == 0, exponent, jnp.where(row == 1, mantissa, 0.0))
        codes[cols:, :] = head.astype(jnp.int32).astype(jnp.int16)
        for shift in range(devices):

            @pl.when((place_ref[0] ^ shift) == block * signals + signal)
            def _(shift=shift):
                outs[shift][...] = codes[...]


def first_section(place, records, at, signals, devices, section, twiddle):
    first_len, cols = records.shape[-2:]
    blocks = devices // signals
    shape = (cols + HALO, 2 * LANES)
    return pl.pallas_call(
        functools.partial(first_kernel, devices),
        out_shape=[jax.ShapeDtypeStruct(shape, jnp.int16)] * devices,
        grid_spec=pltpu.PrefetchScalarGridSpec(
            num_scalar_prefetch=1,
            grid=(blocks,),
            in_specs=[
                pl.BlockSpec((signals, first_len, cols), lambda i, s: (at, 0, 0)),
                pl.BlockSpec((2, first_len, 2 * LANES), lambda i, s: (0, 0, i)),
                pl.BlockSpec((cols, 2 * LANES), lambda i, s: (s[0], i)),
            ],
            out_specs=[pl.BlockSpec(shape, lambda i, s: (0, 0))] * devices,
            scratch_shapes=[
                pltpu.VMEM((signals, cols, first_len), BF16),
                pltpu.VMEM((signals, cols, first_len), BF16),
                pltpu.VMEM(shape, jnp.int16),
            ],
        ),
        compiler_params=pltpu.CompilerParams(vmem_limit_bytes=60 * 1024 * 1024),
        cost_estimate=pl.CostEstimate(
            flops=6 * signals * first_len * first_len * cols, bytes_accessed=2**23, transcendentals=0
        ),
        name="first_section",
    )(place, records, section, twiddle)


def second_kernel(devices, total_len, place_ref, *refs):
    received, refs = refs[:devices], refs[devices:]
    (spread_ref, table_ref, flip_ref), refs = refs[:3], refs[3:]
    outs, (signal, right, rest, packed) = refs[:devices], refs[devices:]
    place = place_ref[0]
    cols = signal.shape[0] // devices
    quarter = signal.shape[0] // 4
    run = quarter // 2 // devices
    for shift in range(devices):
        source = place ^ shift
        head = received[shift][cols:, :].astype(jnp.int32).astype(F32)
        values = received[shift][:cols, :].astype(jnp.int32).astype(F32)
        rows = pl.ds(pl.multiple_of(source * cols, cols), cols)
        signal[rows, :] = values * level_of(head[0:1], head[1:2])
    step = min(quarter, 128)
    for at in range(0, quarter, step):
        parts = [signal[g * quarter + at : g * quarter + at + step, :] for g in range(4)]
        re = [v[:, :LANES] for v in parts]
        im = [v[:, LANES:] for v in parts]
        sum_r, dif_r = re[0] + re[2], re[0] - re[2]
        sum_i, dif_i = im[0] + im[2], im[0] - im[2]
        odd_r, odm_r = re[1] + re[3], re[1] - re[3]
        odd_i, odm_i = im[1] + im[3], im[1] - im[3]
        turned = [
            (sum_r + odd_r, sum_i + odd_i),
            (dif_r + odm_i, dif_i - odm_r),
            (sum_r - odd_r, sum_i - odd_i),
            (dif_r - odm_i, dif_i + odm_r),
        ]
        for c in range(4):
            real, imag = turned[c]
            if c:
                cosine = spread_ref[c - 1, 0, at : at + step, :]
                sine = spread_ref[c - 1, 1, at : at + step, :]
                real, imag = real * cosine + imag * sine, imag * cosine - real * sine
            first = slice(2 * LANES * c, 2 * LANES * c + LANES)
            second = slice(2 * LANES * c + LANES, 2 * LANES * (c + 1))
            for ref, r, i in zip((right, rest), split16(real), split16(imag)):
                ref[at : at + step, first] = r
                ref[at : at + step, second] = i
                ref[quarter + at : quarter + at + step, first] = i
                ref[quarter + at : quarter + at + step, second] = -r
    row = lax.broadcasted_iota(jnp.int32, (HALO, LANES), 0)
    edges = [jnp.zeros((HALO, LANES), F32) for _ in range(devices)]
    for c in range(4):
        lanes = slice(2 * LANES * c, 2 * LANES * (c + 1))
        both = jnp.dot(table_ref[0], right[:, lanes], preferred_element_type=F32)
        both += jnp.dot(table_ref[0], rest[:, lanes], preferred_element_type=F32)
        both += jnp.dot(table_ref[1], right[:, lanes], preferred_element_type=F32)
        power = both[:, :LANES] ** 2 + both[:, LANES:] ** 2
        features = jnp.log1p(power * (1.0 / total_len))
        low = features[: quarter // 2].astype(BF16)
        high = jnp.dot(
            features[quarter // 2 :].astype(BF16), flip_ref[...], preferred_element_type=F32
        )
        for part, values, group in ((0, low, c), (1, high.astype(BF16), 4 + 3 - c)):
            wide = values.astype(F32)
            for to in range(devices):
                packed[to, group * run : (group + 1) * run, :] = values[to * run : (to + 1) * run]
                if group % 4 == 3 and to > 0:
                    edges[to] = jnp.where(
                        row == 2 * part, wide[to * run - 1 : to * run], edges[to]
                    )
                if group % 4 == 0 and to < devices - 1:
                    edges[to] = jnp.where(
                        row == 2 * part + 1, wide[(to + 1) * run : (to + 1) * run + 1], edges[to]
                    )
    for to in range(devices):
        packed[to, 8 * run :, :] = edges[to].astype(BF16)
    for shift in range(devices):
        outs[shift][...] = packed[place ^ shift]


def second_section(place, received, second_len, total_len, spread, table, flip):
    devices = len(received)
    quarter = second_len // 4
    run = quarter // 2 // devices
    shape = (8 * run + HALO, LANES)
    vmem = pl.BlockSpec(memory_space=pltpu.VMEM)
    return pl.pallas_call(
        functools.partial(second_kernel, devices, total_len),
        out_shape=[jax.ShapeDtypeStruct(shape, BF16)] * devices,
        in_specs=[pl.BlockSpec(memory_space=pltpu.SMEM)] + [vmem] * (devices + 3),
        out_specs=[vmem] * devices,
        scratch_shapes=[
            pltpu.VMEM((second_len, 2 * LANES), F32),
            pltpu.VMEM((2 * quarter, 8 * LANES), BF16),
            pltpu.VMEM((2 * quarter, 8 * LANES), BF16),
            pltpu.VMEM((devices,) + shape, BF16),
        ],
        compiler_params=pltpu.CompilerParams(vmem_limit_bytes=32 * 1024 * 1024),
        cost_estimate=pl.CostEstimate(
            flops=96 * LANES * quarter * quarter, bytes_accessed=2**23, transcendentals=0
        ),
        name="second_section",
    )(place, *received, spread, table, flip)


def position_column(start, run, at, rows):
    row = at + lax.broadcasted_iota(jnp.int32, (rows, 1), 0)
    return start + row // run + 32 * (row % run)


def halo_column(start, count):
    row = lax.broadcasted_iota(jnp.int32, (HALO, 1), 0)
    return start + jnp.where(row < 8, row - 8, count + row - 8)


def silu_gate(v):
    return 0.5 + 0.5 * jnp.tanh(0.5 * v)


def close_ends(padded, halo, run):
    count = padded.shape[0] - 2 * run - HALO
    row = lax.broadcasted_iota(jnp.int32, (run, 1), 0)
    tail = padded[count : count + run, :].astype(F32)
    head = padded[run : 2 * run, :].astype(F32)
    before = jnp.where(row == 0, halo[7:8], pltpu.roll(tail, 1, 0))
    after = jnp.where(row == run - 1, halo[8:9], pltpu.roll(head, run - 1, 0))
    padded[:run, :] = before.astype(BF16)
    padded[run + count : 2 * run + count, :] = after.astype(BF16)
    padded[2 * run + count :, :] = halo.astype(BF16)
    row = lax.broadcasted_iota(jnp.int32, (HALO, 1), 0)
    down = jnp.where(row == 8, tail[run - 1 : run], pltpu.roll(halo, 1, 0))
    up = jnp.where(row == 7, head[:1], pltpu.roll(halo, HALO - 1, 0))
    return [v.astype(BF16) for v in (down, halo, up)]


def taps_product(windows, kernels):
    halves = []
    for half in range(kernels.shape[0]):
        lanes = slice(half * HALF_MXU, (half + 1) * HALF_MXU)
        total = None
        for tap in range(KW):
            term = jnp.dot(
                windows[tap](lanes), kernels[half, tap], preferred_element_type=F32
            )
            total = term if total is None else total + term
        halves.append(total)
    return jnp.concatenate(halves, axis=1)


def forward_kernel(run, devices, chunks, place_ref, *refs):
    received, refs = refs[: chunks * devices], refs[chunks * devices :]
    (stem_in, kernels_in, mix_in, bounds, preacts_out, scales_out, padded_out, feats_out, partial_out,
     preacts, scales, padded, feats, stem, kernels, mix, stream, halos, sems, sems_in, sems_tile) = refs
    layers = mix.shape[0]
    weights = [pltpu.make_async_copy(stem_in, stem, sems_in.at[0])]
    for layer in range(layers):
        for k, (src, dst) in enumerate(((kernels_in, kernels), (mix_in, mix))):
            weights.append(
                pltpu.make_async_copy(src.at[layer], dst.at[layer], sems_in.at[1 + 2 * layer + k])
            )
    for copy in weights:
        copy.start()
    count = 32 * run
    place = place_ref[0]
    start = place * count
    signals = 2 // chunks
    blocks = devices // signals

    row16 = lax.broadcasted_iota(jnp.int32, (HALO, LANES), 0)
    edge = [jnp.zeros((HALO, LANES), F32) for _ in range(2)]
    for chunk in range(chunks):
        for shift in range(devices):
            ref = received[chunk * devices + shift]
            source = place ^ shift
            ends = ref[8 * run :, :].astype(F32)
            channel = chunk if chunks == 2 else source % 2
            lanes = pl.ds(pl.multiple_of(channel * LANES, LANES), LANES)
            for part in range(2):
                block = source // signals
                block = 2 * blocks - 1 - block if part else block
                for c in range(4):
                    at = pl.multiple_of((block + 8 * c) * run, run)
                    feats[pl.ds(at, run), lanes] = ref[
                        (part * 4 + c) * run : (part * 4 + c + 1) * run, :
                    ]
                for which in range(2):
                    value = ends[2 * part + which : 2 * part + which + 1]
                    at = row16 == block + 8 * which
                    for k in range(2):
                        edge[k] = jnp.where(at & (channel == k), value, edge[k])
    for k in range(2):
        feats[count:, k * LANES : (k + 1) * LANES] = edge[k].astype(BF16)
    copies = []

    saved = []

    def save(source, target):
        copy = pltpu.make_async_copy(source, target, sems.at[len(saved)])
        copy.start()
        saved.append(copy)

    save(feats, feats_out)
    halo_place = halo_column(start, count)
    inside = ((halo_place >= 0) & (halo_place < devices * count)).astype(F32)
    tile = min(TILE, count)

    def norm(layer, rows, values):
        scale = lax.rsqrt(jnp.mean(values * values, axis=-1, keepdims=True) + EPS)
        scales[layer, rows, :] = jnp.broadcast_to(scale, (values.shape[0], LANES))
        return values * scale

    def put_normed(layer, at, values):
        normed = norm(layer, pl.ds(at, tile), values)
        padded[layer, pl.ds(pl.multiple_of(at + run, run), tile), :] = normed.astype(BF16)

    def stem_tile(i, _):
        at = pl.multiple_of(i * tile, tile)
        values = jnp.dot(feats[pl.ds(at, tile), :], stem[...], preferred_element_type=F32)
        stream[pl.ds(at, tile), :] = values
        put_normed(0, at, values)
        return 0

    weights[0].wait()
    lax.fori_loop(0, count // tile, stem_tile, 0)
    values = jnp.dot(feats[count:, :], stem[...], preferred_element_type=F32)
    stream[count:, :] = values
    halos[...] = norm(0, slice(count, count + HALO), values) * inside
    partial_out[...] = jnp.zeros_like(partial_out)

    for layer in range(layers):
        here = padded.at[layer]
        windows = close_ends(here, halos[...].astype(BF16).astype(F32), run)
        save(here, padded_out.at[layer])
        save(scales.at[layer], scales_out.at[layer])
        last = layer == layers - 1
        weights[1 + 2 * layer].wait()
        weights[2 + 2 * layer].wait()

        def save_tile(i, layer=layer):
            rows = pl.ds(pl.multiple_of(i * tile, tile), tile)
            return pltpu.make_async_copy(
                preacts.at[layer, rows, :], preacts_out.at[layer, rows, :], sems_tile.at[layer, i]
            )

        def layer_tile(i, _, layer=layer, here=here, last=last, save_tile=save_tile):
            at = pl.multiple_of(i * tile, tile)
            rows = pl.ds(at, tile)
            taps = [
                lambda lanes, t=t: here[pl.ds(pl.multiple_of(at + t * run, run), tile), lanes]
                for t in range(KW)
            ]
            preact = taps_product(taps, kernels.at[layer])
            preacts[layer, rows, :] = preact
            save_tile(i).start()
            active = (preact * silu_gate(preact)).astype(BF16)
            values = stream[rows, :] + jnp.dot(active, mix[layer], preferred_element_type=F32)
            if last:
                place = position_column(start, run, at, tile)
                member = (place >= bounds[0:1, :]) & (place < bounds[1:2, :])
                kept = jnp.where(member, values, 0.0)
                partial_out[...] += jnp.sum(kept.reshape(tile // 8, 8, kept.shape[1]), axis=0)
            else:
                stream[rows, :] = values
                put_normed(layer + 1, at, values)
            return 0

        lax.fori_loop(0, count // tile, layer_tile, 0)
        preact = taps_product([lambda lanes, v=v: v[:, lanes] for v in windows], kernels.at[layer])
        preacts[layer, count:, :] = preact
        rest = pl.ds(count, HALO)
        save(preacts.at[layer, rest, :], preacts_out.at[layer, rest, :])
        copies.extend(save_tile(i) for i in range(count // tile))
        if not last:
            active = (preact * silu_gate(preact)).astype(BF16)
            values = stream[count:, :] + jnp.dot(active, mix[layer], preferred_element_type=F32)
            stream[count:, :] = values
            halos[...] = norm(layer + 1, slice(count, count + HALO), values) * inside
    for copy in saved + copies:
        copy.wait()


def backward_kernel(run, devices, all_records, place_ref, *refs):
    sums, refs = refs[:devices], refs[devices:]
    (preacts_in, scales_in, padded_in, feats_in, bounds, head, kernels_in, mix_in, kept, sent,
     preacts, scales, padded, feats, kernels, mix_t, sums_out, codes, grad, ahead, active_t, out16,
     sems, sems_out) = refs
    layers = mix_t.shape[0]
    channels = grad.shape[1]
    count = 32 * run
    start = place_ref[0] * count
    core = place_ref[3]
    tile = min(TILE, count)
    tiles = count // tile

    arriving = []
    for layer in reversed(range(layers)):
        cuts = [pl.ds(k * tile, tile) for k in range(tiles)] + [pl.ds(count, HALO)]
        copies = [(preacts_in.at[layer, cut, :], preacts.at[layer, cut, :]) for cut in cuts]
        copies += [(padded_in.at[layer], padded.at[layer]), (scales_in.at[layer], scales.at[layer])]
        copies += [(kernels_in.at[layer], kernels.at[layer])]
        copies = [(mix_in.at[layer], mix_t.at[layer])] + copies
        arriving.append(copies)
    arriving.append([(feats_in, feats)])
    at = 0
    for k, copies in enumerate(arriving):
        arriving[k] = [
            pltpu.make_async_copy(*copy, sems.at[at + j]) for j, copy in enumerate(copies)
        ]
        at += len(copies)
        for copy in arriving[k]:
            copy.start()

    half_rows = kept.shape[0]
    leaving = []

    def put(at, value):
        sums_out[at : at + value.shape[0], :] = value

    def leave(region):
        half, inside = divmod(region, sent.shape[0])
        rows = pl.ds(region * channels, channels)
        sem = sems_out.at[region]
        plain = pltpu.make_async_copy(
            sums_out.at[rows, :], kept.at[pl.ds(inside * channels, channels), :], sem
        )
        coded = pltpu.make_async_copy(codes.at[region], sent.at[inside], sem)
        leaving.append((half, plain, coded))

        @pl.when(core == half)
        def _():
            plain.start()

        @pl.when(core != half)
        def _():
            encode(sums_out[rows, :], codes.at[region])
            coded.start()

    total = sums[0][...]
    for ref in sums[1:]:
        total = total + ref[...]
    band_sum = jnp.sum(total, axis=0, keepdims=True)
    counts = (bounds[1:2, :] - bounds[0:1, :]).astype(F32)
    pooled = band_sum / counts
    row = lax.broadcasted_iota(jnp.int32, (HALO, 1), 0)
    logits = jnp.sum(head[...] * pooled, axis=1, keepdims=True)
    exponents = jnp.where(row < place_ref[2], jnp.exp(logits), 0.0)
    denominator = jnp.sum(exponents, axis=0, keepdims=True)
    one_hot = (row == place_ref[1]).astype(F32)
    loss = jnp.log(denominator) - jnp.sum(one_hot * logits, axis=0, keepdims=True)
    loss = loss / all_records
    grad_logits = (exponents / denominator - one_hot) / all_records
    grad_pooled = jnp.sum(head[...] * grad_logits, axis=0, keepdims=True)
    grad_band = grad_pooled / counts
    lead = (place_ref[0] == 0).astype(F32)
    stem_at = layers * channels
    conv_at = stem_at + 2 * LANES
    head_at = conv_at + layers * KW * GROUP_WIDTH
    put(head_at, lead * jnp.where(row == HALO - 1, loss, grad_logits * pooled))
    rest = 2 * half_rows - head_at - HALO
    if rest:
        put(head_at + HALO, jnp.zeros((rest, channels), F32))

    def spread(place):
        member = (place >= bounds[0:1, :]) & (place < bounds[1:2, :])
        return jnp.where(member, grad_band, 0.0)

    halo_place = halo_column(start, count)
    inside = ((halo_place >= 0) & (halo_place < devices * count)).astype(F32)
    grad[count:, :] = spread(halo_place)

    def gate_grad(value, grad_act):
        gate = silu_gate(value)
        return grad_act * gate * (1.0 + value * (1.0 - gate)), value * gate

    def stream_grad(layer, outgoing, rows, normed, grad_normed):
        scale = jnp.concatenate([scales[layer, rows, :]] * (channels // LANES), axis=1)
        normed = normed.astype(F32)
        inner = jnp.mean(normed * grad_normed, axis=-1, keepdims=True)
        return outgoing + scale * (grad_normed - normed * inner)

    at_row = lax.broadcasted_iota(jnp.int32, (HALF_MXU, HALF_MXU), 0) // GROUP_WIDTH
    at_col = lax.broadcasted_iota(jnp.int32, (HALF_MXU, HALF_MXU), 1) // GROUP_WIDTH
    for layer in reversed(range(layers)):
        copies = arriving[layers - 1 - layer]
        top, bottom = layer == layers - 1, layer == 0

        def act_tile(i, _, layer=layer, top=top):
            at = pl.multiple_of(i * tile, tile)
            rows = pl.ds(at, tile)
            if top:
                values = spread(position_column(start, run, at, tile))
                grad[rows, :] = values
            else:
                values = grad[rows, :]
            outgoing = values.astype(BF16)
            out16[rows, :] = outgoing
            grad_act = jnp.dot(outgoing, mix_t[layer], preferred_element_type=F32)
            grad_pre, act = gate_grad(preacts[layer, rows, :], grad_act)
            grad_pre = grad_pre.astype(BF16)
            active_t[:, rows] = act.astype(BF16).T
            ahead[pl.ds(pl.multiple_of(at + run, run), tile), :] = grad_pre
            return 0

        copies[0].wait()
        if top:
            for k in range(tiles):
                copies[1 + k].wait()
                lax.fori_loop(k, k + 1, act_tile, 0)
        else:
            for k in range(tiles):
                copies[1 + k].wait()
            lax.fori_loop(0, tiles, act_tile, 0)
        copies[1 + tiles].wait()
        grad_act = jnp.dot(grad[count:, :].astype(BF16), mix_t[layer], preferred_element_type=F32)
        halo, _ = gate_grad(preacts[layer, count:, :], grad_act)
        halo = (halo * inside).astype(BF16).astype(F32)
        windows = close_ends(ahead, halo, run)

        put(
            layer * channels,
            jnp.dot(active_t[...], out16[...], preferred_element_type=F32),
        )
        leave(layer)

        copies[tiles + 2].wait()
        for tap in range(KW):
            folded = []
            for half in range(channels // HALF_MXU):
                lanes = slice(half * HALF_MXU, (half + 1) * HALF_MXU)
                full = lax.dot_general(
                    padded[layer, tap * run : tap * run + count, lanes],
                    ahead[run : run + count, lanes],
                    (((0,), (0,)), ((), ())),
                    preferred_element_type=F32,
                )
                full = jnp.where(at_row == at_col, full, 0.0)
                folded.append(
                    jnp.sum(full.reshape(HALF_MXU // GROUP_WIDTH, GROUP_WIDTH, HALF_MXU), axis=0)
                )
            at = conv_at + (layer * KW + tap) * GROUP_WIDTH
            put(at, jnp.concatenate(folded, axis=1))
        copies[tiles + 3].wait()
        copies[tiles + 4].wait()

        def stream_tile(i, _, layer=layer, bottom=bottom):
            at = pl.multiple_of(i * tile, tile)
            rows = pl.ds(at, tile)
            taps = [
                lambda lanes, t=t: ahead[
                    pl.ds(pl.multiple_of(at + (KW - 1 - t) * run, run), tile), lanes
                ]
                for t in range(KW)
            ]
            grad_normed = taps_product(taps, kernels.at[layer])
            normed = padded[layer, pl.ds(pl.multiple_of(at + run, run), tile), :]
            value = stream_grad(layer, grad[rows, :], rows, normed, grad_normed)
            if bottom:
                high, low = split16(value)
                out16[rows, :] = high
                active_t[:, rows] = low.T
            else:
                grad[rows, :] = value
            return 0

        lax.fori_loop(0, tiles, stream_tile, 0)
        if not bottom:
            grad_normed = taps_product(
                [lambda lanes, v=v: v[:, lanes] for v in reversed(windows)], kernels.at[layer]
            )
            normed = padded[layer, count + 2 * run :, :]
            rows = slice(count, count + HALO)
            grad[rows, :] = stream_grad(layer, grad[rows, :], rows, normed, grad_normed)

    arriving[-1][0].wait()
    value = lax.dot_general(
        feats[:count, :], out16[...], (((0,), (0,)), ((), ())), preferred_element_type=F32
    )
    rest = jnp.dot(active_t[...], feats[:count, :], preferred_element_type=F32)
    put(stem_at, value + rest.T)
    leave(layers)
    for half, plain, coded in leaving:
        pl.when(core == half)(plain.wait)
        pl.when(core != half)(coded.wait)


def network_back(scalars, sums, saved, bounds, head_t, kernels_t, mix_t, half_rows):
    preacts, scales, padded, feats = saved
    layers, rows, channels = preacts.shape
    count = rows - HALO
    tiles = count // min(TILE, count)
    devices = len(sums)
    region = (channels + HALO, channels)
    vmem = pl.BlockSpec(memory_space=pltpu.VMEM)
    hbm = pl.BlockSpec(memory_space=pl.ANY)
    return pl.pallas_call(
        functools.partial(backward_kernel, count // 32, devices, lax.axis_size("dp")),
        out_shape=[
            jax.ShapeDtypeStruct((half_rows, channels), F32),
            jax.ShapeDtypeStruct((half_rows // channels,) + region, jnp.int16),
        ],
        in_specs=[pl.BlockSpec(memory_space=pltpu.SMEM)]
        + [vmem] * devices
        + [hbm] * 4
        + [vmem] * 2
        + [hbm] * 2,
        out_specs=[hbm] * 2,
        scratch_shapes=[pltpu.VMEM(x.shape, x.dtype) for x in saved]
        + [
            pltpu.VMEM(kernels_t.shape, BF16),
            pltpu.VMEM(mix_t.shape, BF16),
            pltpu.VMEM((2 * half_rows, channels), F32),
            pltpu.VMEM((2 * half_rows // channels,) + region, jnp.int16),
            pltpu.VMEM((rows, channels), F32),
            pltpu.VMEM(padded.shape[1:], BF16),
            pltpu.VMEM((channels, count), BF16),
            pltpu.VMEM((count, channels), BF16),
            pltpu.SemaphoreType.DMA((layers * (tiles + 5) + 1,)),
            pltpu.SemaphoreType.DMA((layers + 1,)),
        ],
        compiler_params=pltpu.CompilerParams(vmem_limit_bytes=60 * 1024 * 1024),
        name="network_back",
    )(scalars, *sums, *saved, bounds, head_t, kernels_t, mix_t)


def weights_kernel(conv_ref, mix_ref, kernels_ref, turned_ref, mix_t_ref):
    row = lax.broadcasted_iota(jnp.int32, (HALF_MXU, HALF_MXU), 0) // GROUP_WIDTH
    col = lax.broadcasted_iota(jnp.int32, (HALF_MXU, HALF_MXU), 1) // GROUP_WIDTH
    for tap in range(KW):
        for half in range(kernels_ref.shape[0]):
            taps = conv_ref[tap, :, half * HALF_MXU : (half + 1) * HALF_MXU].astype(F32)
            dense = jnp.concatenate([taps] * (HALF_MXU // GROUP_WIDTH), axis=0)
            dense = jnp.where(row == col, dense, 0.0)
            kernels_ref[half, tap] = dense.astype(BF16)
            turned_ref[half, tap] = dense.T.astype(BF16)
    mix_t_ref[...] = mix_ref[...].astype(F32).T.astype(BF16)


def dense_weights(conv_weight, mix_weight):
    layers, taps, width, channels = conv_weight.shape
    dense = (layers, channels // HALF_MXU, taps, HALF_MXU, HALF_MXU)
    by_layer = lambda shape: pl.BlockSpec(
        (None,) + shape[1:], lambda i: (i,) + (0,) * (len(shape) - 1)
    )
    return pl.pallas_call(
        weights_kernel,
        out_shape=[
            jax.ShapeDtypeStruct(dense, BF16),
            jax.ShapeDtypeStruct(dense, BF16),
            jax.ShapeDtypeStruct(mix_weight.shape, BF16),
        ],
        grid=(layers,),
        in_specs=[by_layer(conv_weight.shape), by_layer(mix_weight.shape)],
        out_specs=[by_layer(dense), by_layer(dense), by_layer(mix_weight.shape)],
        compiler_params=pltpu.CompilerParams(vmem_limit_bytes=32 * 1024 * 1024),
        cost_estimate=pl.CostEstimate(flops=0, bytes_accessed=2**24, transcendentals=0),
        name="dense_weights",
    )(conv_weight, mix_weight)


def swap(x, axis, step):
    return lax.ppermute(x, axis, [(i, i ^ step) for i in range(lax.axis_size(axis))])


def encode(values, out_ref):
    rows = values.shape[0]
    top = jnp.maximum(jnp.max(jnp.abs(values), axis=1, keepdims=True), 1e-30)
    exponent = jnp.ceil(jnp.log(top) * (1.0 / np.log(2.0)) + 1e-4)
    scale = jnp.exp(-exponent * np.log(2.0).astype(np.float32)) * 32767.0
    out_ref[:rows, :] = jnp.round(values * scale).astype(jnp.int32).astype(jnp.int16)
    out_ref[rows:, :] = jnp.zeros((HALO, values.shape[1]), jnp.int16)
    across = jnp.broadcast_to(exponent, (rows, LANES)).T[:HALO, :]
    out_ref[rows:, :rows] = across.astype(jnp.int32).astype(jnp.int16)


def decode(ref, at=0, rows=None):
    total = ref.shape[0] - HALO
    rows = total if rows is None else rows
    across = ref[total:, pl.ds(at, rows)].astype(jnp.int32).astype(F32)
    exponent = jnp.concatenate([across] * (LANES // HALO), axis=0).T[:, :1]
    scale = jnp.exp(exponent * np.log(2.0).astype(np.float32)) * (1.0 / 32767.0)
    return ref[pl.ds(at, rows), :].astype(jnp.int32).astype(F32) * scale


def cut_kernel(size, place_ref, whole_ref, *refs):
    regions, outs = refs[:-size], refs[-size:]
    rows = whole_ref.shape[0] // size
    for k in range(size):
        at = pl.multiple_of((place_ref[0] ^ k) * rows, rows)
        value = whole_ref[pl.ds(at, rows), :]
        for ref in regions:
            height = ref.shape[1] - HALO
            inside = pl.multiple_of(at % height, rows)
            value = value + decode(ref.at[at // height], inside, rows)
        if k:
            encode(value, outs[k])
        else:
            outs[0][...] = value


def sum_kernel(first_ref, *refs):
    value = first_ref[...]
    for ref in refs[:-1]:
        value = value + decode(ref)
    refs[-1][...] = value


def pieces_kernel(place_ref, *refs):
    inputs, out_ref = refs[:-1], refs[-1]
    rows = inputs[0].shape[0] - HALO
    for k, ref in enumerate(inputs):
        at = pl.multiple_of((place_ref[0] ^ k) * rows, rows)
        out_ref[pl.ds(at, rows), :] = decode(ref)


def coded_pieces_kernel(place_ref, *refs):
    inputs, out_ref = refs[:-1], refs[-1]
    for k, ref in enumerate(inputs):
        out_ref[place_ref[0] ^ k] = ref[...]


def encode_kernel(x_ref, out_ref):
    encode(x_ref[...], out_ref)


def small_call(kernel, name, out_shape, place, *args):
    vmem = pl.BlockSpec(memory_space=pltpu.VMEM)
    smem = pl.BlockSpec(memory_space=pltpu.SMEM)
    several = isinstance(out_shape, list)
    lead = [] if place is None else [place.reshape(1).astype(jnp.int32)]
    return pl.pallas_call(
        kernel,
        out_shape=out_shape,
        in_specs=[smem] * len(lead) + [vmem] * len(args),
        out_specs=[vmem] * len(out_shape) if several else vmem,
        compiler_params=pltpu.CompilerParams(vmem_limit_bytes=32 * 1024 * 1024),
        name=name,
    )(*lead, *args)


def scatter_pieces(whole, regions, axis, stride):
    size = lax.axis_size(axis) // stride
    place = lax.axis_index(axis) // stride
    rows, channels = whole.shape[0] // size, whole.shape[1]
    shapes = [jax.ShapeDtypeStruct((rows, channels), F32)]
    shapes += [jax.ShapeDtypeStruct((rows + HALO, channels), jnp.int16)] * (size - 1)
    own, *others = small_call(
        functools.partial(cut_kernel, size), "cut_pieces", shapes, place, whole, *regions
    )
    parts = [own] + [swap(piece, axis, (k + 1) * stride) for k, piece in enumerate(others)]
    return small_call(
        sum_kernel, "sum_pieces", jax.ShapeDtypeStruct((rows, channels), F32), None, *parts
    )


def gather_pieces(x, axis, stride, coded):
    size = lax.axis_size(axis) // stride
    place = lax.axis_index(axis) // stride
    rows, channels = x.shape
    piece = (rows + HALO, channels)
    mine = small_call(encode_kernel, "code_piece", jax.ShapeDtypeStruct(piece, jnp.int16), None, x)
    pieces = [mine] + [swap(mine, axis, k * stride) for k in range(1, size)]
    if coded:
        shape = jax.ShapeDtypeStruct((size,) + piece, jnp.int16)
        return small_call(coded_pieces_kernel, "lay_coded_pieces", shape, place, *pieces)
    shape = jax.ShapeDtypeStruct((size * rows, channels), F32)
    return small_call(pieces_kernel, "lay_pieces", shape, place, *pieces)


def spread_half(core, coded_ref, half_ref, is_mine, outs, sems):
    half_rows = half_ref.shape[0]
    rows = half_rows // coded_ref.shape[0]
    for k in range(coded_ref.shape[0]):
        half_ref[k * rows : (k + 1) * rows, :] = decode(coded_ref.at[k])
    for half in range(2):

        @pl.when((core == half) if is_mine else (core != half))
        def _(half=half):
            copies, first = [], 0
            for out_ref in outs:
                low = max(first, half * half_rows)
                high = min(first + out_ref.shape[0], (half + 1) * half_rows)
                if low < high:
                    copies.append(
                        pltpu.make_async_copy(
                            half_ref.at[pl.ds(low - half * half_rows, high - low), :],
                            out_ref.at[pl.ds(low - first, high - low), :],
                            sems.at[len(copies)],
                        )
                    )
                first += out_ref.shape[0]
            for copy in copies:
                copy.start()
            for copy in copies:
                copy.wait()


def spread_mine(core_ref, mine_ref, *refs):
    *outs, half_ref, sems = refs
    spread_half(core_ref[0], mine_ref, half_ref, True, outs, sems)


def spread_other(classes, head_at, core_ref, mine_ref, other_ref, *refs):
    refs = refs[(len(refs) - 4) // 2 :]
    *outs, head_ref, loss_ref, half_ref, sems = refs
    spread_half(core_ref[0], other_ref, half_ref, False, outs, sems)
    half, at = divmod(head_at, half_ref.shape[0])
    piece, inside = divmod(at, mine_ref.shape[1] - HALO)
    mine = decode(mine_ref.at[piece])[inside : inside + HALO]
    ends = jnp.where(core_ref[0] == half, mine, half_ref[at : at + HALO, :])
    head_ref[...] = ends[:classes]
    loss_ref[...] = ends[HALO - 1 : HALO, :1]


def sum_everywhere(kept, sent, sizes, classes):
    core = (lax.axis_index("dp") % 2).reshape(1).astype(jnp.int32)
    x = scatter_pieces(kept, [swap(sent, "dp", 1)], "dp", 2)
    x = scatter_pieces(x, [], "freq", 1)
    x = gather_pieces(x, "freq", 1, False)
    x = gather_pieces(x, "dp", 2, True)
    other = swap(x, "dp", 1)
    channels = x.shape[2]
    shapes = [jax.ShapeDtypeStruct((rows, channels), F32) for rows in sizes[:-1]]
    hbm = pl.BlockSpec(memory_space=pl.ANY)
    vmem = pl.BlockSpec(memory_space=pltpu.VMEM)
    smem = pl.BlockSpec(memory_space=pltpu.SMEM)
    scratch = [pltpu.VMEM(kept.shape, F32), pltpu.SemaphoreType.DMA((len(sizes),))]
    halves = pl.pallas_call(
        spread_mine,
        out_shape=shapes,
        in_specs=[smem, vmem],
        out_specs=[hbm] * len(shapes),
        scratch_shapes=scratch,
        compiler_params=pltpu.CompilerParams(vmem_limit_bytes=32 * 1024 * 1024),
        cost_estimate=pl.CostEstimate(flops=0, bytes_accessed=2**23, transcendentals=0),
        name="spread_mine",
    )(core, x)
    return pl.pallas_call(
        functools.partial(spread_other, classes, sum(sizes[:-1])),
        out_shape=shapes
        + [
            jax.ShapeDtypeStruct((classes, channels), F32),
            jax.ShapeDtypeStruct((1, 1), F32),
        ],
        in_specs=[smem, vmem, vmem] + [hbm] * len(shapes),
        out_specs=[hbm] * len(shapes) + [vmem] * 2,
        scratch_shapes=scratch,
        input_output_aliases={3 + k: k for k in range(len(shapes))},
        compiler_params=pltpu.CompilerParams(vmem_limit_bytes=32 * 1024 * 1024),
        name="spread_other",
    )(core, x, other, *halves)


def traded(pieces, axis):
    return [pieces[0]] + [swap(pieces[k], axis, k) for k in range(1, len(pieces))]


def local(records, stem_weight, conv_weight, mix_weight, head_weight, labels, band_bounds):
    freq = lax.axis_size("freq")
    place = lax.axis_index("freq").astype(jnp.int32)
    first_len, cols = records.shape[2:]
    second_len = cols * freq
    total_len = first_len * second_len
    layers, channels = mix_weight.shape[:2]
    classes = head_weight.shape[1]
    blocks = first_len // 2 // LANES
    run = second_len // 8 // freq
    count = 32 * run

    section, twiddle = (jnp.asarray(t) for t in first_tables(first_len, second_len))
    spread, table, flip = (jnp.asarray(t) for t in second_tables(second_len))
    here = place.reshape(1)
    signals = freq // blocks
    chunks = 2 // signals
    sent = [
        first_section(here, records[0], c, signals, freq, section, twiddle) for c in range(chunks)
    ]
    arrived = [traded(pieces, "freq") for pieces in sent]
    dense = dense_weights(conv_weight, mix_weight)
    arrived[0], (kernels, kernels_t, mix_t) = lax.optimization_barrier((arrived[0], dense))
    features = [
        second_section(here, a, second_len, total_len, spread, table, flip) for a in arrived
    ]
    received = [piece for f in features for piece in traded(f, "freq")]
    head_t = jnp.pad(head_weight.T, ((0, HALO - classes), (0, 0)))
    steps = jnp.repeat(band_bounds // POOL, GROUP_WIDTH)
    bounds = jnp.stack([steps[:channels], steps[GROUP_WIDTH:]]).astype(jnp.int32)

    vmem = pl.BlockSpec(memory_space=pltpu.VMEM)
    hbm = pl.BlockSpec(memory_space=pl.ANY)
    smem = pl.BlockSpec(memory_space=pltpu.SMEM)
    saved = [
        ((layers, count + HALO, channels), F32),
        ((layers, count + HALO, LANES), F32),
        ((layers, count + 2 * run + HALO, channels), BF16),
        ((count + HALO, 2 * LANES), BF16),
    ]
    *kept, partial = pl.pallas_call(
        functools.partial(forward_kernel, run, freq, chunks),
        out_shape=[jax.ShapeDtypeStruct(s, d) for s, d in saved]
        + [jax.ShapeDtypeStruct((8, channels), F32)],
        in_specs=[smem] + [vmem] * len(received) + [hbm] * 3 + [vmem],
        out_specs=[hbm] * 4 + [vmem],
        scratch_shapes=[pltpu.VMEM(s, d) for s, d in saved]
        + [
            pltpu.VMEM(stem_weight.shape, BF16),
            pltpu.VMEM(kernels.shape, BF16),
            pltpu.VMEM(mix_weight.shape, BF16),
            pltpu.VMEM((count + HALO, channels), F32),
            pltpu.VMEM((HALO, channels), F32),
            pltpu.SemaphoreType.DMA((3 * layers + 1,)),
            pltpu.SemaphoreType.DMA((2 * layers + 1,)),
            pltpu.SemaphoreType.DMA((layers, count // min(TILE, count))),
        ],
        compiler_params=pltpu.CompilerParams(vmem_limit_bytes=56 * 1024 * 1024),
        name="network_ahead",
    )(here, *received, stem_weight, kernels, mix_weight, bounds)

    sums = traded([partial] * freq, "freq")
    core = (lax.axis_index("dp") % 2).astype(jnp.int32)
    scalars = jnp.stack([place, labels[0], jnp.int32(classes), core])
    sizes = [layers * channels, 2 * LANES, layers * KW * GROUP_WIDTH, HALO]
    step = HALO * lax.axis_size("dp") // 2 * freq
    half_rows = -(-sum(sizes) // (2 * step)) * step
    halves = network_back(scalars, sums, kept, bounds, head_t, kernels_t, mix_t, half_rows)
    mix, stem, conv, head, loss = sum_everywhere(*halves, sizes, classes)
    return (
        loss.reshape(()),
        stem,
        conv.reshape(layers, KW, GROUP_WIDTH, channels),
        mix.reshape(layers, channels, channels),
        head.T,
    )


def solution(mesh):
    in_specs = (P("dp", None, None, "freq"), P(), P(), P(), P(), P("dp"), P())
    out_specs = (P(), P(), P(), P(), P())
    return jax.shard_map(local, mesh=mesh, in_specs=in_specs, out_specs=out_specs, check_vma=False)
```

```python
import functools

import jax
import jax.numpy as jnp
import numpy as np
from jax import lax
from jax.experimental import pallas as pl
from jax.experimental.pallas import tpu as pltpu
from jax.sharding import PartitionSpec as P

POOL = 128
GROUP_WIDTH = 16
KW = 3
EPS = 1e-05
LANES = 128
HALF_MXU = 256
HALO = 16
TILE = 1024
F32 = jnp.float32
BF16 = jnp.bfloat16


def split16(values):
    high = values.astype(BF16)
    return high, (values - high.astype(F32)).astype(BF16)


def table_pair(values):
    high = values.astype(jnp.bfloat16)
    return np.stack([high, (values - high.astype(np.float64)).astype(jnp.bfloat16)])


def first_tables(first_len, second_len):
    total_len = first_len * second_len
    rows = np.arange(first_len // 2)
    odd = 2 * rows + 1
    angles = (np.outer(np.arange(first_len), odd) % (2 * first_len)) * (np.pi / first_len)
    twiddles = (np.outer(np.arange(second_len), odd) % (2 * total_len)) * (np.pi / total_len)

    def by_block(a, b):
        blocks = first_len // 2 // LANES
        a = a.reshape(a.shape[0], blocks, 1, LANES)
        b = b.reshape(b.shape[0], blocks, 1, LANES)
        return np.concatenate([a, b], axis=2).reshape(a.shape[0], -1)

    section = table_pair(by_block(np.cos(angles), -np.sin(angles)))
    twiddle = by_block(np.cos(twiddles), np.sin(twiddles)).astype(np.float32)
    return section, twiddle


def second_tables(second_len):
    quarter = second_len // 4
    idx = np.arange(quarter)
    angles = np.outer(np.arange(1, 4), idx) * (2 * np.pi / second_len)
    spread = np.stack([np.cos(angles), np.sin(angles)], axis=1)[..., None] * np.ones(LANES)
    order = np.concatenate([idx[: quarter // 2], idx[quarter // 2 :][::-1]])
    inner = (np.outer(order, idx) % quarter) * (2 * np.pi / quarter)
    table = table_pair(np.concatenate([np.cos(inner), np.sin(inner)], axis=1))
    flip = np.eye(LANES)[::-1].astype(jnp.bfloat16)
    return spread.astype(np.float32), table, flip


def level_of(exponent, mantissa):
    return mantissa * jnp.exp(exponent * np.log(2.0).astype(np.float32)) * (1.0 / (16384.0 * 32767.0))


def first_kernel(devices, place_ref, x_ref, table_ref, twiddle_ref, *refs):
    outs, (highs, lows, codes) = refs[:devices], refs[devices:]
    signals, cols, _ = highs.shape
    block = pl.program_id(0)

    @pl.when(block == 0)
    def _():
        for signal in range(signals):
            highs[signal], lows[signal] = split16(x_ref[signal].T)

    row = lax.broadcasted_iota(jnp.int32, (HALO, 2 * LANES), 0)
    cosine, sine = twiddle_ref[:, :LANES], twiddle_ref[:, LANES:]
    for signal in range(signals):
        both = jnp.dot(highs[signal], table_ref[0], preferred_element_type=F32)
        both += jnp.dot(lows[signal], table_ref[0], preferred_element_type=F32)
        both += jnp.dot(highs[signal], table_ref[1], preferred_element_type=F32)
        real, imag = both[:, :LANES], both[:, LANES:]
        turned = jnp.concatenate(
            [real * cosine + imag * sine, imag * cosine - real * sine], axis=1
        )
        top = jnp.maximum(jnp.max(jnp.abs(turned), axis=0, keepdims=True), 1e-20)
        exponent = jnp.ceil(jnp.log(top) * (1.0 / np.log(2.0)))
        mantissa = jnp.floor(
            top * jnp.exp(-exponent * np.log(2.0).astype(np.float32)) * 16384.0
        ) + 1.0
        level = 1.0 / level_of(exponent, mantissa)
        codes[:cols, :] = jnp.round(turned * level).astype(jnp.int32).astype(jnp.int16)
        head = jnp.where(row == 0, exponent, jnp.where(row == 1, mantissa, 0.0))
        codes[cols:, :] = head.astype(jnp.int32).astype(jnp.int16)
        for shift in range(devices):

            @pl.when((place_ref[0] ^ shift) == block * signals + signal)
            def _(shift=shift):
                outs[shift][...] = codes[...]


def first_section(place, records, at, signals, devices, section, twiddle):
    first_len, cols = records.shape[-2:]
    blocks = devices // signals
    shape = (cols + HALO, 2 * LANES)
    return pl.pallas_call(
        functools.partial(first_kernel, devices),
        out_shape=[jax.ShapeDtypeStruct(shape, jnp.int16)] * devices,
        grid_spec=pltpu.PrefetchScalarGridSpec(
            num_scalar_prefetch=1,
            grid=(blocks,),
            in_specs=[
                pl.BlockSpec((signals, first_len, cols), lambda i, s: (at, 0, 0)),
                pl.BlockSpec((2, first_len, 2 * LANES), lambda i, s: (0, 0, i)),
                pl.BlockSpec((cols, 2 * LANES), lambda i, s: (s[0], i)),
            ],
            out_specs=[pl.BlockSpec(shape, lambda i, s: (0, 0))] * devices,
            scratch_shapes=[
                pltpu.VMEM((signals, cols, first_len), BF16),
                pltpu.VMEM((signals, cols, first_len), BF16),
                pltpu.VMEM(shape, jnp.int16),
            ],
        ),
        compiler_params=pltpu.CompilerParams(vmem_limit_bytes=60 * 1024 * 1024),
        cost_estimate=pl.CostEstimate(
            flops=6 * signals * first_len * first_len * cols, bytes_accessed=2**23, transcendentals=0
        ),
        name="first_section",
    )(place, records, section, twiddle)


def second_kernel(devices, total_len, place_ref, *refs):
    received, refs = refs[:devices], refs[devices:]
    (spread_ref, table_ref, flip_ref), refs = refs[:3], refs[3:]
    outs, (signal, right, rest, packed) = refs[:devices], refs[devices:]
    place = place_ref[0]
    cols = signal.shape[0] // devices
    quarter = signal.shape[0] // 4
    run = quarter // 2 // devices
    for shift in range(devices):
        source = place ^ shift
        head = received[shift][cols:, :].astype(jnp.int32).astype(F32)
        values = received[shift][:cols, :].astype(jnp.int32).astype(F32)
        rows = pl.ds(pl.multiple_of(source * cols, cols), cols)
        signal[rows, :] = values * level_of(head[0:1], head[1:2])
    step = min(quarter, 128)
    for at in range(0, quarter, step):
        parts = [signal[g * quarter + at : g * quarter + at + step, :] for g in range(4)]
        re = [v[:, :LANES] for v in parts]
        im = [v[:, LANES:] for v in parts]
        sum_r, dif_r = re[0] + re[2], re[0] - re[2]
        sum_i, dif_i = im[0] + im[2], im[0] - im[2]
        odd_r, odm_r = re[1] + re[3], re[1] - re[3]
        odd_i, odm_i = im[1] + im[3], im[1] - im[3]
        turned = [
            (sum_r + odd_r, sum_i + odd_i),
            (dif_r + odm_i, dif_i - odm_r),
            (sum_r - odd_r, sum_i - odd_i),
            (dif_r - odm_i, dif_i + odm_r),
        ]
        for c in range(4):
            real, imag = turned[c]
            if c:
                cosine = spread_ref[c - 1, 0, at : at + step, :]
                sine = spread_ref[c - 1, 1, at : at + step, :]
                real, imag = real * cosine + imag * sine, imag * cosine - real * sine
            first = slice(2 * LANES * c, 2 * LANES * c + LANES)
            second = slice(2 * LANES * c + LANES, 2 * LANES * (c + 1))
            for ref, r, i in zip((right, rest), split16(real), split16(imag)):
                ref[at : at + step, first] = r
                ref[at : at + step, second] = i
                ref[quarter + at : quarter + at + step, first] = i
                ref[quarter + at : quarter + at + step, second] = -r
    row = lax.broadcasted_iota(jnp.int32, (HALO, LANES), 0)
    edges = [jnp.zeros((HALO, LANES), F32) for _ in range(devices)]
    for c in range(4):
        lanes = slice(2 * LANES * c, 2 * LANES * (c + 1))
        both = jnp.dot(table_ref[0], right[:, lanes], preferred_element_type=F32)
        both += jnp.dot(table_ref[0], rest[:, lanes], preferred_element_type=F32)
        both += jnp.dot(table_ref[1], right[:, lanes], preferred_element_type=F32)
        power = both[:, :LANES] ** 2 + both[:, LANES:] ** 2
        features = jnp.log1p(power * (1.0 / total_len))
        low = features[: quarter // 2].astype(BF16)
        high = jnp.dot(
            features[quarter // 2 :].astype(BF16), flip_ref[...], preferred_element_type=F32
        )
        for part, values, group in ((0, low, c), (1, high.astype(BF16), 4 + 3 - c)):
            wide = values.astype(F32)
            for to in range(devices):
                packed[to, group * run : (group + 1) * run, :] = values[to * run : (to + 1) * run]
                if group % 4 == 3 and to > 0:
                    edges[to] = jnp.where(
                        row == 2 * part, wide[to * run - 1 : to * run], edges[to]
                    )
                if group % 4 == 0 and to < devices - 1:
                    edges[to] = jnp.where(
                        row == 2 * part + 1, wide[(to + 1) * run : (to + 1) * run + 1], edges[to]
                    )
    for to in range(devices):
        packed[to, 8 * run :, :] = edges[to].astype(BF16)
    for shift in range(devices):
        outs[shift][...] = packed[place ^ shift]


def second_section(place, received, second_len, total_len, spread, table, flip):
    devices = len(received)
    quarter = second_len // 4
    run = quarter // 2 // devices
    shape = (8 * run + HALO, LANES)
    vmem = pl.BlockSpec(memory_space=pltpu.VMEM)
    return pl.pallas_call(
        functools.partial(second_kernel, devices, total_len),
        out_shape=[jax.ShapeDtypeStruct(shape, BF16)] * devices,
        in_specs=[pl.BlockSpec(memory_space=pltpu.SMEM)] + [vmem] * (devices + 3),
        out_specs=[vmem] * devices,
        scratch_shapes=[
            pltpu.VMEM((second_len, 2 * LANES), F32),
            pltpu.VMEM((2 * quarter, 8 * LANES), BF16),
            pltpu.VMEM((2 * quarter, 8 * LANES), BF16),
            pltpu.VMEM((devices,) + shape, BF16),
        ],
        compiler_params=pltpu.CompilerParams(vmem_limit_bytes=32 * 1024 * 1024),
        cost_estimate=pl.CostEstimate(
            flops=96 * LANES * quarter * quarter, bytes_accessed=2**23, transcendentals=0
        ),
        name="second_section",
    )(place, *received, spread, table, flip)


def position_column(start, run, at, rows):
    row = at + lax.broadcasted_iota(jnp.int32, (rows, 1), 0)
    return start + row // run + 32 * (row % run)


def halo_column(start, count):
    row = lax.broadcasted_iota(jnp.int32, (HALO, 1), 0)
    return start + jnp.where(row < 8, row - 8, count + row - 8)


def silu_gate(v):
    return 0.5 + 0.5 * jnp.tanh(0.5 * v)


def close_ends(padded, halo, run):
    count = padded.shape[0] - 2 * run - HALO
    row = lax.broadcasted_iota(jnp.int32, (run, 1), 0)
    tail = padded[count : count + run, :].astype(F32)
    head = padded[run : 2 * run, :].astype(F32)
    before = jnp.where(row == 0, halo[7:8], pltpu.roll(tail, 1, 0))
    after = jnp.where(row == run - 1, halo[8:9], pltpu.roll(head, run - 1, 0))
    padded[:run, :] = before.astype(BF16)
    padded[run + count : 2 * run + count, :] = after.astype(BF16)
    padded[2 * run + count :, :] = halo.astype(BF16)
    row = lax.broadcasted_iota(jnp.int32, (HALO, 1), 0)
    down = jnp.where(row == 8, tail[run - 1 : run], pltpu.roll(halo, 1, 0))
    up = jnp.where(row == 7, head[:1], pltpu.roll(halo, HALO - 1, 0))
    return [v.astype(BF16) for v in (down, halo, up)]


def taps_product(windows, kernels):
    halves = []
    for half in range(kernels.shape[0]):
        lanes = slice(half * HALF_MXU, (half + 1) * HALF_MXU)
        total = None
        for tap in range(KW):
            term = jnp.dot(
                windows[tap](lanes), kernels[half, tap], preferred_element_type=F32
            )
            total = term if total is None else total + term
        halves.append(total)
    return jnp.concatenate(halves, axis=1)


def forward_kernel(run, devices, chunks, place_ref, *refs):
    received, refs = refs[: chunks * devices], refs[chunks * devices :]
    (stem_in, kernels_in, mix_in, bounds, preacts_out, scales_out, padded_out, feats_out, partial_out,
     preacts, scales, padded, feats, stem, kernels, mix, stream, halos, sems, sems_in, sems_tile) = refs
    layers = mix.shape[0]
    weights = [pltpu.make_async_copy(stem_in, stem, sems_in.at[0])]
    for layer in range(layers):
        for k, (src, dst) in enumerate(((kernels_in, kernels), (mix_in, mix))):
            weights.append(
                pltpu.make_async_copy(src.at[layer], dst.at[layer], sems_in.at[1 + 2 * layer + k])
            )
    for copy in weights:
        copy.start()
    count = 32 * run
    place = place_ref[0]
    start = place * count
    signals = 2 // chunks
    blocks = devices // signals

    row16 = lax.broadcasted_iota(jnp.int32, (HALO, LANES), 0)
    edge = [jnp.zeros((HALO, LANES), F32) for _ in range(2)]
    for chunk in range(chunks):
        for shift in range(devices):
            ref = received[chunk * devices + shift]
            source = place ^ shift
            ends = ref[8 * run :, :].astype(F32)
            channel = chunk if chunks == 2 else source % 2
            lanes = pl.ds(pl.multiple_of(channel * LANES, LANES), LANES)
            for part in range(2):
                block = source // signals
                block = 2 * blocks - 1 - block if part else block
                for c in range(4):
                    at = pl.multiple_of((block + 8 * c) * run, run)
                    feats[pl.ds(at, run), lanes] = ref[
                        (part * 4 + c) * run : (part * 4 + c + 1) * run, :
                    ]
                for which in range(2):
                    value = ends[2 * part + which : 2 * part + which + 1]
                    at = row16 == block + 8 * which
                    for k in range(2):
                        edge[k] = jnp.where(at & (channel == k), value, edge[k])
    for k in range(2):
        feats[count:, k * LANES : (k + 1) * LANES] = edge[k].astype(BF16)
    copies = []

    saved = []

    def save(source, target):
        copy = pltpu.make_async_copy(source, target, sems.at[len(saved)])
        copy.start()
        saved.append(copy)

    save(feats, feats_out)
    halo_place = halo_column(start, count)
    inside = ((halo_place >= 0) & (halo_place < devices * count)).astype(F32)
    tile = min(TILE, count)

    def norm(layer, rows, values):
        scale = lax.rsqrt(jnp.mean(values * values, axis=-1, keepdims=True) + EPS)
        scales[layer, rows, :] = jnp.broadcast_to(scale, (values.shape[0], LANES))
        return values * scale

    def put_normed(layer, at, values):
        normed = norm(layer, pl.ds(at, tile), values)
        padded[layer, pl.ds(pl.multiple_of(at + run, run), tile), :] = normed.astype(BF16)

    def stem_tile(i, _):
        at = pl.multiple_of(i * tile, tile)
        values = jnp.dot(feats[pl.ds(at, tile), :], stem[...], preferred_element_type=F32)
        stream[pl.ds(at, tile), :] = values
        put_normed(0, at, values)
        return 0

    weights[0].wait()
    lax.fori_loop(0, count // tile, stem_tile, 0)
    values = jnp.dot(feats[count:, :], stem[...], preferred_element_type=F32)
    stream[count:, :] = values
    halos[...] = norm(0, slice(count, count + HALO), values) * inside
    partial_out[...] = jnp.zeros_like(partial_out)

    for layer in range(layers):
        here = padded.at[layer]
        windows = close_ends(here, halos[...].astype(BF16).astype(F32), run)
        save(here, padded_out.at[layer])
        save(scales.at[layer], scales_out.at[layer])
        last = layer == layers - 1
        weights[1 + 2 * layer].wait()
        weights[2 + 2 * layer].wait()

        def save_tile(i, layer=layer):
            rows = pl.ds(pl.multiple_of(i * tile, tile), tile)
            return pltpu.make_async_copy(
                preacts.at[layer, rows, :], preacts_out.at[layer, rows, :], sems_tile.at[layer, i]
            )

        def layer_tile(i, _, layer=layer, here=here, last=last, save_tile=save_tile):
            at = pl.multiple_of(i * tile, tile)
            rows = pl.ds(at, tile)
            taps = [
                lambda lanes, t=t: here[pl.ds(pl.multiple_of(at + t * run, run), tile), lanes]
                for t in range(KW)
            ]
            preact = taps_product(taps, kernels.at[layer])
            preacts[layer, rows, :] = preact
            save_tile(i).start()
            active = (preact * silu_gate(preact)).astype(BF16)
            values = stream[rows, :] + jnp.dot(active, mix[layer], preferred_element_type=F32)
            if last:
                place = position_column(start, run, at, tile)
                member = (place >= bounds[0:1, :]) & (place < bounds[1:2, :])
                kept = jnp.where(member, values, 0.0)
                partial_out[...] += jnp.sum(kept.reshape(tile // 8, 8, kept.shape[1]), axis=0)
            else:
                stream[rows, :] = values
                put_normed(layer + 1, at, values)
            return 0

        lax.fori_loop(0, count // tile, layer_tile, 0)
        preact = taps_product([lambda lanes, v=v: v[:, lanes] for v in windows], kernels.at[layer])
        preacts[layer, count:, :] = preact
        rest = pl.ds(count, HALO)
        save(preacts.at[layer, rest, :], preacts_out.at[layer, rest, :])
        copies.extend(save_tile(i) for i in range(count // tile))
        if not last:
            active = (preact * silu_gate(preact)).astype(BF16)
            values = stream[count:, :] + jnp.dot(active, mix[layer], preferred_element_type=F32)
            stream[count:, :] = values
            halos[...] = norm(layer + 1, slice(count, count + HALO), values) * inside
    for copy in saved + copies:
        copy.wait()


def backward_kernel(run, devices, all_records, place_ref, *refs):
    sums, refs = refs[:devices], refs[devices:]
    (preacts_in, scales_in, padded_in, feats_in, bounds, head, kernels_in, mix_in, kept, sent,
     preacts, scales, padded, feats, kernels, mix_t, sums_out, codes, grad, ahead, active_t, out16,
     sems, sems_out) = refs
    layers = mix_t.shape[0]
    channels = grad.shape[1]
    count = 32 * run
    start = place_ref[0] * count
    core = place_ref[3]
    tile = min(TILE, count)
    tiles = count // tile

    arriving = []
    for layer in reversed(range(layers)):
        cuts = [pl.ds(k * tile, tile) for k in range(tiles)] + [pl.ds(count, HALO)]
        copies = [(preacts_in.at[layer, cut, :], preacts.at[layer, cut, :]) for cut in cuts]
        copies += [(padded_in.at[layer], padded.at[layer]), (scales_in.at[layer], scales.at[layer])]
        copies += [(kernels_in.at[layer], kernels.at[layer])]
        copies = [(mix_in.at[layer], mix_t.at[layer])] + copies
        arriving.append(copies)
    arriving.append([(feats_in, feats)])
    at = 0
    for k, copies in enumerate(arriving):
        arriving[k] = [
            pltpu.make_async_copy(*copy, sems.at[at + j]) for j, copy in enumerate(copies)
        ]
        at += len(copies)
        for copy in arriving[k]:
            copy.start()

    half_rows = kept.shape[0]
    leaving = []

    def put(at, value):
        sums_out[at : at + value.shape[0], :] = value

    def leave(region):
        half, inside = divmod(region, sent.shape[0])
        rows = pl.ds(region * channels, channels)
        sem = sems_out.at[region]
        plain = pltpu.make_async_copy(
            sums_out.at[rows, :], kept.at[pl.ds(inside * channels, channels), :], sem
        )
        coded = pltpu.make_async_copy(codes.at[region], sent.at[inside], sem)
        leaving.append((half, plain, coded))

        @pl.when(core == half)
        def _():
            plain.start()

        @pl.when(core != half)
        def _():
            encode(sums_out[rows, :], codes.at[region])
            coded.start()

    total = sums[0][...]
    for ref in sums[1:]:
        total = total + ref[...]
    band_sum = jnp.sum(total, axis=0, keepdims=True)
    counts = (bounds[1:2, :] - bounds[0:1, :]).astype(F32)
    pooled = band_sum / counts
    row = lax.broadcasted_iota(jnp.int32, (HALO, 1), 0)
    logits = jnp.sum(head[...] * pooled, axis=1, keepdims=True)
    exponents = jnp.where(row < place_ref[2], jnp.exp(logits), 0.0)
    denominator = jnp.sum(exponents, axis=0, keepdims=True)
    one_hot = (row == place_ref[1]).astype(F32)
    loss = jnp.log(denominator) - jnp.sum(one_hot * logits, axis=0, keepdims=True)
    loss = loss / all_records
    grad_logits = (exponents / denominator - one_hot) / all_records
    grad_pooled = jnp.sum(head[...] * grad_logits, axis=0, keepdims=True)
    grad_band = grad_pooled / counts
    lead = (place_ref[0] == 0).astype(F32)
    stem_at = layers * channels
    conv_at = stem_at + 2 * LANES
    head_at = conv_at + layers * KW * GROUP_WIDTH
    put(head_at, lead * jnp.where(row == HALO - 1, loss, grad_logits * pooled))
    rest = 2 * half_rows - head_at - HALO
    if rest:
        put(head_at + HALO, jnp.zeros((rest, channels), F32))

    def spread(place):
        member = (place >= bounds[0:1, :]) & (place < bounds[1:2, :])
        return jnp.where(member, grad_band, 0.0)

    halo_place = halo_column(start, count)
    inside = ((halo_place >= 0) & (halo_place < devices * count)).astype(F32)
    grad[count:, :] = spread(halo_place)

    def gate_grad(value, grad_act):
        gate = silu_gate(value)
        return grad_act * gate * (1.0 + value * (1.0 - gate)), value * gate

    def stream_grad(layer, outgoing, rows, normed, grad_normed):
        scale = jnp.concatenate([scales[layer, rows, :]] * (channels // LANES), axis=1)
        normed = normed.astype(F32)
        inner = jnp.mean(normed * grad_normed, axis=-1, keepdims=True)
        return outgoing + scale * (grad_normed - normed * inner)

    at_row = lax.broadcasted_iota(jnp.int32, (HALF_MXU, HALF_MXU), 0) // GROUP_WIDTH
    at_col = lax.broadcasted_iota(jnp.int32, (HALF_MXU, HALF_MXU), 1) // GROUP_WIDTH
    for layer in reversed(range(layers)):
        copies = arriving[layers - 1 - layer]
        top, bottom = layer == layers - 1, layer == 0

        def act_tile(i, _, layer=layer, top=top):
            at = pl.multiple_of(i * tile, tile)
            rows = pl.ds(at, tile)
            if top:
                values = spread(position_column(start, run, at, tile))
                grad[rows, :] = values
            else:
                values = grad[rows, :]
            outgoing = values.astype(BF16)
            out16[rows, :] = outgoing
            grad_act = jnp.dot(outgoing, mix_t[layer], preferred_element_type=F32)
            grad_pre, act = gate_grad(preacts[layer, rows, :], grad_act)
            grad_pre = grad_pre.astype(BF16)
            active_t[:, rows] = act.astype(BF16).T
            ahead[pl.ds(pl.multiple_of(at + run, run), tile), :] = grad_pre
            return 0

        copies[0].wait()
        if top:
            for k in range(tiles):
                copies[1 + k].wait()
                lax.fori_loop(k, k + 1, act_tile, 0)
        else:
            for k in range(tiles):
                copies[1 + k].wait()
            lax.fori_loop(0, tiles, act_tile, 0)
        copies[1 + tiles].wait()
        grad_act = jnp.dot(grad[count:, :].astype(BF16), mix_t[layer], preferred_element_type=F32)
        halo, _ = gate_grad(preacts[layer, count:, :], grad_act)
        halo = (halo * inside).astype(BF16).astype(F32)
        windows = close_ends(ahead, halo, run)

        put(
            layer * channels,
            jnp.dot(active_t[...], out16[...], preferred_element_type=F32),
        )
        leave(layer)

        copies[tiles + 2].wait()
        for tap in range(KW):
            folded = []
            for half in range(channels // HALF_MXU):
                lanes = slice(half * HALF_MXU, (half + 1) * HALF_MXU)
                full = lax.dot_general(
                    padded[layer, tap * run : tap * run + count, lanes],
                    ahead[run : run + count, lanes],
                    (((0,), (0,)), ((), ())),
                    preferred_element_type=F32,
                )
                full = jnp.where(at_row == at_col, full, 0.0)
                folded.append(
                    jnp.sum(full.reshape(HALF_MXU // GROUP_WIDTH, GROUP_WIDTH, HALF_MXU), axis=0)
                )
            at = conv_at + (layer * KW + tap) * GROUP_WIDTH
            put(at, jnp.concatenate(folded, axis=1))
        copies[tiles + 3].wait()
        copies[tiles + 4].wait()

        def stream_tile(i, _, layer=layer, bottom=bottom):
            at = pl.multiple_of(i * tile, tile)
            rows = pl.ds(at, tile)
            taps = [
                lambda lanes, t=t: ahead[
                    pl.ds(pl.multiple_of(at + (KW - 1 - t) * run, run), tile), lanes
                ]
                for t in range(KW)
            ]
            grad_normed = taps_product(taps, kernels.at[layer])
            normed = padded[layer, pl.ds(pl.multiple_of(at + run, run), tile), :]
            value = stream_grad(layer, grad[rows, :], rows, normed, grad_normed)
            if bottom:
                high, low = split16(value)
                out16[rows, :] = high
                active_t[:, rows] = low.T
            else:
                grad[rows, :] = value
            return 0

        lax.fori_loop(0, tiles, stream_tile, 0)
        if not bottom:
            grad_normed = taps_product(
                [lambda lanes, v=v: v[:, lanes] for v in reversed(windows)], kernels.at[layer]
            )
            normed = padded[layer, count + 2 * run :, :]
            rows = slice(count, count + HALO)
            grad[rows, :] = stream_grad(layer, grad[rows, :], rows, normed, grad_normed)

    arriving[-1][0].wait()
    value = lax.dot_general(
        feats[:count, :], out16[...], (((0,), (0,)), ((), ())), preferred_element_type=F32
    )
    rest = jnp.dot(active_t[...], feats[:count, :], preferred_element_type=F32)
    put(stem_at, value + rest.T)
    leave(layers)
    for half, plain, coded in leaving:
        pl.when(core == half)(plain.wait)
        pl.when(core != half)(coded.wait)


def network_back(scalars, sums, saved, bounds, head_t, kernels_t, mix_t, half_rows):
    preacts, scales, padded, feats = saved
    layers, rows, channels = preacts.shape
    count = rows - HALO
    tiles = count // min(TILE, count)
    devices = len(sums)
    region = (channels + HALO, channels)
    vmem = pl.BlockSpec(memory_space=pltpu.VMEM)
    hbm = pl.BlockSpec(memory_space=pl.ANY)
    return pl.pallas_call(
        functools.partial(backward_kernel, count // 32, devices, lax.axis_size("dp")),
        out_shape=[
            jax.ShapeDtypeStruct((half_rows, channels), F32),
            jax.ShapeDtypeStruct((half_rows // channels,) + region, jnp.int16),
        ],
        in_specs=[pl.BlockSpec(memory_space=pltpu.SMEM)]
        + [vmem] * devices
        + [hbm] * 4
        + [vmem] * 2
        + [hbm] * 2,
        out_specs=[hbm] * 2,
        scratch_shapes=[pltpu.VMEM(x.shape, x.dtype) for x in saved]
        + [
            pltpu.VMEM(kernels_t.shape, BF16),
            pltpu.VMEM(mix_t.shape, BF16),
            pltpu.VMEM((2 * half_rows, channels), F32),
            pltpu.VMEM((2 * half_rows // channels,) + region, jnp.int16),
            pltpu.VMEM((rows, channels), F32),
            pltpu.VMEM(padded.shape[1:], BF16),
            pltpu.VMEM((channels, count), BF16),
            pltpu.VMEM((count, channels), BF16),
            pltpu.SemaphoreType.DMA((layers * (tiles + 5) + 1,)),
            pltpu.SemaphoreType.DMA((layers + 1,)),
        ],
        compiler_params=pltpu.CompilerParams(vmem_limit_bytes=54 * 1024 * 1024),
        name="network_back",
    )(scalars, *sums, *saved, bounds, head_t, kernels_t, mix_t)


def weights_kernel(conv_ref, mix_ref, kernels_ref, turned_ref, mix_t_ref):
    row = lax.broadcasted_iota(jnp.int32, (HALF_MXU, HALF_MXU), 0) // GROUP_WIDTH
    col = lax.broadcasted_iota(jnp.int32, (HALF_MXU, HALF_MXU), 1) // GROUP_WIDTH
    for tap in range(KW):
        for half in range(kernels_ref.shape[0]):
            taps = conv_ref[tap, :, half * HALF_MXU : (half + 1) * HALF_MXU].astype(F32)
            dense = jnp.concatenate([taps] * (HALF_MXU // GROUP_WIDTH), axis=0)
            dense = jnp.where(row == col, dense, 0.0)
            kernels_ref[half, tap] = dense.astype(BF16)
            turned_ref[half, tap] = dense.T.astype(BF16)
    mix_t_ref[...] = mix_ref[...].astype(F32).T.astype(BF16)


def dense_weights(conv_weight, mix_weight):
    layers, taps, width, channels = conv_weight.shape
    dense = (layers, channels // HALF_MXU, taps, HALF_MXU, HALF_MXU)
    by_layer = lambda shape: pl.BlockSpec(
        (None,) + shape[1:], lambda i: (i,) + (0,) * (len(shape) - 1)
    )
    return pl.pallas_call(
        weights_kernel,
        out_shape=[
            jax.ShapeDtypeStruct(dense, BF16),
            jax.ShapeDtypeStruct(dense, BF16),
            jax.ShapeDtypeStruct(mix_weight.shape, BF16),
        ],
        grid=(layers,),
        in_specs=[by_layer(conv_weight.shape), by_layer(mix_weight.shape)],
        out_specs=[by_layer(dense), by_layer(dense), by_layer(mix_weight.shape)],
        compiler_params=pltpu.CompilerParams(vmem_limit_bytes=32 * 1024 * 1024),
        cost_estimate=pl.CostEstimate(flops=0, bytes_accessed=2**24, transcendentals=0),
        name="dense_weights",
    )(conv_weight, mix_weight)


def swap(x, axis, step):
    return lax.ppermute(x, axis, [(i, i ^ step) for i in range(lax.axis_size(axis))])


def encode(values, out_ref):
    rows = values.shape[0]
    top = jnp.maximum(jnp.max(jnp.abs(values), axis=1, keepdims=True), 1e-30)
    exponent = jnp.ceil(jnp.log(top) * (1.0 / np.log(2.0)) + 1e-4)
    scale = jnp.exp(-exponent * np.log(2.0).astype(np.float32)) * 32767.0
    out_ref[:rows, :] = jnp.round(values * scale).astype(jnp.int32).astype(jnp.int16)
    out_ref[rows:, :] = jnp.zeros((HALO, values.shape[1]), jnp.int16)
    across = jnp.broadcast_to(exponent, (rows, LANES)).T[:HALO, :]
    out_ref[rows:, :rows] = across.astype(jnp.int32).astype(jnp.int16)


def decode(ref, at=0, rows=None):
    total = ref.shape[0] - HALO
    rows = total if rows is None else rows
    across = ref[total:, pl.ds(at, rows)].astype(jnp.int32).astype(F32)
    exponent = jnp.concatenate([across] * (LANES // HALO), axis=0).T[:, :1]
    scale = jnp.exp(exponent * np.log(2.0).astype(np.float32)) * (1.0 / 32767.0)
    return ref[pl.ds(at, rows), :].astype(jnp.int32).astype(F32) * scale


def cut_kernel(size, place_ref, whole_ref, *refs):
    regions, outs = refs[:-size], refs[-size:]
    rows = whole_ref.shape[0] // size
    for k in range(size):
        at = pl.multiple_of((place_ref[0] ^ k) * rows, rows)
        value = whole_ref[pl.ds(at, rows), :]
        for ref in regions:
            height = ref.shape[1] - HALO
            inside = pl.multiple_of(at % height, rows)
            value = value + decode(ref.at[at // height], inside, rows)
        if k:
            encode(value, outs[k])
        else:
            outs[0][...] = value


def sum_kernel(first_ref, *refs):
    value = first_ref[...]
    for ref in refs[:-1]:
        value = value + decode(ref)
    refs[-1][...] = value


def pieces_kernel(place_ref, *refs):
    inputs, out_ref = refs[:-1], refs[-1]
    rows = inputs[0].shape[0] - HALO
    for k, ref in enumerate(inputs):
        at = pl.multiple_of((place_ref[0] ^ k) * rows, rows)
        out_ref[pl.ds(at, rows), :] = decode(ref)


def coded_pieces_kernel(place_ref, *refs):
    inputs, out_ref = refs[:-1], refs[-1]
    for k, ref in enumerate(inputs):
        out_ref[place_ref[0] ^ k] = ref[...]


def small_call(kernel, name, out_shape, place, *args, scratch=()):
    vmem = pl.BlockSpec(memory_space=pltpu.VMEM)
    smem = pl.BlockSpec(memory_space=pltpu.SMEM)
    several = isinstance(out_shape, list)
    lead = [] if place is None else [place.reshape(1).astype(jnp.int32)]
    return pl.pallas_call(
        kernel,
        out_shape=out_shape,
        in_specs=[smem] * len(lead) + [vmem] * len(args),
        out_specs=[vmem] * len(out_shape) if several else vmem,
        scratch_shapes=list(scratch),
        compiler_params=pltpu.CompilerParams(vmem_limit_bytes=32 * 1024 * 1024),
        name=name,
    )(*lead, *args)


def sum_encode_kernel(first_ref, *refs):
    value = first_ref[...]
    for ref in refs[:-1]:
        value = value + decode(ref)
    encode(value, refs[-1])


def sum_cut_kernel(size, count, place_ref, *refs):
    refs, total = refs[:-1], refs[-1]
    sum_kernel(*refs[:count], total)
    cut_kernel(size, place_ref, total, *refs[count:])


def lay_encode_kernel(place_ref, *refs):
    inputs, (out_ref, whole) = refs[:-2], refs[-2:]
    pieces_kernel(place_ref, *inputs, whole)
    encode(whole[...], out_ref)


def scatter_shapes(rows, channels, size):
    piece = jax.ShapeDtypeStruct((rows + HALO, channels), jnp.int16)
    return [jax.ShapeDtypeStruct((rows, channels), F32)] + [piece] * (size - 1)


def trade_summands(pieces, axis, stride):
    return [pieces[0]] + [
        swap(piece, axis, k * stride) for k, piece in enumerate(pieces) if k
    ]


def sum_coded(kept, sent):
    chips, freq = lax.axis_size("dp") // 2, lax.axis_size("freq")
    chip, place = lax.axis_index("dp") // 2, lax.axis_index("freq")
    channels = kept.shape[1]
    rows = kept.shape[0] // chips
    part = rows // freq
    pieces = small_call(
        functools.partial(cut_kernel, chips), "cut_pieces", scatter_shapes(rows, channels, chips),
        chip, kept, swap(sent, "dp", 1),
    )
    summands = trade_summands(pieces, "dp", 2)
    pieces = small_call(
        functools.partial(sum_cut_kernel, freq, chips), "sum_cut_pieces",
        scatter_shapes(part, channels, freq), place, *summands,
        scratch=[pltpu.VMEM((rows, channels), F32)],
    )
    summands = trade_summands(pieces, "freq", 1)
    mine = small_call(
        sum_encode_kernel, "sum_code_piece",
        jax.ShapeDtypeStruct((part + HALO, channels), jnp.int16), None, *summands,
    )
    pieces = [mine] + [swap(mine, "freq", k) for k in range(1, freq)]
    mine = small_call(
        lay_encode_kernel, "lay_code_piece",
        jax.ShapeDtypeStruct((rows + HALO, channels), jnp.int16), place, *pieces,
        scratch=[pltpu.VMEM((rows, channels), F32)],
    )
    pieces = [mine] + [swap(mine, "dp", 2 * k) for k in range(1, chips)]
    shape = jax.ShapeDtypeStruct((chips, rows + HALO, channels), jnp.int16)
    return small_call(coded_pieces_kernel, "lay_coded_pieces", shape, chip, *pieces)


def spread_half(core, coded_ref, half_ref, is_mine, outs, sems):
    half_rows = half_ref.shape[0]
    rows = half_rows // coded_ref.shape[0]
    for k in range(coded_ref.shape[0]):
        half_ref[k * rows : (k + 1) * rows, :] = decode(coded_ref.at[k])
    for half in range(2):

        @pl.when((core == half) if is_mine else (core != half))
        def _(half=half):
            copies, first = [], 0
            for out_ref in outs:
                low = max(first, half * half_rows)
                high = min(first + out_ref.shape[0], (half + 1) * half_rows)
                if low < high:
                    copies.append(
                        pltpu.make_async_copy(
                            half_ref.at[pl.ds(low - half * half_rows, high - low), :],
                            out_ref.at[pl.ds(low - first, high - low), :],
                            sems.at[len(copies)],
                        )
                    )
                first += out_ref.shape[0]
            for copy in copies:
                copy.start()
            for copy in copies:
                copy.wait()


def spread_mine(core_ref, mine_ref, *refs):
    *outs, half_ref, sems = refs
    spread_half(core_ref[0], mine_ref, half_ref, True, outs, sems)


def spread_other(classes, head_at, core_ref, mine_ref, other_ref, *refs):
    refs = refs[(len(refs) - 4) // 2 :]
    *outs, head_ref, loss_ref, half_ref, sems = refs
    spread_half(core_ref[0], other_ref, half_ref, False, outs, sems)
    half, at = divmod(head_at, half_ref.shape[0])
    piece, inside = divmod(at, mine_ref.shape[1] - HALO)
    mine = decode(mine_ref.at[piece])[inside : inside + HALO]
    ends = jnp.where(core_ref[0] == half, mine, half_ref[at : at + HALO, :])
    head_ref[...] = ends[:classes]
    loss_ref[...] = ends[HALO - 1 : HALO, :1]


def sum_everywhere(kept, sent, sizes, classes):
    core = (lax.axis_index("dp") % 2).reshape(1).astype(jnp.int32)
    x = sum_coded(kept, sent)
    other = swap(x, "dp", 1)
    channels = x.shape[2]
    shapes = [jax.ShapeDtypeStruct((rows, channels), F32) for rows in sizes[:-1]]
    hbm = pl.BlockSpec(memory_space=pl.ANY)
    vmem = pl.BlockSpec(memory_space=pltpu.VMEM)
    smem = pl.BlockSpec(memory_space=pltpu.SMEM)
    scratch = [pltpu.VMEM(kept.shape, F32), pltpu.SemaphoreType.DMA((len(sizes),))]
    halves = pl.pallas_call(
        spread_mine,
        out_shape=shapes,
        in_specs=[smem, vmem],
        out_specs=[hbm] * len(shapes),
        scratch_shapes=scratch,
        compiler_params=pltpu.CompilerParams(vmem_limit_bytes=32 * 1024 * 1024),
        cost_estimate=pl.CostEstimate(flops=0, bytes_accessed=2**23, transcendentals=0),
        name="spread_mine",
    )(core, x)
    return pl.pallas_call(
        functools.partial(spread_other, classes, sum(sizes[:-1])),
        out_shape=shapes
        + [
            jax.ShapeDtypeStruct((classes, channels), F32),
            jax.ShapeDtypeStruct((1, 1), F32),
        ],
        in_specs=[smem, vmem, vmem] + [hbm] * len(shapes),
        out_specs=[hbm] * len(shapes) + [vmem] * 2,
        scratch_shapes=scratch,
        input_output_aliases={3 + k: k for k in range(len(shapes))},
        compiler_params=pltpu.CompilerParams(vmem_limit_bytes=32 * 1024 * 1024),
        name="spread_other",
    )(core, x, other, *halves)


def traded(pieces, axis):
    return [pieces[0]] + [swap(pieces[k], axis, k) for k in range(1, len(pieces))]


def local(records, stem_weight, conv_weight, mix_weight, head_weight, labels, band_bounds):
    freq = lax.axis_size("freq")
    place = lax.axis_index("freq").astype(jnp.int32)
    first_len, cols = records.shape[2:]
    second_len = cols * freq
    total_len = first_len * second_len
    layers, channels = mix_weight.shape[:2]
    classes = head_weight.shape[1]
    blocks = first_len // 2 // LANES
    run = second_len // 8 // freq
    count = 32 * run

    section, twiddle = (jnp.asarray(t) for t in first_tables(first_len, second_len))
    spread, table, flip = (jnp.asarray(t) for t in second_tables(second_len))
    here = place.reshape(1)
    signals = freq // blocks
    chunks = 2 // signals
    sent = [
        first_section(here, records[0], c, signals, freq, section, twiddle) for c in range(chunks)
    ]
    arrived = [traded(pieces, "freq") for pieces in sent]
    dense = dense_weights(conv_weight, mix_weight)
    arrived[0], (kernels, kernels_t, mix_t) = lax.optimization_barrier((arrived[0], dense))
    features = [
        second_section(here, a, second_len, total_len, spread, table, flip) for a in arrived
    ]
    received = [piece for f in features for piece in traded(f, "freq")]
    head_t = jnp.pad(head_weight.T, ((0, HALO - classes), (0, 0)))
    steps = jnp.repeat(band_bounds // POOL, GROUP_WIDTH)
    bounds = jnp.stack([steps[:channels], steps[GROUP_WIDTH:]]).astype(jnp.int32)

    vmem = pl.BlockSpec(memory_space=pltpu.VMEM)
    hbm = pl.BlockSpec(memory_space=pl.ANY)
    smem = pl.BlockSpec(memory_space=pltpu.SMEM)
    saved = [
        ((layers, count + HALO, channels), F32),
        ((layers, count + HALO, LANES), F32),
        ((layers, count + 2 * run + HALO, channels), BF16),
        ((count + HALO, 2 * LANES), BF16),
    ]
    *kept, partial = pl.pallas_call(
        functools.partial(forward_kernel, run, freq, chunks),
        out_shape=[jax.ShapeDtypeStruct(s, d) for s, d in saved]
        + [jax.ShapeDtypeStruct((8, channels), F32)],
        in_specs=[smem] + [vmem] * len(received) + [hbm] * 3 + [vmem],
        out_specs=[hbm] * 4 + [vmem],
        scratch_shapes=[pltpu.VMEM(s, d) for s, d in saved]
        + [
            pltpu.VMEM(stem_weight.shape, BF16),
            pltpu.VMEM(kernels.shape, BF16),
            pltpu.VMEM(mix_weight.shape, BF16),
            pltpu.VMEM((count + HALO, channels), F32),
            pltpu.VMEM((HALO, channels), F32),
            pltpu.SemaphoreType.DMA((3 * layers + 1,)),
            pltpu.SemaphoreType.DMA((2 * layers + 1,)),
            pltpu.SemaphoreType.DMA((layers, count // min(TILE, count))),
        ],
        compiler_params=pltpu.CompilerParams(vmem_limit_bytes=56 * 1024 * 1024),
        name="network_ahead",
    )(here, *received, stem_weight, kernels, mix_weight, bounds)

    sums = traded([partial] * freq, "freq")
    core = (lax.axis_index("dp") % 2).astype(jnp.int32)
    scalars = jnp.stack([place, labels[0], jnp.int32(classes), core])
    sizes = [layers * channels, 2 * LANES, layers * KW * GROUP_WIDTH, HALO]
    step = HALO * lax.axis_size("dp") // 2 * freq
    half_rows = -(-sum(sizes) // (2 * step)) * step
    halves = network_back(scalars, sums, kept, bounds, head_t, kernels_t, mix_t, half_rows)
    mix, stem, conv, head, loss = sum_everywhere(*halves, sizes, classes)
    return (
        loss.reshape(()),
        stem,
        conv.reshape(layers, KW, GROUP_WIDTH, channels),
        mix.reshape(layers, channels, channels),
        head.T,
    )


def solution(mesh):
    in_specs = (P("dp", None, None, "freq"), P(), P(), P(), P(), P("dp"), P())
    out_specs = (P(), P(), P(), P(), P())
    return jax.shard_map(local, mesh=mesh, in_specs=in_specs, out_specs=out_specs, check_vma=False)
```
